32 devices in a mesh: dp: 4 (over y, x), fsdp: 8 (over z, core).
Axes of the slice: x: 2, y: 2, z: 4, core: 2. Of those that a mesh axis runs over, the one named last changes fastest.
Arguments:
- unit_states: bfloat16 [32, 1024, 1024], P(('dp', 'fsdp')), may hold values from -6 to 6
- dec_states: bfloat16 [32, 256, 1024], P(('dp', 'fsdp')), may hold values from -6 to 6
- enc_states: bfloat16 [32, 256, 1024], P(('dp', 'fsdp')), may hold values from -6 to 6
- unit_len: int32 [32], P(('dp', 'fsdp')), may hold values from 512 to 1024, as said below
- text_len: int32 [32], P(('dp', 'fsdp')), may hold values from 64 to 256, as said below
- task_flag: int32 [32], P(('dp', 'fsdp')), may hold values from 0 to 1
- cotangent: bfloat16 [32, 1024, 1024], P(('dp', 'fsdp')), may hold values from -6 to 6
- ln1_gain: bfloat16 [1024], P(('dp', 'fsdp')), may hold values from 0.25 to 1.75
- ln1_shift: bfloat16 [1024], P(('dp', 'fsdp')), may hold values from -2 to 2
- self_wq: bfloat16 [1024, 1024], P(('dp', 'fsdp')), may hold values from -0.1875 to 0.1875
- self_bq: bfloat16 [1024], P(('dp', 'fsdp')), may hold values from -2 to 2
- self_wk: bfloat16 [1024, 1024], P(('dp', 'fsdp')), may hold values from -0.1875 to 0.1875
- self_wv: bfloat16 [1024, 1024], P(('dp', 'fsdp')), may hold values from -0.1875 to 0.1875
- self_bv: bfloat16 [1024], P(('dp', 'fsdp')), may hold values from -2 to 2
- self_wo: bfloat16 [1024, 1024], P(('dp', 'fsdp')), may hold values from -0.75 to 0.75
- self_bo: bfloat16 [1024], P(('dp', 'fsdp')), may hold values from -2 to 2
- ln2_gain: bfloat16 [1024], P(('dp', 'fsdp')), may hold values from 0.25 to 1.75
- ln2_shift: bfloat16 [1024], P(('dp', 'fsdp')), may hold values from -2 to 2
- cross_wq: bfloat16 [1024, 1024], P(('dp', 'fsdp')), may hold values from -0.1875 to 0.1875
- cross_bq: bfloat16 [1024], P(('dp', 'fsdp')), may hold values from -2 to 2
- cross_wk: bfloat16 [1024, 1024], P(('dp', 'fsdp')), may hold values from -0.1875 to 0.1875
- cross_wv: bfloat16 [1024, 1024], P(('dp', 'fsdp')), may hold values from -0.1875 to 0.1875
- cross_bv: bfloat16 [1024], P(('dp', 'fsdp')), may hold values from -2 to 2
- cross_wo: bfloat16 [1024, 1024], P(('dp', 'fsdp')), may hold values from -0.75 to 0.75
- cross_bo: bfloat16 [1024], P(('dp', 'fsdp')), may hold values from -2 to 2
- ln3_gain: bfloat16 [1024], P(('dp', 'fsdp')), may hold values from 0.25 to 1.75
- ln3_shift: bfloat16 [1024], P(('dp', 'fsdp')), may hold values from -2 to 2
- ffn_w1: bfloat16 [1024, 4096], P(('dp', 'fsdp')), may hold values from -0.1875 to 0.1875
- ffn_b1: bfloat16 [4096], P(('dp', 'fsdp')), may hold values from -2 to 2
- ffn_w2: bfloat16 [4096, 1024], P(('dp', 'fsdp')), may hold values from -0.09375 to 0.09375
- ffn_b2: bfloat16 [1024], P(('dp', 'fsdp')), may hold values from -2 to 2
Outputs:
- mixed: bfloat16 [32, 1024, 1024], P(('dp', 'fsdp'))
- grad_units: float32 [32, 1024, 1024], P(('dp', 'fsdp'))
- grad_dec_states: float32 [32, 256, 1024], P(('dp', 'fsdp'))
- grad_enc_states: float32 [32, 256, 1024], P(('dp', 'fsdp'))
- grad_ln1_gain: float32 [1024], P(('dp', 'fsdp'))
- grad_ln1_shift: float32 [1024], P(('dp', 'fsdp'))
- grad_self_wq: float32 [1024, 1024], P(('dp', 'fsdp'))
- grad_self_bq: float32 [1024], P(('dp', 'fsdp'))
- grad_self_wk: float32 [1024, 1024], P(('dp', 'fsdp'))
- grad_self_wv: float32 [1024, 1024], P(('dp', 'fsdp'))
- grad_self_bv: float32 [1024], P(('dp', 'fsdp'))
- grad_self_wo: float32 [1024, 1024], P(('dp', 'fsdp'))
- grad_self_bo: float32 [1024], P(('dp', 'fsdp'))
- grad_ln2_gain: float32 [1024], P(('dp', 'fsdp'))
- grad_ln2_shift: float32 [1024], P(('dp', 'fsdp'))
- grad_cross_wq: float32 [1024, 1024], P(('dp', 'fsdp'))
- grad_cross_bq: float32 [1024], P(('dp', 'fsdp'))
- grad_cross_wk: float32 [1024, 1024], P(('dp', 'fsdp'))
- grad_cross_wv: float32 [1024, 1024], P(('dp', 'fsdp'))
- grad_cross_bv: float32 [1024], P(('dp', 'fsdp'))
- grad_cross_wo: float32 [1024, 1024], P(('dp', 'fsdp'))
- grad_cross_bo: float32 [1024], P(('dp', 'fsdp'))
- grad_ln3_gain: float32 [1024], P(('dp', 'fsdp'))
- grad_ln3_shift: float32 [1024], P(('dp', 'fsdp'))
- grad_ffn_w1: float32 [1024, 4096], P(('dp', 'fsdp'))
- grad_ffn_b1: float32 [4096], P(('dp', 'fsdp'))
- grad_ffn_w2: float32 [4096, 1024], P(('dp', 'fsdp'))
- grad_ffn_b2: float32 [1024], P(('dp', 'fsdp'))
The draws below stay inside these ranges and needn't reach their ends.
Inputs may be any that keep to these rules, and one draw needn't show every extreme that they name: `unit_len`: at least half of 1024; some item has exactly 1024. `text_len`: at least a quarter of 256; some item has exactly 256.
All inputs are finite; a program needn't handle non-finite values.
Results may differ from the reference program's by a relative error of at most 0.02.
Values may be sent and summed in bfloat16 or wider, within the bound.
A program may use at most 384 MiB of HBM per device.

```python
import jax
import jax.numpy as jnp
from jax import lax

D = 1024
HEADS = 16
FF = 4096
LMAX = 1024
TXT = 256
ITEMS = 32


def draw_unit_len(key, part):
    key = jax.random.fold_in(key, 11)
    first_key, second_key = jax.random.split(key)
    lengths = jax.random.randint(first_key, (ITEMS,), LMAX // 2, LMAX + 1)
    chosen = jax.random.randint(second_key, (), 0, ITEMS)
    return jnp.where(jnp.arange(ITEMS) == chosen, LMAX, lengths).astype(jnp.int32)


def draw_text_len(key, part):
    key = jax.random.fold_in(key, 23)
    first_key, second_key = jax.random.split(key)
    lengths = jax.random.randint(first_key, (ITEMS,), TXT // 4, TXT + 1)
    chosen = jax.random.randint(second_key, (), 0, ITEMS)
    return jnp.where(jnp.arange(ITEMS) == chosen, TXT, lengths).astype(jnp.int32)


def touch_ends(drawn, own_key, least, high):
    extent = drawn.shape
    place = [jax.random.randint(jax.random.fold_in(own_key, axis), (), 0, extent[axis]) for axis in range(len(extent))]
    drawn = drawn.at[tuple(place)].set(least)
    longest = extent.index(max(extent))
    place[longest] = (place[longest] + 1) % extent[longest]
    return drawn.at[tuple(place)].set(high)


def block_levels(stream_key, shape, cuts, smallest, largest):
    gain = 1.0
    for position, parts in cuts:
        draws = jax.random.uniform(jax.random.fold_in(jax.random.fold_in(stream_key, 6), position), (parts,), jnp.float32, smallest / len(cuts), largest / len(cuts))
        gain = gain * jnp.repeat(jnp.exp(draws), shape[position] // parts).reshape((-1,) + (1,) * (len(shape) - 1 - position))
    return gain


def centred(key, dims, deviation, bound, cuts=(), kind=jnp.bfloat16):
    array = jax.random.normal(key, dims, jnp.float32) * deviation
    if len(cuts) > 0:
        array = block_levels(key, dims, cuts, -0.22, 0.18) * array
    return jnp.clip(array, min=-bound, max=bound).astype(kind)


def setup_inputs(seed: int = 0) -> dict:
    seeds = jax.random.split(jax.random.key(seed), 32)
    return {
        "unit_states": centred(seeds[0], (ITEMS, LMAX, D), 1.0, 6.0, ((0, 32),)),
        "dec_states": centred(seeds[1], (ITEMS, TXT, D), 1.0, 6.0, ((0, 32),)),
        "enc_states": centred(seeds[2], (ITEMS, TXT, D), 1.0, 6.0, ((0, 32),)),
        "unit_len": draw_unit_len(jax.random.fold_in(seeds[31], 71), 0),
        "text_len": draw_text_len(jax.random.fold_in(seeds[31], 71), 0),
        "task_flag": touch_ends(jax.random.randint(seeds[5], (ITEMS,), 0, 2), jax.random.fold_in(seeds[5], 1), 0, 1).astype(jnp.int32),
        "cotangent": centred(seeds[6], (ITEMS, LMAX, D), 1.0, 6.0, ((0, 32),)),
        "ln1_gain": jnp.clip(1.0 + 0.15 * jax.random.normal(seeds[7], (D,), jnp.float32), 0.25, 1.75).astype(jnp.bfloat16),
        "ln1_shift": centred(seeds[8], (D,), 0.3, 2.0, ((0, 32),)),
        "self_wq": centred(seeds[9], (D, D), D ** -0.5, 0.1875, ((0, 32),)),
        "self_bq": centred(seeds[10], (D,), 0.3, 2.0, ((0, 32),)),
        "self_wk": centred(seeds[11], (D, D), D ** -0.5, 0.1875, ((0, 32),)),
        "self_wv": centred(seeds[12], (D, D), D ** -0.5, 0.1875, ((0, 32),)),
        "self_bv": centred(seeds[13], (D,), 0.3, 2.0, ((0, 32),)),
        "self_wo": centred(seeds[14], (D, D), (D // 16) ** -0.5, 0.75, ((0, 32),)),
        "self_bo": centred(seeds[15], (D,), 0.3, 2.0, ((0, 32),)),
        "ln2_gain": jnp.clip(1.0 + 0.15 * jax.random.normal(seeds[16], (D,), jnp.float32), 0.25, 1.75).astype(jnp.bfloat16),
        "ln2_shift": centred(seeds[17], (D,), 0.3, 2.0, ((0, 32),)),
        "cross_wq": centred(seeds[18], (D, D), D ** -0.5, 0.1875, ((0, 32),)),
        "cross_bq": centred(seeds[19], (D,), 0.3, 2.0, ((0, 32),)),
        "cross_wk": centred(seeds[20], (D, D), D ** -0.5, 0.1875, ((0, 32),)),
        "cross_wv": centred(seeds[21], (D, D), D ** -0.5, 0.1875, ((0, 32),)),
        "cross_bv": centred(seeds[22], (D,), 0.3, 2.0, ((0, 32),)),
        "cross_wo": centred(seeds[23], (D, D), (D // 16) ** -0.5, 0.75, ((0, 32),)),
        "cross_bo": centred(seeds[24], (D,), 0.3, 2.0, ((0, 32),)),
        "ln3_gain": jnp.clip(1.0 + 0.15 * jax.random.normal(seeds[25], (D,), jnp.float32), 0.25, 1.75).astype(jnp.bfloat16),
        "ln3_shift": centred(seeds[26], (D,), 0.3, 2.0, ((0, 32),)),
        "ffn_w1": centred(seeds[27], (D, FF), D ** -0.5, 0.1875, ((0, 32),)),
        "ffn_b1": centred(seeds[28], (FF,), 0.3, 2.0, ((0, 32),)),
        "ffn_w2": centred(seeds[29], (FF, D), FF ** -0.5, 0.09375, ((0, 32),)),
        "ffn_b2": centred(seeds[30], (D,), 0.3, 2.0, ((0, 32),)),
    }


@jax.custom_vjp
def low(v):
    return lax.optimization_barrier(v.astype(jnp.bfloat16)).astype(jnp.float32)

@jax.custom_vjp
def low_back(v):
    return v

def low_keep(v):
    return (low(v), None)

def low_pass(kept, grad):
    return (grad,)

def back_keep(v):
    return (v, None)

def back_low(kept, grad):
    return (low(grad),)
low.defvjp(low_keep, low_pass)
low_back.defvjp(back_keep, back_low)
EPSILON = 1e-05
NEGATIVE = -1e+30
HIGHEST = lax.Precision.HIGHEST

def round_both(tensor):
    return low_back(low(tensor))

def product(left_side, right_side):
    return jnp.dot(left_side, right_side, precision=HIGHEST)

def layer_norm(tensor, norm_gain, norm_shift):
    centre = tensor - lax.optimization_barrier(jnp.mean(tensor, axis=-1, keepdims=True))
    spread = lax.optimization_barrier(jnp.mean(centre * centre, axis=-1, keepdims=True))
    return centre * lax.rsqrt(spread + EPSILON) * norm_gain + norm_shift

def split_heads(tensor):
    return tensor.reshape(tensor.shape[0], HEADS, -1)

def attend(queries, key_rows, value_rows, allowed):
    scaling = queries.shape[-1] ** (-0.5)
    scores = low_back(jnp.einsum('qhe,khe->hqk', queries, key_rows, precision=HIGHEST) * scaling)
    scores = jnp.where(allowed[None], scores, NEGATIVE)
    weights = low(jax.nn.softmax(scores, axis=-1))
    return jnp.einsum('hqk,khe->qhe', weights, value_rows, precision=HIGHEST)

def self_attend(queries, key_rows, value_rows):
    block_rows = min(512, LMAX)
    columns = jnp.arange(LMAX, dtype=jnp.int32)

    def one_block(block_index):
        start_row = (block_index * block_rows).astype(jnp.int32)
        query_part = lax.dynamic_slice_in_dim(queries, start_row, block_rows, 0)
        positions = start_row + jnp.arange(block_rows, dtype=jnp.int32)
        return attend(query_part, key_rows, value_rows, columns[None, :] <= positions[:, None])
    blocks = lax.map(jax.checkpoint(one_block), jnp.arange(LMAX // block_rows, dtype=jnp.int32))
    return blocks.reshape(LMAX, HEADS, -1)

def item_forward(params, unit_row, memory, length, text_length):
    gain_one, shift_one, self_q, self_qb, self_k, self_v, self_vb, self_o, self_ob, gain_two, shift_two, cross_q, cross_qb, cross_k, cross_v, cross_vb, cross_o, cross_ob, gain_three, shift_three, ffn_one, ffn_bone, ffn_two, ffn_btwo = params
    normed = low(layer_norm(unit_row, gain_one, shift_one))
    queries = round_both(product(normed, self_q) + self_qb)
    key_rows = round_both(product(normed, self_k))
    value_rows = round_both(product(normed, self_v) + self_vb)
    context = round_both(self_attend(split_heads(queries), split_heads(key_rows), split_heads(value_rows)).reshape(LMAX, D))
    after_self = unit_row + low_back(product(context, self_o) + self_ob)
    normed = low(layer_norm(after_self, gain_two, shift_two))
    queries = round_both(product(normed, cross_q) + cross_qb)
    key_rows = round_both(product(memory, cross_k))
    value_rows = round_both(product(memory, cross_v) + cross_vb)
    allowed = jnp.broadcast_to(jnp.arange(TXT, dtype=jnp.int32)[None, :] < text_length, (LMAX, TXT))
    context = round_both(attend(split_heads(queries), split_heads(key_rows), split_heads(value_rows), allowed).reshape(LMAX, D))
    after_cross = after_self + low_back(product(context, cross_o) + cross_ob)
    normed = low(layer_norm(after_cross, gain_three, shift_three))
    hidden = round_both(jax.nn.gelu(low_back(product(normed, ffn_one) + ffn_bone), approximate=True))
    branch = low_back(product(hidden, ffn_two) + ffn_btwo)
    valid_rows = (jnp.arange(LMAX, dtype=jnp.int32) < length).astype(jnp.float32)
    return (after_cross + branch) * valid_rows[:, None]

def forward(params, unit_states, dec_states, enc_states, unit_len, text_len, task_flag):
    memory = jnp.where((task_flag == 1)[:, None, None], dec_states, enc_states)

    def item_step(carried, item_data):
        return (carried, jax.checkpoint(item_forward)(params, item_data[0], item_data[1], item_data[2], item_data[3]))
    _, mixed = lax.scan(item_step, jnp.zeros((), jnp.float32), (unit_states, memory, unit_len, text_len))
    return mixed

def reference(unit_states, dec_states, enc_states, unit_len, text_len, task_flag, cotangent, ln1_gain, ln1_shift, self_wq, self_bq, self_wk, self_wv, self_bv, self_wo, self_bo, ln2_gain, ln2_shift, cross_wq, cross_bq, cross_wk, cross_wv, cross_bv, cross_wo, cross_bo, ln3_gain, ln3_shift, ffn_w1, ffn_b1, ffn_w2, ffn_b2):
    params = jax.tree.map(lambda tensor: tensor.astype(jnp.float32), (ln1_gain, ln1_shift, self_wq, self_bq, self_wk, self_wv, self_bv, self_wo, self_bo, ln2_gain, ln2_shift, cross_wq, cross_bq, cross_wk, cross_wv, cross_bv, cross_wo, cross_bo, ln3_gain, ln3_shift, ffn_w1, ffn_b1, ffn_w2, ffn_b2))

    def whole_layer(weights, units_float, dec_float, enc_float):
        return forward(weights, units_float, dec_float, enc_float, unit_len, text_len, task_flag)
    mixed, pullback = jax.vjp(whole_layer, params, unit_states.astype(jnp.float32), dec_states.astype(jnp.float32), enc_states.astype(jnp.float32))
    grad_params, grad_units, grad_dec, grad_enc = pullback(cotangent.astype(jnp.float32))
    return (mixed.astype(jnp.bfloat16), grad_units, grad_dec, grad_enc, grad_params[0], grad_params[1], grad_params[2], grad_params[3], grad_params[4], grad_params[5], grad_params[6], grad_params[7], grad_params[8], grad_params[9], grad_params[10], grad_params[11], grad_params[12], grad_params[13], grad_params[14], grad_params[15], grad_params[16], grad_params[17], grad_params[18], grad_params[19], grad_params[20], grad_params[21], grad_params[22], grad_params[23])
```

```python
import functools

import jax
import jax.numpy as jnp
from jax import lax
from jax.experimental import pallas as pl
from jax.experimental.pallas import tpu as pltpu
from jax.sharding import PartitionSpec as P

MIB=1<<20
NEGATIVE=-1e30
NN=(((1,),(0,)),((),()))
NT=(((1,),(1,)),((),()))
TN=(((0,),(0,)),((),()))
def dot(a,b,dims=NN):
    return lax.dot_general(a,b,dims,preferred_element_type=jnp.float32)

def head_masks(width):
    lane=lax.broadcasted_iota(jnp.int32,(1,128),1)
    return [((lane//width)==h) for h in range(128//width)]

def allowed(scores, first_row, first_col, causal, limit):
    cols=first_col+lax.broadcasted_iota(jnp.int32,scores.shape,1)
    if causal:
        rows=first_row+lax.broadcasted_iota(jnp.int32,scores.shape,0)
        keep=cols<=rows
    else:
        keep=cols<limit
    return jnp.where(keep,scores,NEGATIVE)

def fwd_kernel(causal, block, width, lim_ref, q_ref, k_ref, v_ref, ctx_ref, lse_ref):
    rows=q_ref.shape[0]; keys=k_ref.shape[0]
    masks=head_masks(width)
    k=k_ref[...]
    v=v_ref[...]
    vm=[jnp.where(m,v,jnp.zeros_like(v)) for m in masks]
    for i in range(rows//block):
        kend=(i+1)*block if causal else keys
        q=q_ref[pl.ds(i*block,block),:]*jnp.bfloat16(width**-0.5)
        ctx=None
        for h,m in enumerate(masks):
            s=dot(jnp.where(m,q,jnp.zeros_like(q)),k[:kend],NT)
            if causal:
                tail=allowed(s[:,kend-block:],0,0,True,None)
                s=tail if kend==block else jnp.concatenate([s[:,:kend-block],tail],1)
            else:
                s=allowed(s,0,0,False,lim_ref[0])
            top=jnp.max(s,axis=1,keepdims=True)
            p=jnp.exp(s-top)
            total=jnp.sum(p,axis=1,keepdims=True)
            part=dot(p.astype(jnp.bfloat16),vm[h][:kend])*(1.0/total)
            ctx=part if ctx is None else ctx+part
            lse=jnp.broadcast_to(top+jnp.log(total),(block,128))
            lse_ref[0,pl.ds(h,1),pl.ds(i*block,block)]=jnp.transpose(lse)[:1]
        ctx_ref[pl.ds(i*block,block),:]=ctx.astype(jnp.bfloat16)

def flash_fwd(q,k,v,limit,causal,block=256,width=64):
    rows,d=q.shape; keys=k.shape[0]
    pairs=d//128
    per=128//width
    spec=lambda n: pl.BlockSpec((n,128),lambda i,lim:(0,i))
    return pl.pallas_call(
        functools.partial(fwd_kernel,causal,block,width),
        grid_spec=pltpu.PrefetchScalarGridSpec(
            num_scalar_prefetch=1, grid=(pairs,),
            in_specs=[spec(rows),spec(keys),spec(keys)],
            out_specs=[spec(rows),pl.BlockSpec((1,per,rows),lambda i,lim:(i,0,0))]),
        out_shape=[jax.ShapeDtypeStruct((rows,d),jnp.bfloat16),jax.ShapeDtypeStruct((pairs,per,rows),jnp.float32)],
        compiler_params=pltpu.CompilerParams(vmem_limit_bytes=48*MIB),
        cost_estimate=pl.CostEstimate(flops=4*rows*keys*d//(2 if causal else 1),bytes_accessed=4*rows*d*2,transcendentals=rows*keys*16//(2 if causal else 1)),
        name="attend_causal" if causal else "attend_text",
    )(limit,q,k,v)

def bwd_kernel(causal, block, width, lim_ref, q_ref,k_ref,v_ref,g_ref,ctx_ref,lse_ref,dq_ref,dk_ref,dv_ref,dk_acc,dv_acc):
    rows=q_ref.shape[0]; keys=k_ref.shape[0]
    masks=head_masks(width)
    scale=jnp.bfloat16(width**-0.5)
    k=k_ref[...]; v=v_ref[...]
    km=[jnp.where(m,k*scale,jnp.zeros_like(k)) for m in masks]
    ones=[jnp.where(m,1.0,0.0) for m in masks]
    dk_acc[...]=jnp.zeros_like(dk_acc); dv_acc[...]=jnp.zeros_like(dv_acc)
    for i in range(rows//block):
        kend=(i+1)*block if causal else keys
        sl=pl.ds(i*block,block)
        q=q_ref[sl,:]*scale
        g=g_ref[sl,:]
        prod=g.astype(jnp.float32)*ctx_ref[sl,:].astype(jnp.float32)
        dq=None
        for h,m in enumerate(masks):
            qm=jnp.where(m,q,jnp.zeros_like(q))
            gm=jnp.where(m,g,jnp.zeros_like(g))
            delta=jnp.sum(jnp.where(m,prod,0.0),axis=1,keepdims=True)
            delta=jnp.transpose(jnp.broadcast_to(delta,(block,128)))[:1]
            lse=lse_ref[0,pl.ds(h,1),sl]
            s=dot(k[:kend],qm,NT)
            if causal:
                tail=s[kend-block:]
                r=lax.broadcasted_iota(jnp.int32,tail.shape,0)
                c=lax.broadcasted_iota(jnp.int32,tail.shape,1)
                tail=jnp.where(r<=c,tail,NEGATIVE)
                s=tail if kend==block else jnp.concatenate([s[:kend-block],tail],0)
            else:
                r=lax.broadcasted_iota(jnp.int32,s.shape,0)
                s=jnp.where(r<lim_ref[0],s,NEGATIVE)
            p=jnp.exp(s-lse)
            dp=dot(v[:kend],gm,NT)
            ds=(p*(dp-delta)).astype(jnp.bfloat16)
            dk_acc[:kend,:]+=dot(ds,qm)
            dv_acc[:kend,:]+=dot(p.astype(jnp.bfloat16),gm)
            part=dot(ds,km[h][:kend],TN)
            dq=part if dq is None else dq+part
        dq_ref[sl,:]=dq.astype(jnp.bfloat16)
    dk_ref[...]=dk_acc[...].astype(jnp.bfloat16)
    dv_ref[...]=dv_acc[...].astype(jnp.bfloat16)

def flash_bwd(q,k,v,g,ctx,lse,limit,causal,block=256,width=64):
    rows,d=q.shape; keys=k.shape[0]
    pairs=d//128; per=128//width
    spec=lambda n: pl.BlockSpec((n,128),lambda i,lim:(0,i))
    return pl.pallas_call(
        functools.partial(bwd_kernel,causal,block,width),
        grid_spec=pltpu.PrefetchScalarGridSpec(
            num_scalar_prefetch=1, grid=(pairs,),
            in_specs=[spec(rows),spec(keys),spec(keys),spec(rows),spec(rows),pl.BlockSpec((1,per,rows),lambda i,lim:(i,0,0))],
            out_specs=[spec(rows),spec(keys),spec(keys)],
            scratch_shapes=[pltpu.VMEM((keys,128),jnp.float32)]*2),
        out_shape=[jax.ShapeDtypeStruct((rows,d),jnp.bfloat16),jax.ShapeDtypeStruct((keys,d),jnp.bfloat16),jax.ShapeDtypeStruct((keys,d),jnp.bfloat16)],
        compiler_params=pltpu.CompilerParams(vmem_limit_bytes=48*MIB),
        cost_estimate=pl.CostEstimate(flops=10*rows*keys*d//(2 if causal else 1),bytes_accessed=8*rows*d*2,transcendentals=rows*keys*16//(2 if causal else 1)),
        name="attend_causal_back" if causal else "attend_text_back",
    )(limit,q,k,v,g,ctx,lse)

MESH=pl.DeviceIdType.MESH

def place():
    dp=lax.axis_index("dp"); fs=lax.axis_index("fsdp")
    return dp,fs,fs//2,fs%2

def turned(index,bit):
    return index+bit-2*bit*((index//bit)%2)

def greet(partners):
    barrier=pltpu.get_barrier_semaphore()
    for device in partners:
        pl.semaphore_signal(barrier,inc=1,device_id=device,device_id_type=MESH)
    pl.semaphore_wait(barrier,len(partners))

def gather_kernel(count,depth,*refs):
    ins,outs=refs[:count],refs[count:2*count]
    local,z_send,z_recv,a_send,a_recv,c_send,c_recv=refs[2*count:]
    dp,fs,z,c=place()
    ups=[((dp),lax.rem(z+k,depth)) for k in range(1,depth)]
    greet([(dp,lax.rem(z+k,depth)*2+c) for k in range(1,depth)]+[(turned(dp,1),fs),(turned(dp,2),fs),(dp,z*2+1-c)])
    sib=(dp,z*2+1-c)
    def line(w,k):
        return pltpu.make_async_remote_copy(ins[w],outs[w].at[dp,z,c],z_send.at[w,k-1],z_recv.at[w,k-1],(dp,lax.rem(z+k,depth)*2+c),MESH)
    def across(w,n,src_dp,bit):
        ref=outs[w].at[src_dp,:,c]
        return pltpu.make_async_remote_copy(ref,ref,a_send.at[w,n],a_recv.at[w,n],(turned(dp,bit),fs),MESH)
    def core(w,n,src_dp):
        ref=outs[w].at[src_dp,:,c]
        return pltpu.make_async_remote_copy(ref,ref,c_send.at[w,n],c_recv.at[w,n],sib,MESH)
    def own(w):
        return pltpu.make_async_copy(ins[w],outs[w].at[dp,z,c],local.at[w])
    for w in range(count):
        own(w).start()
        for k in range(1,depth): line(w,k).start()
    def first_bit(w): return 1+w%2
    def step0(w):
        own(w).wait()
        for k in range(1,depth): line(w,k).wait_recv()
        f,g=first_bit(w),3-first_bit(w)
        across(w,0,dp,f).start()
        across(w,1,dp,g).start()
        core(w,0,dp).start()
    def step1(w):
        f,g=first_bit(w),3-first_bit(w)
        across(w,0,dp,f).wait_recv()
        across(w,2,turned(dp,f),g).start()
        core(w,1,turned(dp,f)).start()
    def step2(w):
        f,g=first_bit(w),3-first_bit(w)
        across(w,1,dp,g).wait_recv()
        core(w,2,turned(dp,g)).start()
    def step3(w):
        f,g=first_bit(w),3-first_bit(w)
        across(w,2,turned(dp,f),g).wait_recv()
        core(w,3,turned(turned(dp,f),g)).start()
    for t in range(count+3):
        for n,step in enumerate((step0,step1,step2,step3)):
            if 0<=t-n<count: step(t-n)
    for w in range(count):
        f,g=first_bit(w),3-first_bit(w)
        for k in range(1,depth): line(w,k).wait_send()
        across(w,0,dp,f).wait_send(); across(w,1,dp,g).wait_send(); across(w,2,dp,g).wait_send()
        for n in range(4):
            core(w,n,dp).wait()

def gather(shards,depth,collective_id):
    count=len(shards)
    sem=pltpu.SemaphoreType.DMA
    outs=pl.pallas_call(
        functools.partial(gather_kernel,count,depth),
        in_specs=[pl.BlockSpec(memory_space=pl.ANY)]*count,
        out_specs=[pl.BlockSpec(memory_space=pl.ANY)]*count,
        out_shape=[jax.ShapeDtypeStruct((4,depth,2)+s.shape,s.dtype) for s in shards],
        scratch_shapes=[sem((count,)),sem((count,depth-1)),sem((count,depth-1)),sem((count,3)),sem((count,3)),sem((count,4)),sem((count,4))],
        compiler_params=pltpu.CompilerParams(collective_id=collective_id,has_side_effects=True),
        name="gather_rows",
    )(*shards)
    return [o.reshape((-1,)+s.shape[1:]) for o,s in zip(outs,shards)]

def reduce_kernel(count,depth,*refs):
    ins,outs=refs[:count],refs[count:2*count]
    held=refs[2*count:3*count]; r0=refs[3*count:4*count]; r1=refs[4*count:5*count]; r2=refs[5*count:6*count]; r3=refs[6*count:7*count]
    local,c_send,c_recv,a_send,a_recv,z_send,z_recv=refs[7*count:]
    dp,fs,z,c=place()
    hi,lo=dp//2,dp%2
    sib=(dp,z*2+1-c)
    greet([(dp,lax.rem(z+k,depth)*2+c) for k in range(1,depth)]+[(turned(dp,1),fs),(turned(dp,2),fs),sib])
    def own(w):
        return pltpu.make_async_copy(ins[w].at[:,:,:,c],held[w],local.at[w])
    def core(w):
        return pltpu.make_async_remote_copy(ins[w].at[:,:,:,1-c],r0[w],c_send.at[w],c_recv.at[w],sib,MESH)
    def first(w):
        if w%2: return pltpu.make_async_remote_copy(held[w].at[1-hi],r1[w],a_send.at[w,0],a_recv.at[w,0],(turned(dp,2),fs),MESH)
        return pltpu.make_async_remote_copy(held[w].at[:,1-lo],r1[w],a_send.at[w,0],a_recv.at[w,0],(turned(dp,1),fs),MESH)
    def second(w):
        if w%2: return pltpu.make_async_remote_copy(held[w].at[hi,1-lo],r2[w],a_send.at[w,1],a_recv.at[w,1],(turned(dp,1),fs),MESH)
        return pltpu.make_async_remote_copy(held[w].at[1-hi,lo],r2[w],a_send.at[w,1],a_recv.at[w,1],(turned(dp,2),fs),MESH)
    def line(w,k):
        return pltpu.make_async_remote_copy(held[w].at[hi,lo,lax.rem(z+k,depth)],r3[w].at[k-1],z_send.at[w,k-1],z_recv.at[w,k-1],(dp,lax.rem(z+k,depth)*2+c),MESH)
    def step0(w):
        own(w).wait(); core(w).wait_recv()
        def add(n,_):
            i,k=n//depth,n%depth
            held[w][i//2,i%2,k]=held[w][i//2,i%2,k]+r0[w][i//2,i%2,k]
            return 0
        lax.fori_loop(0,4*depth,add,0)
        first(w).start()
    def step1(w):
        first(w).wait_recv()
        def add(n,_):
            i,k=n//depth,n%depth
            if w%2: held[w][hi,i,k]=held[w][hi,i,k]+r1[w][i,k]
            else: held[w][i,lo,k]=held[w][i,lo,k]+r1[w][i,k]
            return 0
        lax.fori_loop(0,2*depth,add,0)
        second(w).start()
    def step2(w):
        second(w).wait_recv()
        def add(k,_):
            held[w][hi,lo,k]=held[w][hi,lo,k]+r2[w][k]
            return 0
        lax.fori_loop(0,depth,add,0)
        for k in range(1,depth): line(w,k).start()
    def step3(w):
        total=held[w][hi,lo,z].astype(jnp.float32)
        for k in range(1,depth):
            line(w,k).wait_recv()
            total=total+r3[w][k-1].astype(jnp.float32)
        outs[w][...]=total
    for w in range(count):
        core(w).start(); own(w).start()
    for t in range(count+3):
        for n,step in enumerate((step0,step1,step2,step3)):
            if 0<=t-n<count: step(t-n)
    for w in range(count):
        core(w).wait_send(); first(w).wait_send(); second(w).wait_send()
        for k in range(1,depth): line(w,k).wait_send()

def reduce_rows(partials,depth,collective_id):
    count=len(partials)
    sem=pltpu.SemaphoreType.DMA
    parts=[p.reshape((2,2,depth,2,p.shape[0]//(8*depth),p.shape[1])) for p in partials]
    tails=[p.shape[4:] for p in parts]
    vmem=lambda lead: [pltpu.VMEM(lead+t,p.dtype) for t,p in zip(tails,parts)]
    outs=pl.pallas_call(
        functools.partial(reduce_kernel,count,depth),
        in_specs=[pl.BlockSpec(memory_space=pl.ANY)]*count,
        out_specs=[pl.BlockSpec(memory_space=pltpu.VMEM)]*count,
        out_shape=[jax.ShapeDtypeStruct(t,jnp.float32) for t in tails],
        scratch_shapes=vmem((2,2,depth))+vmem((2,2,depth))+vmem((2,depth))+vmem((depth,))+vmem((depth-1,))
          +[sem((count,)),sem((count,)),sem((count,)),sem((count,2)),sem((count,2)),sem((count,depth-1)),sem((count,depth-1))],
        compiler_params=pltpu.CompilerParams(collective_id=collective_id,has_side_effects=True,vmem_limit_bytes=60*MIB),
        name="reduce_rows",
    )(*parts)
    return outs

AXES=("dp","fsdp")
EPSILON=1e-05

def layer_norm(tensor, gain, shift):
    centre=tensor-jnp.mean(tensor,axis=-1,keepdims=True)
    spread=jnp.mean(centre*centre,axis=-1,keepdims=True)
    return centre*lax.rsqrt(spread+EPSILON)*gain+shift

def layer_norm_back(tensor, gain, grad):
    centre=tensor-jnp.mean(tensor,axis=-1,keepdims=True)
    spread=jnp.mean(centre*centre,axis=-1,keepdims=True)
    inverse=lax.rsqrt(spread+EPSILON)
    hat=centre*inverse
    scaled=grad*gain
    pulled=inverse*(scaled-jnp.mean(scaled,axis=-1,keepdims=True)-hat*jnp.mean(scaled*hat,axis=-1,keepdims=True))
    return pulled,jnp.sum(grad*hat,axis=0),jnp.sum(grad,axis=0)

def low(tensor):
    return tensor.astype(jnp.bfloat16)

def columns(tensor):
    return jnp.sum(tensor.astype(jnp.float32),axis=0)

def gather_all(shards,depth,collective_id):
    if depth: return gather(shards,depth,collective_id)
    return [lax.all_gather(s,AXES,axis=0,tiled=True) for s in shards]

def reduce_all(partials,depth,collective_id):
    if depth: return reduce_rows(partials,depth,collective_id)
    return [lax.psum_scatter(p,AXES,scatter_dimension=0,tiled=True).astype(jnp.float32) for p in partials]

def pack_vectors(vectors,wide):
    flat=jnp.concatenate(list(vectors)+[wide])
    return jnp.pad(flat,(0,2048-flat.shape[0])).reshape(16,128)

def unpack_vectors(whole,devices,count):
    flat=whole.reshape(devices,2048)
    each=1024//devices
    vectors=flat[:,:count*each].reshape(devices,count,each).transpose(1,0,2).reshape(count,1024)
    wide=flat[:,count*each:(count+4)*each].reshape(4096)
    return vectors.astype(jnp.float32),wide.astype(jnp.float32)

def pack_grads(vectors,wide,devices):
    each=1024//devices
    flat=jnp.stack(vectors).reshape(len(vectors),devices,each).transpose(1,0,2).reshape(devices,-1)
    flat=jnp.concatenate([flat,wide.reshape(devices,4*each)],1)
    return jnp.pad(flat,((0,0),(0,1024-flat.shape[1]))).reshape(devices*8,128)

def shards(devices, depth, unit_states, dec_states, enc_states, unit_len, text_len, task_flag, cotangent,
    ln1_gain, ln1_shift, self_wq, self_bq, self_wk, self_wv, self_bv, self_wo, self_bo,
    ln2_gain, ln2_shift, cross_wq, cross_bq, cross_wk, cross_wv, cross_bv, cross_wo, cross_bo,
    ln3_gain, ln3_shift, ffn_w1, ffn_b1, ffn_w2, ffn_b2):
    w1=lax.all_gather(ffn_w1,AXES,axis=0,tiled=True)
    w2=lax.all_gather(ffn_w2,AXES,axis=0,tiled=True)
    small=pack_vectors([ln1_gain,ln1_shift,self_bq,self_bv,self_bo,ln2_gain,ln2_shift,cross_bq,cross_bv,cross_bo,ln3_gain,ln3_shift,ffn_b2],ffn_b1)
    small,wq,wk,wv,wo,cwq,cwk,cwv,cwo=gather_all([small,self_wq,self_wk,self_wv,self_wo,cross_wq,cross_wk,cross_wv,cross_wo],depth,1)
    vectors,b1=unpack_vectors(small,devices,13)
    g1,s1,bq,bv,bo,g2,s2,cbq,cbv,cbo,g3,s3,b2=[vectors[i] for i in range(13)]
    units=unit_states[0].astype(jnp.float32)
    memory=jnp.where(task_flag[0]==1,dec_states[0],enc_states[0])
    valid=(jnp.arange(units.shape[0],dtype=jnp.int32)<unit_len[0]).astype(jnp.float32)[:,None]
    n1=low(layer_norm(units,g1,s1))
    q=low(dot(n1,wq)+bq); k=low(dot(n1,wk)); v=low(dot(n1,wv)+bv)
    ctx,lse=flash_fwd(q,k,v,text_len,True)
    after_self=units+(dot(ctx,wo)+bo)
    n2=low(layer_norm(after_self,g2,s2))
    cq=low(dot(n2,cwq)+cbq); ck=low(dot(memory,cwk)); cv=low(dot(memory,cwv)+cbv)
    cctx,clse=flash_fwd(cq,ck,cv,text_len,False)
    after_cross=after_self+(dot(cctx,cwo)+cbo)
    n3=low(layer_norm(after_cross,g3,s3))
    pre=dot(n3,w1)+b1
    hidden=low(jax.nn.gelu(pre,approximate=True))
    mixed=low((after_cross+(dot(hidden,w2)+b2))*valid)
    top=cotangent[0].astype(jnp.float32)*valid
    gf=low(top)
    dw2=low(dot(hidden,gf,TN))
    _,gelu_pull=jax.vjp(functools.partial(jax.nn.gelu,approximate=True),pre)
    g_pre=low(gelu_pull(low(dot(gf,w2,NT)).astype(jnp.float32))[0])
    dw1=low(dot(n3,g_pre,TN))
    dw1=lax.psum_scatter(dw1,AXES,scatter_dimension=0,tiled=True).astype(jnp.float32)
    dw2=lax.psum_scatter(dw2,AXES,scatter_dimension=0,tiled=True).astype(jnp.float32)
    pulled,dg3,ds3=layer_norm_back(after_cross,g3,dot(g_pre,w1,NT))
    g_cross=top+pulled
    gc=low(g_cross)
    dcwo=low(dot(cctx,gc,TN))
    gcq,gck,gcv=flash_bwd(cq,ck,cv,low(dot(gc,cwo,NT)),cctx,clse,text_len,False)
    dcwq=low(dot(n2,gcq,TN)); dcwk=low(dot(memory,gck,TN)); dcwv=low(dot(memory,gcv,TN))
    g_memory=dot(gck,cwk,NT)+dot(gcv,cwv,NT)
    pulled,dg2,ds2=layer_norm_back(after_self,g2,dot(gcq,cwq,NT))
    g_self=g_cross+pulled
    gs=low(g_self)
    dwo=low(dot(ctx,gs,TN))
    gq,gk,gv=flash_bwd(q,k,v,low(dot(gs,wo,NT)),ctx,lse,text_len,True)
    dwq=low(dot(n1,gq,TN)); dwk=low(dot(n1,gk,TN)); dwv=low(dot(n1,gv,TN))
    pulled,dg1,ds1=layer_norm_back(units,g1,dot(gq,wq,NT)+dot(gk,wk,NT)+dot(gv,wv,NT))
    g_units=g_self+pulled
    is_dec=(task_flag[0]==1).astype(jnp.float32)
    grads=pack_grads([dg1,ds1,columns(gq),columns(gv),columns(gs),dg2,ds2,columns(gcq),columns(gcv),columns(gc),dg3,ds3,columns(gf)],columns(g_pre),devices)
    dcwo,dcwq,dcwk,dcwv,dwo,dwq,dwk,dwv,grads=reduce_all([dcwo,dcwq,dcwk,dcwv,dwo,dwq,dwk,dwv,grads],depth,2)
    each=1024//devices
    grads=grads.reshape(1024)
    ng=[grads[i*each:(i+1)*each] for i in range(13)]
    db1=grads[13*each:17*each]
    return (mixed[None],g_units[None],(g_memory*is_dec)[None],(g_memory*(1.0-is_dec))[None],
        ng[0],ng[1],dwq,ng[2],dwk,dwv,ng[3],dwo,ng[4],ng[5],ng[6],dcwq,ng[7],dcwk,dcwv,ng[8],dcwo,ng[9],ng[10],ng[11],dw1,db1,dw2,ng[12])

def solution(mesh):
    devices=mesh.shape["dp"]*mesh.shape["fsdp"]
    depth=mesh.shape["fsdp"]//2 if mesh.shape["dp"]==4 and (1024//devices)%16==0 else 0
    cube,flat,row=P(AXES,None,None),P(AXES),P(AXES,None)
    return jax.shard_map(
        functools.partial(shards,devices,depth),
        mesh=mesh,
        in_specs=(cube,)*3+(flat,)*3+(cube,flat,flat,row,flat,row,row,flat,row,flat,flat,flat,row,flat,row,row,flat,row,flat,flat,flat,row,flat,row,flat),
        out_specs=(cube,)*4+(flat,flat,row,flat,row,row,flat,row,flat,flat,flat,row,flat,row,row,flat,row,flat,flat,flat,row,flat,row,flat),
        check_vma=False,
    )
```

```python
import functools

import jax
import jax.numpy as jnp
from jax import lax
from jax.experimental import pallas as pl
from jax.experimental.pallas import tpu as pltpu
from jax.sharding import PartitionSpec as P

MIB=1<<20

NEGATIVE=-1e30
NN=(((1,),(0,)),((),()))
NT=(((1,),(1,)),((),()))
TN=(((0,),(0,)),((),()))
def dot(a,b,dims=NN):
    return lax.dot_general(a,b,dims,preferred_element_type=jnp.float32)

def head_masks(width):
    lane=lax.broadcasted_iota(jnp.int32,(1,128),1)
    return [((lane//width)==h) for h in range(128//width)]

def run_beside(plan,depth):
    begin,ticks,finish=plan
    step=pl.program_id(0); steps=pl.num_programs(0)
    @pl.when(step==0)
    def _():
        greet(depth)
        begin()
    for n in range(7):
        @pl.when(step==n+1)
        def _():
            if n<len(ticks): ticks[n]()
    def after():
        @pl.when(step==steps-1)
        def _():
            for tick in ticks[7:]: tick()
            finish()
    return after

def fwd_kernel(causal, block, width, moved, depth, lim_ref, q_ref, k_ref, v_ref, *refs):
    ctx_ref,lse_ref=refs[moved:moved+2]
    if moved:
        after=run_beside(gather_plan(refs[:moved],refs[moved+2:2*moved+2],refs[2*moved+2:],depth),depth)
    rows=q_ref.shape[0]; keys=k_ref.shape[0]
    masks=head_masks(width)
    k=k_ref[...]
    v=v_ref[...]
    vm=[jnp.where(m,v,jnp.zeros_like(v)) for m in masks]
    for i in range(rows//block):
        kend=(i+1)*block if causal else keys
        q=q_ref[pl.ds(i*block,block),:]*jnp.bfloat16(width**-0.5)
        ctx=None
        for h,m in enumerate(masks):
            s=dot(jnp.where(m,q,jnp.zeros_like(q)),k[:kend],NT)
            if causal:
                tail=s[:,kend-block:]
                r=lax.broadcasted_iota(jnp.int32,tail.shape,0)
                c=lax.broadcasted_iota(jnp.int32,tail.shape,1)
                tail=jnp.where(c<=r,tail,NEGATIVE)
                s=tail if kend==block else jnp.concatenate([s[:,:kend-block],tail],1)
            else:
                c=lax.broadcasted_iota(jnp.int32,s.shape,1)
                s=jnp.where(c<lim_ref[0],s,NEGATIVE)
            top=jnp.max(s,axis=1,keepdims=True)
            p=jnp.exp(s-top)
            total=jnp.sum(p,axis=1,keepdims=True)
            part=dot(p.astype(jnp.bfloat16),vm[h][:kend])*(1.0/total)
            ctx=part if ctx is None else ctx+part
            lse=jnp.broadcast_to(top+jnp.log(total),(block,128))
            lse_ref[0,pl.ds(h,1),pl.ds(i*block,block)]=jnp.transpose(lse)[:1]
        ctx_ref[pl.ds(i*block,block),:]=ctx.astype(jnp.bfloat16)
    if moved: after()

def flash_fwd(q,k,v,limit,causal,block=256,width=64,moves=(),depth=0,collective_id=None):
    rows,d=q.shape; keys=k.shape[0]
    pairs=d//128
    per=128//width
    count=len(moves)
    any_=pl.BlockSpec(memory_space=pl.ANY)
    spec=lambda n: pl.BlockSpec((n,128),lambda i,lim:(0,i))
    outs=pl.pallas_call(
        functools.partial(fwd_kernel,causal,block,width,count,depth),
        grid_spec=pltpu.PrefetchScalarGridSpec(
            num_scalar_prefetch=1, grid=(pairs,),
            in_specs=[spec(rows),spec(keys),spec(keys)]+[any_]*count,
            out_specs=[spec(rows),pl.BlockSpec((1,per,rows),lambda i,lim:(i,0,0))]+[any_]*count,
            scratch_shapes=gather_sems(count,depth) if count else []),
        out_shape=[jax.ShapeDtypeStruct((rows,d),jnp.bfloat16),jax.ShapeDtypeStruct((pairs,per,rows),jnp.float32)]+gather_shapes(moves,depth),
        compiler_params=pltpu.CompilerParams(vmem_limit_bytes=48*MIB,collective_id=collective_id,has_side_effects=count>0),
        cost_estimate=pl.CostEstimate(flops=4*rows*keys*d//(2 if causal else 1),bytes_accessed=4*rows*d*2,transcendentals=rows*keys*16//(2 if causal else 1)),
        name="attend_causal" if causal else "attend_text",
    )(limit,q,k,v,*moves)
    return outs[0],outs[1],gather_result(outs[2:],moves)

def bwd_kernel(causal, block, width, moved, depth, lim_ref, q_ref,k_ref,v_ref,g_ref,ctx_ref,lse_ref,*refs):
    dq_ref,dk_ref,dv_ref=refs[moved:moved+3]
    dk_acc,dv_acc=refs[2*moved+3:2*moved+5]
    if moved:
        after=run_beside(reduce_plan(refs[:moved],refs[moved+3:2*moved+3],refs[2*moved+5:],depth),depth)
    rows=q_ref.shape[0]; keys=k_ref.shape[0]
    masks=head_masks(width)
    scale=jnp.bfloat16(width**-0.5)
    k=k_ref[...]; v=v_ref[...]
    km=[jnp.where(m,k*scale,jnp.zeros_like(k)) for m in masks]
    dk_acc[...]=jnp.zeros_like(dk_acc); dv_acc[...]=jnp.zeros_like(dv_acc)
    for i in range(rows//block):
        kend=(i+1)*block if causal else keys
        sl=pl.ds(i*block,block)
        q=q_ref[sl,:]*scale
        g=g_ref[sl,:]
        prod=g.astype(jnp.float32)*ctx_ref[sl,:].astype(jnp.float32)
        dq=None
        for h,m in enumerate(masks):
            qm=jnp.where(m,q,jnp.zeros_like(q))
            gm=jnp.where(m,g,jnp.zeros_like(g))
            delta=jnp.sum(jnp.where(m,prod,0.0),axis=1,keepdims=True)
            delta=jnp.transpose(jnp.broadcast_to(delta,(block,128)))[:1]
            lse=lse_ref[0,pl.ds(h,1),sl]
            s=dot(k[:kend],qm,NT)
            if causal:
                tail=s[kend-block:]
                r=lax.broadcasted_iota(jnp.int32,tail.shape,0)
                c=lax.broadcasted_iota(jnp.int32,tail.shape,1)
                tail=jnp.where(r<=c,tail,NEGATIVE)
                s=tail if kend==block else jnp.concatenate([s[:kend-block],tail],0)
            else:
                r=lax.broadcasted_iota(jnp.int32,s.shape,0)
                s=jnp.where(r<lim_ref[0],s,NEGATIVE)
            p=jnp.exp(s-lse)
            dp=dot(v[:kend],gm,NT)
            ds=(p*(dp-delta)).astype(jnp.bfloat16)
            dk_acc[:kend,:]+=dot(ds,qm)
            dv_acc[:kend,:]+=dot(p.astype(jnp.bfloat16),gm)
            part=dot(ds,km[h][:kend],TN)
            dq=part if dq is None else dq+part
        dq_ref[sl,:]=dq.astype(jnp.bfloat16)
    dk_ref[...]=dk_acc[...].astype(jnp.bfloat16)
    dv_ref[...]=dv_acc[...].astype(jnp.bfloat16)
    if moved: after()

def flash_bwd(q,k,v,g,ctx,lse,limit,causal,block=256,width=64,moves=(),depth=0,collective_id=None):
    rows,d=q.shape; keys=k.shape[0]
    pairs=d//128; per=128//width
    count=len(moves)
    parts=reduce_parts(moves,depth)
    kinds=[p.shape[4:]+(p.dtype,) for p in parts]
    any_=pl.BlockSpec(memory_space=pl.ANY)
    spec=lambda n: pl.BlockSpec((n,128),lambda i,lim:(0,i))
    outs=pl.pallas_call(
        functools.partial(bwd_kernel,causal,block,width,count,depth),
        grid_spec=pltpu.PrefetchScalarGridSpec(
            num_scalar_prefetch=1, grid=(pairs,),
            in_specs=[spec(rows),spec(keys),spec(keys),spec(rows),spec(rows),pl.BlockSpec((1,per,rows),lambda i,lim:(i,0,0))]+[any_]*count,
            out_specs=[spec(rows),spec(keys),spec(keys)]+[pl.BlockSpec(k[:2],lambda i,lim:(0,0)) for k in kinds],
            scratch_shapes=[pltpu.VMEM((keys,128),jnp.float32)]*2+(reduce_scratch(kinds,depth) if count else [])),
        out_shape=[jax.ShapeDtypeStruct((rows,d),jnp.bfloat16),jax.ShapeDtypeStruct((keys,d),jnp.bfloat16),jax.ShapeDtypeStruct((keys,d),jnp.bfloat16)]
          +[jax.ShapeDtypeStruct(k[:2],jnp.float32) for k in kinds],
        compiler_params=pltpu.CompilerParams(vmem_limit_bytes=56*MIB,collective_id=collective_id,has_side_effects=count>0),
        cost_estimate=pl.CostEstimate(flops=10*rows*keys*d//(2 if causal else 1),bytes_accessed=8*rows*d*2,transcendentals=rows*keys*16//(2 if causal else 1)),
        name="attend_causal_back" if causal else "attend_text_back",
    )(limit,q,k,v,g,ctx,lse,*parts)
    return outs[0],outs[1],outs[2],outs[3:]

MESH=pl.DeviceIdType.MESH
DMA=pltpu.SemaphoreType.DMA

def place():
    dp=lax.axis_index("dp"); fs=lax.axis_index("fsdp")
    return dp,fs,fs//2,fs%2

def turned(index,bit):
    return index+bit-2*bit*((index//bit)%2)

def greet(depth):
    dp,fs,z,c=place()
    partners=[(dp,lax.rem(z+k,depth)*2+c) for k in range(1,depth)]+[(turned(dp,1),fs),(turned(dp,2),fs),(dp,z*2+1-c)]
    barrier=pltpu.get_barrier_semaphore()
    for device in partners:
        pl.semaphore_signal(barrier,inc=1,device_id=device,device_id_type=MESH)
    pl.semaphore_wait(barrier,len(partners))

def gather_sems(count,depth):
    return [DMA((count,)),DMA((count,depth-1)),DMA((count,depth-1)),DMA((count,3)),DMA((count,3)),DMA((count,4)),DMA((count,4))]

def gather_plan(ins,outs,sems,depth):
    count=len(ins)
    local,z_send,z_recv,a_send,a_recv,c_send,c_recv=sems
    dp,fs,z,c=place()
    def line(w,k):
        return pltpu.make_async_remote_copy(ins[w],outs[w].at[dp,z,c],z_send.at[w,k-1],z_recv.at[w,k-1],(dp,lax.rem(z+k,depth)*2+c),MESH)
    def across(w,n,src_dp,bit):
        ref=outs[w].at[src_dp,:,c]
        return pltpu.make_async_remote_copy(ref,ref,a_send.at[w,n],a_recv.at[w,n],(turned(dp,bit),fs),MESH)
    def core(w,n,src_dp):
        ref=outs[w].at[src_dp,:,c]
        return pltpu.make_async_remote_copy(ref,ref,c_send.at[w,n],c_recv.at[w,n],(dp,z*2+1-c),MESH)
    def own(w):
        return pltpu.make_async_copy(ins[w],outs[w].at[dp,z,c],local.at[w])
    def bits(w):
        return 1+w%2,2-w%2
    def step0(w):
        f,g=bits(w)
        own(w).wait()
        for k in range(1,depth): line(w,k).wait_recv()
        across(w,0,dp,f).start()
        across(w,1,dp,g).start()
        core(w,0,dp).start()
    def step1(w):
        f,g=bits(w)
        across(w,0,dp,f).wait_recv()
        across(w,2,turned(dp,f),g).start()
        core(w,1,turned(dp,f)).start()
    def step2(w):
        f,g=bits(w)
        across(w,1,dp,g).wait_recv()
        core(w,2,turned(dp,g)).start()
    def step3(w):
        f,g=bits(w)
        across(w,2,turned(dp,f),g).wait_recv()
        core(w,3,turned(turned(dp,f),g)).start()
    def begin():
        for w in range(count):
            own(w).start()
            for k in range(1,depth): line(w,k).start()
    def tick(t):
        for n,step in enumerate((step0,step1,step2,step3)):
            if 0<=t-n<count: step(t-n)
    def finish():
        for w in range(count):
            f,g=bits(w)
            for k in range(1,depth): line(w,k).wait_send()
            across(w,0,dp,f).wait_send(); across(w,1,dp,g).wait_send(); across(w,2,dp,g).wait_send()
            for n in range(4): core(w,n,dp).wait()
    return begin,[functools.partial(tick,t) for t in range(count+3)],finish

def reduce_scratch(kinds,depth):
    count=len(kinds)
    vmem=lambda *lead: [pltpu.VMEM(lead+(r,n),d) for r,n,d in kinds]
    return (vmem(2,2,depth)+vmem(2,2,depth)+vmem(2,depth)+vmem(depth)+vmem(depth-1)
      +[DMA((count,)),DMA((count,)),DMA((count,)),DMA((count,2)),DMA((count,2)),DMA((count,depth-1)),DMA((count,depth-1))])

def reduce_plan(ins,outs,scratch,depth):
    count=len(ins)
    held,r0,r1,r2,r3=(scratch[n*count:(n+1)*count] for n in range(5))
    local,c_send,c_recv,a_send,a_recv,z_send,z_recv=scratch[5*count:]
    dp,fs,z,c=place()
    hi,lo=dp//2,dp%2
    def own(w):
        return pltpu.make_async_copy(ins[w].at[:,:,:,c],held[w],local.at[w])
    def core(w):
        return pltpu.make_async_remote_copy(ins[w].at[:,:,:,1-c],r0[w],c_send.at[w],c_recv.at[w],(dp,z*2+1-c),MESH)
    def first(w):
        if w%2: return pltpu.make_async_remote_copy(held[w].at[1-hi],r1[w],a_send.at[w,0],a_recv.at[w,0],(turned(dp,2),fs),MESH)
        return pltpu.make_async_remote_copy(held[w].at[:,1-lo],r1[w],a_send.at[w,0],a_recv.at[w,0],(turned(dp,1),fs),MESH)
    def second(w):
        if w%2: return pltpu.make_async_remote_copy(held[w].at[hi,1-lo],r2[w],a_send.at[w,1],a_recv.at[w,1],(turned(dp,1),fs),MESH)
        return pltpu.make_async_remote_copy(held[w].at[1-hi,lo],r2[w],a_send.at[w,1],a_recv.at[w,1],(turned(dp,2),fs),MESH)
    def line(w,k):
        return pltpu.make_async_remote_copy(held[w].at[hi,lo,lax.rem(z+k,depth)],r3[w].at[k-1],z_send.at[w,k-1],z_recv.at[w,k-1],(dp,lax.rem(z+k,depth)*2+c),MESH)
    def step0(w):
        own(w).wait(); core(w).wait_recv()
        def add(n,_):
            i,k=n//depth,n%depth
            held[w][i//2,i%2,k]=held[w][i//2,i%2,k]+r0[w][i//2,i%2,k]
            return 0
        lax.fori_loop(0,4*depth,add,0)
        first(w).start()
    def step1(w):
        first(w).wait_recv()
        def add(n,_):
            i,k=n//depth,n%depth
            if w%2: held[w][hi,i,k]=held[w][hi,i,k]+r1[w][i,k]
            else: held[w][i,lo,k]=held[w][i,lo,k]+r1[w][i,k]
            return 0
        lax.fori_loop(0,2*depth,add,0)
        second(w).start()
    def step2(w):
        second(w).wait_recv()
        def add(k,_):
            held[w][hi,lo,k]=held[w][hi,lo,k]+r2[w][k]
            return 0
        lax.fori_loop(0,depth,add,0)
        for k in range(1,depth): line(w,k).start()
    def step3(w):
        total=held[w][hi,lo,z].astype(jnp.float32)
        for k in range(1,depth):
            line(w,k).wait_recv()
            total=total+r3[w][k-1].astype(jnp.float32)
        outs[w][...]=total
    def begin():
        for w in range(count):
            core(w).start(); own(w).start()
    def tick(t):
        for n,step in enumerate((step0,step1,step2,step3)):
            if 0<=t-n<count: step(t-n)
    def finish():
        for w in range(count):
            core(w).wait_send(); first(w).wait_send(); second(w).wait_send()
            for k in range(1,depth): line(w,k).wait_send()
    return begin,[functools.partial(tick,t) for t in range(count+3)],finish

def gather_shapes(shards,depth):
    return [jax.ShapeDtypeStruct((4,depth,2)+s.shape,s.dtype) for s in shards]

def gather_result(outs,shards):
    return [o.reshape((-1,)+s.shape[1:]) for o,s in zip(outs,shards)]

def reduce_parts(partials,depth):
    return [p.reshape((2,2,depth,2,p.shape[0]//(8*depth),p.shape[1])) for p in partials]

def first_kernel(count,lines,depth,*refs):
    ins,vectors,wide=refs[:count],refs[count:count+lines],refs[count+lines]
    refs=refs[count+lines+1:]
    outs,table,long=refs[:count],refs[count],refs[count+1]
    packed,every=refs[count+2:count+4]
    each=vectors[0].shape[1]
    greet(depth)
    packed[...]=jnp.zeros_like(packed)
    for n in range(lines): packed[n:n+1,:each]=vectors[n][...].astype(jnp.float32)
    packed[lines:lines+1,:]=wide[...].astype(jnp.float32)
    begin,ticks,finish=gather_plan([packed]+list(ins),[every]+list(outs),refs[count+4:],depth)
    begin()
    for tick in ticks: tick()
    finish()
    lane=lax.broadcasted_iota(jnp.int32,(16,128),1)
    group=128//each
    def device(n): return every[n//(2*depth),(n//2)%depth,n%2]
    for m in range(8*depth//group):
        tile=device(m*group)
        for r in range(1,group):
            tile=jnp.where(lane>=r*each,pltpu.roll(device(m*group+r),r*each,1),tile)
        table[:,m*128:(m+1)*128]=tile
    for n in range(8*depth):
        long[:,n*128:(n+1)*128]=device(n)[lines:lines+1]

def gather_first(shards,vectors,wide,depth,collective_id):
    count=len(shards); lines=len(vectors)
    any_=pl.BlockSpec(memory_space=pl.ANY); vm=pl.BlockSpec(memory_space=pltpu.VMEM)
    total=vectors[0].shape[0]*8*depth
    outs=pl.pallas_call(
        functools.partial(first_kernel,count,lines,depth),
        in_specs=[any_]*count+[vm]*(lines+1),
        out_specs=[any_]*count+[vm]*2,
        out_shape=gather_shapes(shards,depth)+[jax.ShapeDtypeStruct((16,total),jnp.float32),jax.ShapeDtypeStruct((1,128*8*depth),jnp.float32)],
        scratch_shapes=[pltpu.VMEM((16,128),jnp.float32),pltpu.VMEM((4,depth,2,16,128),jnp.float32)]+gather_sems(count+1,depth),
        compiler_params=pltpu.CompilerParams(collective_id=collective_id,has_side_effects=True),
        name="gather_first",
    )(*shards,*[v[None] for v in vectors],wide[None])
    return gather_result(outs[:count],shards)+list(outs[count:])

def last_kernel(count,depth,*refs):
    ins,outs,scratch=refs[:count],refs[count:2*count],refs[2*count:]
    greet(depth)
    begin,ticks,finish=reduce_plan(ins,outs,scratch,depth)
    begin()
    for tick in ticks: tick()
    finish()

def reduce_rows(partials,depth,collective_id):
    count=len(partials)
    parts=reduce_parts(partials,depth)
    kinds=[p.shape[4:]+(p.dtype,) for p in parts]
    return pl.pallas_call(
        functools.partial(last_kernel,count,depth),
        in_specs=[pl.BlockSpec(memory_space=pl.ANY)]*count,
        out_specs=[pl.BlockSpec(memory_space=pltpu.VMEM)]*count,
        out_shape=[jax.ShapeDtypeStruct(k[:2],jnp.float32) for k in kinds],
        scratch_shapes=reduce_scratch(kinds,depth),
        compiler_params=pltpu.CompilerParams(collective_id=collective_id,has_side_effects=True,vmem_limit_bytes=60*MIB),
        name="reduce_rows",
    )(*parts)

EPSILON=1e-05
def normal(tensor):
    centre=tensor-jnp.mean(tensor,axis=-1,keepdims=True)
    spread=jnp.mean(centre*centre,axis=-1,keepdims=True)
    inverse=lax.rsqrt(spread+EPSILON)
    return centre*inverse,inverse

def pull_norm(hat,inverse,gain,grad):
    scaled=grad*gain
    return inverse*(scaled-jnp.mean(scaled,axis=-1,keepdims=True)-hat*jnp.mean(scaled*hat,axis=-1,keepdims=True))

def ffn_kernel(strip, length_ref, after_ref, cot_ref, w1_ref, w2_ref, b1_ref, vec_ref,
               mixed_ref, grad_ref, dw1_ref, dw2_ref, db1_ref, dvec_ref, n3, n3t, gf, branch, gn):
    j=pl.program_id(0)
    rows=after_ref.shape[0]
    gain,shift,b2=vec_ref[0:1,:],vec_ref[1:2,:],vec_ref[2:3,:]
    def live(r):
        return (r*strip+lax.broadcasted_iota(jnp.int32,(strip,1),0)<length_ref[0]).astype(jnp.float32)
    @pl.when(j==0)
    def _():
        def one(r,total):
            sl=pl.ds(r*strip,strip)
            hat,_=normal(after_ref[sl,:])
            n3[sl,:]=(hat*gain+shift).astype(jnp.bfloat16)
            top=(cot_ref[sl,:].astype(jnp.float32)*live(r)).astype(jnp.bfloat16)
            gf[sl,:]=top
            return total+jnp.sum(top.astype(jnp.float32),axis=0,keepdims=True)
        dvec_ref[2:3,:]=lax.fori_loop(0,rows//strip,one,jnp.zeros((1,after_ref.shape[1]),jnp.float32))
        n3t[...]=jnp.transpose(n3[...])
        branch[...]=jnp.zeros_like(branch); gn[...]=jnp.zeros_like(gn)
    w1=w1_ref[...]; w2=w2_ref[...]
    pre=dot(n3[...],w1)+b1_ref[...]
    back=dot(gf[...],w2,NT).astype(jnp.bfloat16).astype(jnp.float32)
    root=0.7978845608028654
    square=pre*pre
    t=jnp.tanh(root*pre*(1.0+0.044715*square))
    half=0.5*(1.0+t)
    hidden=(pre*half).astype(jnp.bfloat16)
    slope=half+0.5*pre*(1.0-t*t)*(root*(1.0+3*0.044715*square))
    g_pre=(back*slope).astype(jnp.bfloat16)
    db1_ref[...]=jnp.sum(g_pre.astype(jnp.float32),axis=0,keepdims=True)
    branch[...]+=dot(hidden,w2)
    dw2_ref[...]=dot(hidden,gf[...],TN).astype(jnp.bfloat16)
    dw1_ref[...]=dot(n3t[...],g_pre).astype(jnp.bfloat16)
    gn[...]+=dot(g_pre,w1,NT)
    @pl.when(j==pl.num_programs(0)-1)
    def _():
        def one(r,totals):
            sl=pl.ds(r*strip,strip)
            valid=live(r)
            after=after_ref[sl,:]
            mixed_ref[sl,:]=((after+(branch[sl,:]+b2))*valid).astype(jnp.bfloat16)
            hat,inverse=normal(after)
            grad=gn[sl,:]
            grad_ref[sl,:]=cot_ref[sl,:].astype(jnp.float32)*valid+pull_norm(hat,inverse,gain,grad)
            return totals[0]+jnp.sum(grad*hat,axis=0,keepdims=True),totals[1]+jnp.sum(grad,axis=0,keepdims=True)
        zero=jnp.zeros((1,after_ref.shape[1]),jnp.float32)
        dg,ds=lax.fori_loop(0,rows//strip,one,(zero,zero))
        dvec_ref[0:1,:]=dg
        dvec_ref[1:2,:]=ds

def feed_forward(after,cot,length,w1,w2,b1,vec,block=512,strip=128):
    rows,d=after.shape; ff=w1.shape[1]
    once=lambda shape: pl.BlockSpec(shape,lambda j,n:(0,0),pipeline_mode=pl.Buffered(1))
    keep=lambda shape: pl.BlockSpec(shape,lambda j,n:(0,0))
    wide=pl.BlockSpec((d,block),lambda j,n:(0,j)); tall=pl.BlockSpec((block,d),lambda j,n:(j,0)); line=pl.BlockSpec((1,block),lambda j,n:(0,j))
    bf=jnp.bfloat16; f32=jnp.float32
    return pl.pallas_call(
        functools.partial(ffn_kernel,strip),
        grid_spec=pltpu.PrefetchScalarGridSpec(
            num_scalar_prefetch=1,grid=(ff//block,),
            in_specs=[once((rows,d)),once((rows,d)),wide,tall,line,once(vec.shape)],
            out_specs=[keep((rows,d)),keep((rows,d)),wide,tall,line,keep((8,d))],
            scratch_shapes=[pltpu.VMEM((rows,d),bf),pltpu.VMEM((d,rows),bf),pltpu.VMEM((rows,d),bf),pltpu.VMEM((rows,d),f32),pltpu.VMEM((rows,d),f32)]),
        out_shape=[jax.ShapeDtypeStruct((rows,d),bf),jax.ShapeDtypeStruct((rows,d),f32),jax.ShapeDtypeStruct((d,ff),bf),jax.ShapeDtypeStruct((ff,d),bf),jax.ShapeDtypeStruct((1,ff),f32),jax.ShapeDtypeStruct((8,d),f32)],
        compiler_params=pltpu.CompilerParams(vmem_limit_bytes=60*MIB),
        cost_estimate=pl.CostEstimate(flops=12*rows*d*ff,bytes_accessed=4*d*ff*2+rows*d*12,transcendentals=rows*ff),
        name="feed_forward",
    )(length,after,cot,w1,w2,b1,vec)

AXES=("dp","fsdp")

def layer_norm(tensor, gain, shift):
    return normal(tensor)[0]*gain+shift

def layer_norm_back(tensor, gain, grad):
    hat,inverse=normal(tensor)
    return pull_norm(hat,inverse,gain,grad),jnp.sum(grad*hat,axis=0),jnp.sum(grad,axis=0)

def low(tensor):
    return tensor.astype(jnp.bfloat16)

def columns(tensor):
    return jnp.sum(tensor.astype(jnp.float32),axis=0)

def gather_all(shards):
    return [lax.all_gather(s,AXES,axis=0,tiled=True) for s in shards]

def reduce_all(partials):
    return [lax.psum_scatter(p,AXES,scatter_dimension=0,tiled=True).astype(jnp.float32) for p in partials]

def gather_vectors(vectors,wide):
    rows=jnp.stack([jnp.pad(v,(0,128-v.shape[0])) for v in list(vectors)+[wide]])
    rows=jnp.pad(rows,((0,15-len(vectors)),(0,0)))
    whole=lax.all_gather(rows,AXES).astype(jnp.float32)
    return whole[:,:,:vectors[0].shape[0]].transpose(1,0,2).reshape(16,-1),whole[:,len(vectors),:wide.shape[0]].reshape(1,-1)

def pack_grads(vectors,wide,devices):
    each=1024//devices
    flat=jnp.stack(vectors).reshape(len(vectors),devices,each).transpose(1,0,2).reshape(devices,-1)
    flat=jnp.concatenate([flat,wide.reshape(devices,4*each)],1)
    return jnp.pad(flat,((0,0),(0,1024-flat.shape[1]))).reshape(devices*8,128)

def shards(devices, depth, unit_states, dec_states, enc_states, unit_len, text_len, task_flag, cotangent,
    ln1_gain, ln1_shift, self_wq, self_bq, self_wk, self_wv, self_bv, self_wo, self_bo,
    ln2_gain, ln2_shift, cross_wq, cross_bq, cross_wk, cross_wv, cross_bv, cross_wo, cross_bo,
    ln3_gain, ln3_shift, ffn_w1, ffn_b1, ffn_w2, ffn_b2):
    w1=lax.all_gather(ffn_w1,AXES,axis=0,tiled=True)
    w2=lax.all_gather(ffn_w2,AXES,axis=0,tiled=True)
    small=[ln1_gain,ln1_shift,self_bq,self_bv,self_bo,ln2_gain,ln2_shift,cross_bq,cross_bv,cross_bo,ln3_gain,ln3_shift,ffn_b2]
    late=[self_wo,cross_wq,cross_wk,cross_wv,cross_wo]
    if depth:
        wq,wk,wv,vectors,b1=gather_first([self_wq,self_wk,self_wv],small,ffn_b1,depth,1)
    else:
        wq,wk,wv,*late=gather_all([self_wq,self_wk,self_wv]+late)
        vectors,b1=gather_vectors(small,ffn_b1)
    g1,s1,bq,bv,bo,g2,s2,cbq,cbv,cbo,g3,s3,b2=[vectors[i] for i in range(13)]
    units=unit_states[0].astype(jnp.float32)
    memory=jnp.where(task_flag[0]==1,dec_states[0],enc_states[0])
    n1=low(layer_norm(units,g1,s1))
    q=low(dot(n1,wq)+bq); k=low(dot(n1,wk)); v=low(dot(n1,wv)+bv)
    if depth: ctx,lse,late=flash_fwd(q,k,v,text_len,True,moves=late,depth=depth,collective_id=2)
    else: ctx,lse,_=flash_fwd(q,k,v,text_len,True)
    wo,cwq,cwk,cwv,cwo=late
    after_self=units+(dot(ctx,wo)+bo)
    n2=low(layer_norm(after_self,g2,s2))
    cq=low(dot(n2,cwq)+cbq); ck=low(dot(memory,cwk)); cv=low(dot(memory,cwv)+cbv)
    cctx,clse,_=flash_fwd(cq,ck,cv,text_len,False)
    after_cross=after_self+(dot(cctx,cwo)+cbo)
    mixed,g_cross,dw1,dw2,db1,dvec=feed_forward(after_cross,cotangent[0],unit_len,w1,w2,b1,jnp.concatenate([vectors[10:13],jnp.zeros((5,1024),jnp.float32)]))
    dw1,dw2=reduce_all([dw1,dw2])
    gc=low(g_cross)
    dcwo=low(dot(cctx,gc,TN))
    gcq,gck,gcv,_=flash_bwd(cq,ck,cv,low(dot(gc,cwo,NT)),cctx,clse,text_len,False)
    dcwq=low(dot(n2,gcq,TN)); dcwk=low(dot(memory,gck,TN)); dcwv=low(dot(memory,gcv,TN))
    g_memory=dot(gck,cwk,NT)+dot(gcv,cwv,NT)
    pulled,dg2,ds2=layer_norm_back(after_self,g2,dot(gcq,cwq,NT))
    g_self=g_cross+pulled
    gs=low(g_self)
    dwo=low(dot(ctx,gs,TN))
    early=[dcwo,dcwq,dcwk,dcwv,dwo]
    if depth: gq,gk,gv,early=flash_bwd(q,k,v,low(dot(gs,wo,NT)),ctx,lse,text_len,True,moves=early,depth=depth,collective_id=3)
    else: gq,gk,gv,_=flash_bwd(q,k,v,low(dot(gs,wo,NT)),ctx,lse,text_len,True)
    dwq=low(dot(n1,gq,TN)); dwk=low(dot(n1,gk,TN)); dwv=low(dot(n1,gv,TN))
    pulled,dg1,ds1=layer_norm_back(units,g1,dot(gq,wq,NT)+dot(gk,wk,NT)+dot(gv,wv,NT))
    g_units=g_self+pulled
    is_dec=(task_flag[0]==1).astype(jnp.float32)
    grads=pack_grads([dg1,ds1,columns(gq),columns(gv),columns(gs),dg2,ds2,columns(gcq),columns(gcv),columns(gc),dvec[0],dvec[1],dvec[2]],db1[0],devices)
    if depth: dwq,dwk,dwv,grads=reduce_rows([dwq,dwk,dwv,grads],depth,4)
    else: dwq,dwk,dwv,grads,*early=reduce_all([dwq,dwk,dwv,grads]+early)
    dcwo,dcwq,dcwk,dcwv,dwo=early
    each=1024//devices
    grads=grads.reshape(1024)
    ng=[grads[i*each:(i+1)*each] for i in range(13)]
    db1=grads[13*each:17*each]
    return (mixed[None],g_units[None],(g_memory*is_dec)[None],(g_memory*(1.0-is_dec))[None],
        ng[0],ng[1],dwq,ng[2],dwk,dwv,ng[3],dwo,ng[4],ng[5],ng[6],dcwq,ng[7],dcwk,dcwv,ng[8],dcwo,ng[9],ng[10],ng[11],dw1,db1,dw2,ng[12])

def solution(mesh):
    devices=mesh.shape["dp"]*mesh.shape["fsdp"]
    depth=mesh.shape["fsdp"]//2 if mesh.shape["dp"]==4 and (1024//devices)%16==0 else 0
    cube,flat,row=P(AXES,None,None),P(AXES),P(AXES,None)
    return jax.shard_map(
        functools.partial(shards,devices,depth),
        mesh=mesh,
        in_specs=(cube,)*3+(flat,)*3+(cube,flat,flat,row,flat,row,row,flat,row,flat,flat,flat,row,flat,row,row,flat,row,flat,flat,flat,row,flat,row,flat),
        out_specs=(cube,)*4+(flat,flat,row,flat,row,row,flat,row,flat,flat,flat,row,flat,row,row,flat,row,flat,flat,flat,row,flat,row,flat),
        check_vma=False,
    )
```

```python
import functools

import jax
import jax.numpy as jnp
from jax import lax
from jax.experimental import pallas as pl
from jax.experimental.pallas import tpu as pltpu
from jax.sharding import PartitionSpec as P

MIB=1<<20

NEGATIVE=-1e30
NN=(((1,),(0,)),((),()))
NT=(((1,),(1,)),((),()))
TN=(((0,),(0,)),((),()))
def dot(a,b,dims=NN):
    return lax.dot_general(a,b,dims,preferred_element_type=jnp.float32)

def head_masks(width):
    lane=lax.broadcasted_iota(jnp.int32,(1,128),1)
    return [((lane//width)==h) for h in range(128//width)]

def run_beside(plan,depth):
    begin,ticks,finish=plan
    step=pl.program_id(0); steps=pl.num_programs(0)
    @pl.when(step==0)
    def _():
        greet(depth)
        begin()
    for n in range(7):
        @pl.when(step==n+1)
        def _():
            if n<len(ticks): ticks[n]()
    def after():
        @pl.when(step==steps-1)
        def _():
            for tick in ticks[7:]: tick()
            finish()
    return after

def fwd_kernel(causal, block, width, moved, depth, lim_ref, q_ref, k_ref, v_ref, *refs):
    ctx_ref,lse_ref=refs[moved:moved+2]
    if moved:
        after=run_beside(gather_plan(refs[:moved],refs[moved+2:2*moved+2],refs[2*moved+2:],depth),depth)
    rows=q_ref.shape[0]; keys=k_ref.shape[0]
    masks=head_masks(width)
    k=k_ref[...]
    v=v_ref[...]
    vm=[jnp.where(m,v,jnp.zeros_like(v)) for m in masks]
    for i in range(rows//block):
        kend=(i+1)*block if causal else keys
        q=q_ref[pl.ds(i*block,block),:]*jnp.bfloat16(width**-0.5)
        ctx=None
        for h,m in enumerate(masks):
            s=dot(jnp.where(m,q,jnp.zeros_like(q)),k[:kend],NT)
            if causal:
                tail=s[:,kend-block:]
                r=lax.broadcasted_iota(jnp.int32,tail.shape,0)
                c=lax.broadcasted_iota(jnp.int32,tail.shape,1)
                tail=jnp.where(c<=r,tail,NEGATIVE)
                s=tail if kend==block else jnp.concatenate([s[:,:kend-block],tail],1)
            else:
                c=lax.broadcasted_iota(jnp.int32,s.shape,1)
                s=jnp.where(c<lim_ref[0],s,NEGATIVE)
            top=jnp.max(s,axis=1,keepdims=True)
            p=jnp.exp(s-top)
            total=jnp.sum(p,axis=1,keepdims=True)
            part=dot(p.astype(jnp.bfloat16),vm[h][:kend])*(1.0/total)
            ctx=part if ctx is None else ctx+part
            lse=jnp.broadcast_to(top+jnp.log(total),(block,128))
            lse_ref[0,pl.ds(h,1),pl.ds(i*block,block)]=jnp.transpose(lse)[:1]
        ctx_ref[pl.ds(i*block,block),:]=ctx.astype(jnp.bfloat16)
    if moved: after()

def flash_fwd(q,k,v,limit,causal,block=256,width=64,moves=(),depth=0,collective_id=None):
    rows,d=q.shape; keys=k.shape[0]
    pairs=d//128
    per=128//width
    count=len(moves)
    any_=pl.BlockSpec(memory_space=pl.ANY)
    spec=lambda n: pl.BlockSpec((n,128),lambda i,lim:(0,i))
    outs=pl.pallas_call(
        functools.partial(fwd_kernel,causal,block,width,count,depth),
        grid_spec=pltpu.PrefetchScalarGridSpec(
            num_scalar_prefetch=1, grid=(pairs,),
            in_specs=[spec(rows),spec(keys),spec(keys)]+[any_]*count,
            out_specs=[spec(rows),pl.BlockSpec((1,per,rows),lambda i,lim:(i,0,0))]+[any_]*count,
            scratch_shapes=gather_sems(count,depth) if count else []),
        out_shape=[jax.ShapeDtypeStruct((rows,d),jnp.bfloat16),jax.ShapeDtypeStruct((pairs,per,rows),jnp.float32)]+gather_shapes(moves,depth),
        compiler_params=pltpu.CompilerParams(vmem_limit_bytes=48*MIB,collective_id=collective_id,has_side_effects=count>0),
        cost_estimate=pl.CostEstimate(flops=4*rows*keys*d//(2 if causal else 1),bytes_accessed=4*rows*d*2,transcendentals=rows*keys*16//(2 if causal else 1)),
        name="attend_causal" if causal else "attend_text",
    )(limit,q,k,v,*moves)
    return outs[0],outs[1],gather_result(outs[2:],moves)

def back_of_pair(causal, block, width, lim_ref, q_ref, k_ref, v_ref, g_ref, ctx_ref, lse_ref, dq_ref, dk_acc, dv_acc):
    rows=q_ref.shape[0]; keys=k_ref.shape[0]
    masks=head_masks(width)
    scale=jnp.bfloat16(width**-0.5)
    k=k_ref[...]; v=v_ref[...]
    km=[jnp.where(m,k*scale,jnp.zeros_like(k)) for m in masks]
    dk_acc[...]=jnp.zeros_like(dk_acc); dv_acc[...]=jnp.zeros_like(dv_acc)
    for i in range(rows//block):
        kend=(i+1)*block if causal else keys
        sl=pl.ds(i*block,block)
        q=q_ref[sl,:]*scale
        g=g_ref[sl,:]
        prod=g.astype(jnp.float32)*ctx_ref[sl,:].astype(jnp.float32)
        dq=None
        for h,m in enumerate(masks):
            qm=jnp.where(m,q,jnp.zeros_like(q))
            gm=jnp.where(m,g,jnp.zeros_like(g))
            delta=jnp.sum(jnp.where(m,prod,0.0),axis=1,keepdims=True)
            delta=jnp.transpose(jnp.broadcast_to(delta,(block,128)))[:1]
            lse=lse_ref[0,pl.ds(h,1),sl]
            s=dot(k[:kend],qm,NT)
            if causal:
                tail=s[kend-block:]
                r=lax.broadcasted_iota(jnp.int32,tail.shape,0)
                c=lax.broadcasted_iota(jnp.int32,tail.shape,1)
                tail=jnp.where(r<=c,tail,NEGATIVE)
                s=tail if kend==block else jnp.concatenate([s[:kend-block],tail],0)
            else:
                r=lax.broadcasted_iota(jnp.int32,s.shape,0)
                s=jnp.where(r<lim_ref[0],s,NEGATIVE)
            p=jnp.exp(s-lse)
            dp=dot(v[:kend],gm,NT)
            ds=(p*(dp-delta)).astype(jnp.bfloat16)
            dk_acc[:kend,:]+=dot(ds,qm)
            dv_acc[:kend,:]+=dot(p.astype(jnp.bfloat16),gm)
            part=dot(ds,km[h][:kend],TN)
            dq=part if dq is None else dq+part
        dq_ref[sl,:]=dq.astype(jnp.bfloat16)

def bwd_kernel(causal, block, width, lim_ref, *refs):
    dq_ref,dk_ref,dv_ref,dk_acc,dv_acc=refs[6:]
    back_of_pair(causal,block,width,lim_ref,*refs[:6],dq_ref,dk_acc,dv_acc)
    dk_ref[...]=dk_acc[...].astype(jnp.bfloat16)
    dv_ref[...]=dv_acc[...].astype(jnp.bfloat16)

def flash_bwd(q,k,v,g,ctx,lse,limit,causal,block=256,width=64):
    rows,d=q.shape; keys=k.shape[0]
    pairs=d//128; per=128//width
    spec=lambda n: pl.BlockSpec((n,128),lambda i,lim:(0,i))
    return pl.pallas_call(
        functools.partial(bwd_kernel,causal,block,width),
        grid_spec=pltpu.PrefetchScalarGridSpec(
            num_scalar_prefetch=1,grid=(pairs,),
            in_specs=[spec(rows),spec(keys),spec(keys),spec(rows),spec(rows),pl.BlockSpec((1,per,rows),lambda i,lim:(i,0,0))],
            out_specs=[spec(rows),spec(keys),spec(keys)],
            scratch_shapes=[pltpu.VMEM((keys,128),jnp.float32)]*2),
        out_shape=[jax.ShapeDtypeStruct((n,d),jnp.bfloat16) for n in (rows,keys,keys)],
        compiler_params=pltpu.CompilerParams(vmem_limit_bytes=60*MIB),
        name="attend_causal_back" if causal else "attend_text_back",
    )(limit,q,k,v,g,ctx,lse)

def sub_layer_kernel(causal, block, width, pairs, depth, lim_ref, flag_ref, *refs):
    pair_refs=refs[:6]; refs=refs[6:]
    normed_ref,source_ref,whole_ref,out_ref,gain_ref=refs[:5]; refs=refs[5:]
    late_count=5 if causal else 6
    late_in=refs[:late_count]; refs=refs[late_count:]
    if causal: grad_out,sums_ref=refs[:2]; refs=refs[2:]
    else: grad_out,low_out,ctx_out,dec_ref,enc_ref,sums_ref=refs[:6]; refs=refs[6:]
    results=refs[:4]; refs=refs[4:]
    late=refs[:late_count]; late_sem=refs[late_count]; refs=refs[late_count+1:]
    normed_t,source_t,whole_t,dq_all,dk_all,dv_all,dk_acc,dv_acc=refs[:8]; refs=refs[8:]
    low_all,ctx_all=(None,None) if causal else refs[:2]
    streams=refs if causal else refs[2:]
    half=len(streams)//2
    step=pl.program_id(0)
    rows=pair_refs[0].shape[0]
    def keep_pair(first):
        def store(i,total):
            for n in range(2):
                results[first+n][:,pl.ds(pl.multiple_of(i*128,128),128)]=total[:,n*128:(n+1)*128]
        return store
    tick1,rest1=stream_plan(pairs,lambda i: 0,keep_pair(0),streams[:half],depth)
    tick2,rest2=stream_plan(pairs,lambda i: 1,keep_pair(2),streams[half:],depth)
    def late_copy(n): return pltpu.make_async_copy(late_in[n],late[n],late_sem.at[n])
    @pl.when(step==0)
    def _():
        greet(depth)
        for n in range(late_count): late_copy(n).start()
        normed_t[...]=jnp.transpose(normed_ref[...])
        whole_t[...]=jnp.transpose(whole_ref[...])
        if not causal: source_t[...]=jnp.transpose(source_ref[...])
    tick1(step); tick2(step)
    here=pl.ds(pl.multiple_of(step*128,128),128)
    back_of_pair(causal,block,width,lim_ref,*pair_refs,dq_all.at[:,here],dk_acc,dv_acc)
    dq=dq_all[:,here]; dk=dk_acc[...].astype(jnp.bfloat16); dv=dv_acc[...].astype(jnp.bfloat16); do=out_ref[...]
    dk_all[:,here]=dk; dv_all[:,here]=dv
    source=normed_t[...] if causal else source_t[...]
    write_made(streams[0],step,0,dot(normed_t[...],dq).astype(jnp.bfloat16))
    write_made(streams[0],step,128,dot(source,dk).astype(jnp.bfloat16))
    write_made(streams[half],step,0,dot(source,dv).astype(jnp.bfloat16))
    write_made(streams[half],step,128,dot(whole_t[...],do).astype(jnp.bfloat16))
    for n,value in enumerate((dq,dv,do)):
        sums_ref[n:n+1,here]=jnp.sum(value.astype(jnp.float32),axis=0,keepdims=True)
    @pl.when(step==pairs-1)
    def _():
        for n in range(late_count): late_copy(n).wait()
        gain=gain_ref[0:1,:]
        sums_ref[3:8,:]=jnp.zeros((5,sums_ref.shape[1]),jnp.float32)
        strip=256
        for r in range(rows//strip):
            rest1[r](); rest2[r]()
            sl=pl.ds(r*strip,strip)
            if causal:
                wq,wk,wv,residual,total=late
                grad=dot(dq_all[sl,:],wq[...],NT)+dot(dk_all[sl,:],wk[...],NT)+dot(dv_all[sl,:],wv[...],NT)
            else:
                wq,wk,wv,wo,residual,total=late
                grad=dot(dq_all[sl,:],wq[...],NT)
            hat,inverse=normal(residual[sl,:].astype(jnp.float32))
            sums_ref[3:4,:]+=jnp.sum(grad*hat,axis=0,keepdims=True)
            sums_ref[4:5,:]+=jnp.sum(grad,axis=0,keepdims=True)
            whole=total[sl,:]+pull_norm(hat,inverse,gain,grad)
            total[sl,:]=whole
            if not causal:
                low_all[sl,:]=whole.astype(jnp.bfloat16)
                ctx_all[sl,:]=dot(low_all[sl,:],wo[...],NT).astype(jnp.bfloat16)
        copies=[pltpu.make_async_copy(late[-1],grad_out,late_sem.at[0])]
        if not causal:
            copies+=[pltpu.make_async_copy(low_all,low_out,late_sem.at[1]),pltpu.make_async_copy(ctx_all,ctx_out,late_sem.at[2])]
        for copy in copies: copy.start()
        for n in range(rows//strip,len(rest1)): rest1[n](); rest2[n]()
        if not causal:
            memory_grad=dot(dk_all[...],late[1][...],NT)+dot(dv_all[...],late[2][...],NT)
            flag=jnp.where(flag_ref[0]==1,1.0,0.0)
            dec_ref[...]=memory_grad*flag
            enc_ref[...]=memory_grad*(1.0-flag)
        for copy in copies: copy.wait()

def sub_layer_back(q,k,v,g,ctx,lse,limit,flag,causal,normed,source,out_grad,gain,late,depth,collective_id,block=256,width=64):
    rows,d=q.shape; keys=k.shape[0]
    pairs=d//128; per=128//width
    each=d//(8*depth)
    bf=jnp.bfloat16; f32=jnp.float32
    spec=lambda n: pl.BlockSpec((n,128),lambda i,a,b:(0,i))
    once=lambda shape: pl.BlockSpec(shape,lambda i,a,b:(0,0),pipeline_mode=pl.Buffered(1))
    keep=lambda shape: pl.BlockSpec(shape,lambda i,a,b:(0,0))
    any_=pl.BlockSpec(memory_space=pl.ANY)
    shape=lambda n,t: jax.ShapeDtypeStruct((n,d),t)
    in_specs=[spec(rows),spec(keys),spec(keys),spec(rows),spec(rows),pl.BlockSpec((1,per,rows),lambda i,a,b:(i,0,0))]
    in_specs+=[once((rows,d)),once(source.shape),once((rows,d)),spec(rows),once(gain.shape)]+[any_]*len(late)
    out_specs=[any_]; out_shape=[shape(rows,f32)]
    scratch=[pltpu.VMEM(a.shape,a.dtype) for a in late]+[DMA((len(late),))]
    scratch+=[pltpu.VMEM((d,rows),bf),pltpu.VMEM((8,128) if causal else (d,keys),bf),pltpu.VMEM((d,rows),bf)]
    scratch+=[pltpu.VMEM((n,d),bf) for n in (rows,keys,keys)]+[pltpu.VMEM((keys,128),f32)]*2
    if not causal:
        out_specs+=[any_,any_,keep((keys,d)),keep((keys,d))]
        out_shape+=[shape(rows,bf),shape(rows,bf),shape(keys,f32),shape(keys,f32)]
        scratch+=[pltpu.VMEM((rows,d),bf)]*2
    out_specs+=[keep((8,d))]+[keep((each,d))]*4
    out_shape+=[shape(8,f32)]+[shape(each,f32)]*4
    scratch+=stream_scratch(each,256,depth)*2
    return pl.pallas_call(
        functools.partial(sub_layer_kernel,causal,block,width,pairs,depth),
        grid_spec=pltpu.PrefetchScalarGridSpec(num_scalar_prefetch=2,grid=(pairs,),in_specs=in_specs,out_specs=out_specs,scratch_shapes=scratch),
        out_shape=out_shape,
        compiler_params=pltpu.CompilerParams(vmem_limit_bytes=62*MIB,collective_id=collective_id,has_side_effects=True),
        cost_estimate=pl.CostEstimate(flops=20*rows*keys*d,bytes_accessed=20*rows*d*2,transcendentals=rows*keys*16),
        name="self_back" if causal else "cross_back",
    )(limit,flag,q,k,v,g,ctx,lse,normed,source,ctx,out_grad,gain,*late)

MESH=pl.DeviceIdType.MESH
DMA=pltpu.SemaphoreType.DMA

def place():
    dp=lax.axis_index("dp"); fs=lax.axis_index("fsdp")
    return dp,fs,fs//2,fs%2

def turned(index,bit):
    return index+bit-2*bit*((index//bit)%2)

def greet(depth):
    dp,fs,z,c=place()
    partners=[(dp,lax.rem(z+k,depth)*2+c) for k in range(1,depth)]+[(turned(dp,1),fs),(turned(dp,2),fs),(dp,z*2+1-c)]
    barrier=pltpu.get_barrier_semaphore()
    for device in partners:
        pl.semaphore_signal(barrier,inc=1,device_id=device,device_id_type=MESH)
    pl.semaphore_wait(barrier,len(partners))

def gather_sems(count,depth):
    return [DMA((count,)),DMA((count,depth-1)),DMA((count,depth-1)),DMA((count,3)),DMA((count,3)),DMA((count,4)),DMA((count,4))]

def gather_plan(ins,outs,sems,depth):
    count=len(ins)
    local,z_send,z_recv,a_send,a_recv,c_send,c_recv=sems
    dp,fs,z,c=place()
    def line(w,k):
        return pltpu.make_async_remote_copy(ins[w],outs[w].at[dp,z,c],z_send.at[w,k-1],z_recv.at[w,k-1],(dp,lax.rem(z+k,depth)*2+c),MESH)
    def across(w,n,src_dp,bit):
        ref=outs[w].at[src_dp,:,c]
        return pltpu.make_async_remote_copy(ref,ref,a_send.at[w,n],a_recv.at[w,n],(turned(dp,bit),fs),MESH)
    def core(w,n,src_dp):
        ref=outs[w].at[src_dp,:,c]
        return pltpu.make_async_remote_copy(ref,ref,c_send.at[w,n],c_recv.at[w,n],(dp,z*2+1-c),MESH)
    def own(w):
        return pltpu.make_async_copy(ins[w],outs[w].at[dp,z,c],local.at[w])
    def bits(w):
        return 1+w%2,2-w%2
    def step0(w):
        f,g=bits(w)
        own(w).wait()
        for k in range(1,depth): line(w,k).wait_recv()
        across(w,0,dp,f).start()
        across(w,1,dp,g).start()
        core(w,0,dp).start()
    def step1(w):
        f,g=bits(w)
        across(w,0,dp,f).wait_recv()
        across(w,2,turned(dp,f),g).start()
        core(w,1,turned(dp,f)).start()
    def step2(w):
        f,g=bits(w)
        across(w,1,dp,g).wait_recv()
        core(w,2,turned(dp,g)).start()
    def step3(w):
        f,g=bits(w)
        across(w,2,turned(dp,f),g).wait_recv()
        core(w,3,turned(turned(dp,f),g)).start()
    def begin():
        for w in range(count):
            own(w).start()
            for k in range(1,depth): line(w,k).start()
    def tick(t):
        for n,step in enumerate((step0,step1,step2,step3)):
            if 0<=t-n<count: step(t-n)
    def finish():
        for w in range(count):
            f,g=bits(w)
            for k in range(1,depth): line(w,k).wait_send()
            across(w,0,dp,f).wait_send(); across(w,1,dp,g).wait_send(); across(w,2,dp,g).wait_send()
            for n in range(4): core(w,n,dp).wait()
    return begin,[functools.partial(tick,t) for t in range(count+3)],finish

def reduce_scratch(kinds,depth):
    count=len(kinds)
    vmem=lambda *lead: [pltpu.VMEM(lead+(r,n),d) for r,n,d in kinds]
    return (vmem(2,2,depth)+vmem(2,2,depth)+vmem(2,depth)+vmem(depth)+vmem(depth-1)
      +[DMA((count,)),DMA((count,)),DMA((count,)),DMA((count,2)),DMA((count,2)),DMA((count,depth-1)),DMA((count,depth-1))])

def reduce_plan(ins,outs,scratch,depth):
    count=len(ins)
    held,r0,r1,r2,r3=(scratch[n*count:(n+1)*count] for n in range(5))
    local,c_send,c_recv,a_send,a_recv,z_send,z_recv=scratch[5*count:]
    dp,fs,z,c=place()
    hi,lo=dp//2,dp%2
    def own(w):
        return pltpu.make_async_copy(ins[w].at[:,:,:,c],held[w],local.at[w])
    def core(w):
        return pltpu.make_async_remote_copy(ins[w].at[:,:,:,1-c],r0[w],c_send.at[w],c_recv.at[w],(dp,z*2+1-c),MESH)
    def first(w):
        if w%2: return pltpu.make_async_remote_copy(held[w].at[1-hi],r1[w],a_send.at[w,0],a_recv.at[w,0],(turned(dp,2),fs),MESH)
        return pltpu.make_async_remote_copy(held[w].at[:,1-lo],r1[w],a_send.at[w,0],a_recv.at[w,0],(turned(dp,1),fs),MESH)
    def second(w):
        if w%2: return pltpu.make_async_remote_copy(held[w].at[hi,1-lo],r2[w],a_send.at[w,1],a_recv.at[w,1],(turned(dp,1),fs),MESH)
        return pltpu.make_async_remote_copy(held[w].at[1-hi,lo],r2[w],a_send.at[w,1],a_recv.at[w,1],(turned(dp,2),fs),MESH)
    def line(w,k):
        return pltpu.make_async_remote_copy(held[w].at[hi,lo,lax.rem(z+k,depth)],r3[w].at[k-1],z_send.at[w,k-1],z_recv.at[w,k-1],(dp,lax.rem(z+k,depth)*2+c),MESH)
    def step0(w):
        own(w).wait(); core(w).wait_recv()
        def add(n,_):
            i,k=n//depth,n%depth
            held[w][i//2,i%2,k]=held[w][i//2,i%2,k]+r0[w][i//2,i%2,k]
            return 0
        lax.fori_loop(0,4*depth,add,0)
        first(w).start()
    def step1(w):
        first(w).wait_recv()
        def add(n,_):
            i,k=n//depth,n%depth
            if w%2: held[w][hi,i,k]=held[w][hi,i,k]+r1[w][i,k]
            else: held[w][i,lo,k]=held[w][i,lo,k]+r1[w][i,k]
            return 0
        lax.fori_loop(0,2*depth,add,0)
        second(w).start()
    def step2(w):
        second(w).wait_recv()
        def add(k,_):
            held[w][hi,lo,k]=held[w][hi,lo,k]+r2[w][k]
            return 0
        lax.fori_loop(0,depth,add,0)
        for k in range(1,depth): line(w,k).start()
    def step3(w):
        total=held[w][hi,lo,z].astype(jnp.float32)
        for k in range(1,depth):
            line(w,k).wait_recv()
            total=total+r3[w][k-1].astype(jnp.float32)
        outs[w][...]=total
    def begin():
        for w in range(count):
            core(w).start(); own(w).start()
    def tick(t):
        for n,step in enumerate((step0,step1,step2,step3)):
            if 0<=t-n<count: step(t-n)
    def finish():
        for w in range(count):
            core(w).wait_send(); first(w).wait_send(); second(w).wait_send()
            for k in range(1,depth): line(w,k).wait_send()
    return begin,[functools.partial(tick,t) for t in range(count+3)],finish

def gather_shapes(shards,depth):
    return [jax.ShapeDtypeStruct((4,depth,2)+s.shape,s.dtype) for s in shards]

def gather_result(outs,shards):
    return [o.reshape((-1,)+s.shape[1:]) for o,s in zip(outs,shards)]

def reduce_parts(partials,depth):
    return [p.reshape((2,2,depth,2,p.shape[0]//(8*depth),p.shape[1])) for p in partials]

def first_kernel(count,lines,depth,*refs):
    ins,vectors,wide=refs[:count],refs[count:count+lines],refs[count+lines]
    refs=refs[count+lines+1:]
    outs,table,long=refs[:count],refs[count],refs[count+1]
    packed,every=refs[count+2:count+4]
    each=vectors[0].shape[1]
    greet(depth)
    packed[...]=jnp.zeros_like(packed)
    for n in range(lines): packed[n:n+1,:each]=vectors[n][...].astype(jnp.float32)
    packed[lines:lines+1,:]=wide[...].astype(jnp.float32)
    begin,ticks,finish=gather_plan([packed]+list(ins),[every]+list(outs),refs[count+4:],depth)
    begin()
    for tick in ticks: tick()
    finish()
    lane=lax.broadcasted_iota(jnp.int32,(16,128),1)
    group=128//each
    def device(n): return every[n//(2*depth),(n//2)%depth,n%2]
    for m in range(8*depth//group):
        tile=device(m*group)
        for r in range(1,group):
            tile=jnp.where(lane>=r*each,pltpu.roll(device(m*group+r),r*each,1),tile)
        table[:,m*128:(m+1)*128]=tile
    for n in range(8*depth):
        long[:,n*128:(n+1)*128]=device(n)[lines:lines+1]

def gather_first(shards,vectors,wide,depth,collective_id):
    count=len(shards); lines=len(vectors)
    any_=pl.BlockSpec(memory_space=pl.ANY); vm=pl.BlockSpec(memory_space=pltpu.VMEM)
    total=vectors[0].shape[0]*8*depth
    outs=pl.pallas_call(
        functools.partial(first_kernel,count,lines,depth),
        in_specs=[any_]*count+[vm]*(lines+1),
        out_specs=[any_]*count+[vm]*2,
        out_shape=gather_shapes(shards,depth)+[jax.ShapeDtypeStruct((16,total),jnp.float32),jax.ShapeDtypeStruct((1,128*8*depth),jnp.float32)],
        scratch_shapes=[pltpu.VMEM((16,128),jnp.float32),pltpu.VMEM((4,depth,2,16,128),jnp.float32)]+gather_sems(count+1,depth),
        compiler_params=pltpu.CompilerParams(collective_id=collective_id,has_side_effects=True),
        name="gather_first",
    )(*shards,*[v[None] for v in vectors],wide[None])
    return gather_result(outs[:count],shards)+list(outs[count:])

def last_kernel(count,depth,*refs):
    ins,outs,scratch=refs[:count],refs[count:2*count],refs[2*count:]
    greet(depth)
    begin,ticks,finish=reduce_plan(ins,outs,scratch,depth)
    begin()
    for tick in ticks: tick()
    finish()

def reduce_rows(partials,depth,collective_id):
    count=len(partials)
    parts=reduce_parts(partials,depth)
    kinds=[p.shape[4:]+(p.dtype,) for p in parts]
    return pl.pallas_call(
        functools.partial(last_kernel,count,depth),
        in_specs=[pl.BlockSpec(memory_space=pl.ANY)]*count,
        out_specs=[pl.BlockSpec(memory_space=pltpu.VMEM)]*count,
        out_shape=[jax.ShapeDtypeStruct(k[:2],jnp.float32) for k in kinds],
        scratch_shapes=reduce_scratch(kinds,depth),
        compiler_params=pltpu.CompilerParams(collective_id=collective_id,has_side_effects=True,vmem_limit_bytes=60*MIB),
        name="reduce_rows",
    )(*parts)

SLOTS=4

def stream_scratch(rows,cols,depth):
    vmem=lambda *lead: pltpu.VMEM(lead+(rows,cols),jnp.bfloat16)
    return [vmem(2,2,2,depth,2),vmem(SLOTS,2,2,depth),vmem(SLOTS,2,2,depth),vmem(SLOTS,2,depth),vmem(SLOTS,depth),vmem(SLOTS,depth-1),
      DMA((SLOTS,)),DMA((SLOTS,)),DMA((SLOTS,2)),DMA((SLOTS,2)),DMA((SLOTS,depth-1)),DMA((SLOTS,depth-1))]

def stream_plan(count,parity,store,scratch,depth):
    made,r0,held,r1,r2,r3,c_send,c_recv,a_send,a_recv,z_send,z_recv=scratch
    dp,fs,z,c=place()
    hi,lo=dp//2,dp%2
    def slot(i): return lax.rem(i,SLOTS)
    def core(i):
        s=slot(i)
        return pltpu.make_async_remote_copy(made.at[lax.rem(i,2),:,:,:,1-c],r0.at[s],c_send.at[s],c_recv.at[s],(dp,z*2+1-c),MESH)
    def first(i,odd):
        s=slot(i)
        src=held.at[s,1-hi] if odd else held.at[s,:,1-lo]
        return pltpu.make_async_remote_copy(src,r1.at[s],a_send.at[s,0],a_recv.at[s,0],(turned(dp,2 if odd else 1),fs),MESH)
    def second(i,odd):
        s=slot(i)
        src=held.at[s,hi,1-lo] if odd else held.at[s,1-hi,lo]
        return pltpu.make_async_remote_copy(src,r2.at[s],a_send.at[s,1],a_recv.at[s,1],(turned(dp,1 if odd else 2),fs),MESH)
    def line(i,k):
        s=slot(i)
        return pltpu.make_async_remote_copy(held.at[s,hi,lo,lax.rem(z+k,depth)],r3.at[s,k-1],z_send.at[s,k-1],z_recv.at[s,k-1],(dp,lax.rem(z+k,depth)*2+c),MESH)
    def by_parity(i,run):
        p=parity(i)
        if isinstance(p,int): run(p)
        else:
            for odd in (0,1):
                @pl.when(p==odd)
                def _(): run(odd)
    def step0(i):
        s=slot(i); m=lax.rem(i,2)
        core(i).wait()
        def add(n,_):
            a,k=n//depth,n%depth
            held[s,a//2,a%2,k]=made[m,a//2,a%2,k,c]+r0[s,a//2,a%2,k]
            return 0
        lax.fori_loop(0,4*depth,add,0)
        by_parity(i,lambda odd: first(i,odd).start())
    def step1(i):
        s=slot(i)
        first(i,0).wait_recv()
        def run(odd):
            def add(n,_):
                a,k=n//depth,n%depth
                if odd: held[s,hi,a,k]=held[s,hi,a,k]+r1[s,a,k]
                else: held[s,a,lo,k]=held[s,a,lo,k]+r1[s,a,k]
                return 0
            lax.fori_loop(0,2*depth,add,0)
            second(i,odd).start()
        by_parity(i,run)
    def step2(i):
        s=slot(i)
        second(i,0).wait_recv()
        def add(k,_):
            held[s,hi,lo,k]=held[s,hi,lo,k]+r2[s,k]
            return 0
        lax.fori_loop(0,depth,add,0)
        for k in range(1,depth): line(i,k).start()
    def step3(i):
        s=slot(i)
        total=held[s,hi,lo,z].astype(jnp.float32)
        for k in range(1,depth):
            line(i,k).wait_recv()
            total=total+r3[s,k-1].astype(jnp.float32)
        store(i,total)
        first(i,0).wait_send(); second(i,0).wait_send()
        for k in range(1,depth): line(i,k).wait_send()
    stages=((5,step3),(4,step2),(3,step1),(2,step0),(1,lambda i: core(i).start()))
    def tick(j):
        for lag,step in stages:
            if isinstance(j,int):
                if 0<=j-lag<count: step(jnp.int32(j-lag))
            else:
                @pl.when(j>=lag)
                def _(): step(j-lag)
    return tick,[functools.partial(tick,count+n) for n in range(5)]

def write_made(made,i,col,value):
    shape=made.shape[1:6]+value.shape[1:]
    made[lax.rem(i,2),:,:,:,:,:,col:col+value.shape[1]]=value.reshape(shape)

EPSILON=1e-05
def normal(tensor):
    centre=tensor-jnp.mean(tensor,axis=-1,keepdims=True)
    spread=jnp.mean(centre*centre,axis=-1,keepdims=True)
    inverse=lax.rsqrt(spread+EPSILON)
    return centre*inverse,inverse

def pull_norm(hat,inverse,gain,grad):
    scaled=grad*gain
    return inverse*(scaled-jnp.mean(scaled,axis=-1,keepdims=True)-hat*jnp.mean(scaled*hat,axis=-1,keepdims=True))

def ffn_kernel(strip, steps, depth, length_ref, after_ref, cot_ref, w1_ref, w2_ref, b1_ref, vec_ref, wo_ref,
               mixed_ref, grad_ref, low_ref, ctx_ref, dw1_ref, dw2_ref, db1_ref, dvec_ref, n3, n3t, gf, branch, gn, wo, sem, *refs):
    j=pl.program_id(0)
    rows,d=after_ref.shape
    gain,shift,b2=vec_ref[0:1,:],vec_ref[1:2,:],vec_ref[2:3,:]
    def live(r):
        return (r*strip+lax.broadcasted_iota(jnp.int32,(strip,1),0)<length_ref[0]).astype(jnp.float32)
    if depth:
        half=len(refs)//2
        wide=w1_ref.shape[1]
        def store1(i,total): dw1_ref[:,pl.ds(pl.multiple_of(i*wide,128),wide)]=total
        def store2(i,total): dw2_ref[i]=total
        tick1,rest1=stream_plan(steps,lambda i: 0,store1,refs[:half],depth)
        tick2,rest2=stream_plan(steps,lambda i: 1,store2,refs[half:],depth)
    @pl.when(j==0)
    def _():
        if depth: greet(depth)
        pltpu.make_async_copy(wo_ref,wo,sem.at[2]).start()
        def one(r,total):
            sl=pl.ds(r*strip,strip)
            hat,_=normal(after_ref[sl,:])
            n3[sl,:]=(hat*gain+shift).astype(jnp.bfloat16)
            top=(cot_ref[sl,:].astype(jnp.float32)*live(r)).astype(jnp.bfloat16)
            gf[sl,:]=top
            return total+jnp.sum(top.astype(jnp.float32),axis=0,keepdims=True)
        dvec_ref[...]=jnp.zeros_like(dvec_ref)
        dvec_ref[2:3,:]=lax.fori_loop(0,rows//strip,one,jnp.zeros((1,d),jnp.float32))
        n3t[...]=jnp.transpose(n3[...])
        branch[...]=jnp.zeros_like(branch); gn[...]=jnp.zeros_like(gn)
    if depth:
        tick1(j); tick2(j)
    w1=w1_ref[...]; w2=w2_ref[...].reshape(w1.shape[1],d)
    pre=dot(n3[...],w1)+b1_ref[...]
    back=dot(gf[...],w2,NT).astype(jnp.bfloat16).astype(jnp.float32)
    root=0.7978845608028654
    square=pre*pre
    t=jnp.tanh(root*pre*(1.0+0.044715*square))
    half_t=0.5*(1.0+t)
    hidden=(pre*half_t).astype(jnp.bfloat16)
    slope=half_t+0.5*pre*(1.0-t*t)*(root*(1.0+3*0.044715*square))
    g_pre=(back*slope).astype(jnp.bfloat16)
    db1_ref[...]=jnp.sum(g_pre.astype(jnp.float32),axis=0,keepdims=True)
    branch[...]+=dot(hidden,w2)
    dw2=dot(hidden,gf[...],TN).astype(jnp.bfloat16)
    dw1=dot(n3t[...],g_pre).astype(jnp.bfloat16)
    if depth:
        write_made(refs[0],j,0,dw1)
        write_made(refs[half],j,0,dw2)
    else:
        dw1_ref[...]=dw1
        dw2_ref[...]=dw2.reshape(dw2_ref.shape)
    gn[...]+=dot(g_pre,w1,NT)
    @pl.when(j==steps-1)
    def _():
        def one(r):
            sl=pl.ds(r*strip,strip)
            valid=live(r)
            after=after_ref[sl,:]
            n3[sl,:]=((after+(branch[sl,:]+b2))*valid).astype(jnp.bfloat16)
            hat,inverse=normal(after)
            grad=gn[sl,:]
            dvec_ref[0:1,:]+=jnp.sum(grad*hat,axis=0,keepdims=True)
            dvec_ref[1:2,:]+=jnp.sum(grad,axis=0,keepdims=True)
            grad=cot_ref[sl,:].astype(jnp.float32)*valid+pull_norm(hat,inverse,gain,grad)
            gn[sl,:]=grad
            gf[sl,:]=grad.astype(jnp.bfloat16)
            n3t[sl,:]=dot(gf[sl,:],wo[...],NT).astype(jnp.bfloat16)
        late=list(zip(rest1,rest2)) if depth else []
        pltpu.make_async_copy(wo_ref,wo,sem.at[2]).wait()
        for r in range(rows//strip):
            if r%2==0 and r//2<len(late):
                late[r//2][0](); late[r//2][1]()
            one(r)
        copies=[pltpu.make_async_copy(a,b,sem.at[n]) for n,(a,b) in enumerate(((n3,mixed_ref),(gn,grad_ref),(gf,low_ref),(n3t,ctx_ref)))]
        for copy in copies: copy.start()
        for a,b in late[rows//strip//2:]:
            a(); b()
        for copy in copies: copy.wait()

def feed_forward(after,cot,length,w1,w2,b1,vec,wo,block=512,strip=128,depth=0,collective_id=None):
    rows,d=after.shape; ff=w1.shape[1]
    steps=ff//block
    once=lambda shape: pl.BlockSpec(shape,lambda j,n:(0,0),pipeline_mode=pl.Buffered(1))
    keep=lambda shape: pl.BlockSpec(shape,lambda j,n:(0,)*len(shape))
    any_=pl.BlockSpec(memory_space=pl.ANY)
    wide=pl.BlockSpec((d,block),lambda j,n:(0,j)); line=pl.BlockSpec((1,block),lambda j,n:(0,j))
    tall=pl.BlockSpec((w2.shape[0],block//w2.shape[0],d),lambda j,n:(0,j,0))
    bf=jnp.bfloat16; f32=jnp.float32
    scratch=[pltpu.VMEM((rows,d),bf),pltpu.VMEM((d,rows),bf),pltpu.VMEM((rows,d),bf),pltpu.VMEM((rows,d),f32),pltpu.VMEM((rows,d),f32),pltpu.VMEM((d,d),bf),DMA((4,))]
    if depth:
        each=d//(8*depth); part=block//(8*depth)
        grad_specs=[keep((each,ff)),keep((steps,part,d))]
        grad_shapes=[jax.ShapeDtypeStruct((each,ff),f32),jax.ShapeDtypeStruct((steps,part,d),f32)]
        scratch+=stream_scratch(each,block,depth)+stream_scratch(part,d,depth)
    else:
        grad_specs=[wide,tall]
        grad_shapes=[jax.ShapeDtypeStruct(w1.shape,bf),jax.ShapeDtypeStruct(w2.shape,bf)]
    return pl.pallas_call(
        functools.partial(ffn_kernel,strip,steps,depth),
        grid_spec=pltpu.PrefetchScalarGridSpec(
            num_scalar_prefetch=1,grid=(steps,),
            in_specs=[once((rows,d)),once((rows,d)),wide,tall,line,once(vec.shape),any_],
            out_specs=[any_]*4+grad_specs+[line,keep((8,d))],
            scratch_shapes=scratch),
        out_shape=[jax.ShapeDtypeStruct((rows,d),bf),jax.ShapeDtypeStruct((rows,d),f32)]+[jax.ShapeDtypeStruct((rows,d),bf)]*2+grad_shapes+[jax.ShapeDtypeStruct((1,ff),f32),jax.ShapeDtypeStruct((8,d),f32)],
        compiler_params=pltpu.CompilerParams(vmem_limit_bytes=62*MIB,collective_id=collective_id,has_side_effects=depth>0),
        cost_estimate=pl.CostEstimate(flops=12*rows*d*ff,bytes_accessed=4*d*ff*2+rows*d*12,transcendentals=rows*ff),
        name="feed_forward",
    )(length,after,cot,w1,w2,b1,vec,wo)

AXES=("dp","fsdp")

def layer_norm(tensor, gain, shift):
    return normal(tensor)[0]*gain+shift

def layer_norm_back(tensor, gain, grad):
    hat,inverse=normal(tensor)
    return pull_norm(hat,inverse,gain,grad),jnp.sum(grad*hat,axis=0),jnp.sum(grad,axis=0)

def low(tensor):
    return tensor.astype(jnp.bfloat16)

def columns(tensor):
    return jnp.sum(tensor.astype(jnp.float32),axis=0)

def gather_all(shards):
    return [lax.all_gather(s,AXES,axis=0,tiled=True) for s in shards]

def reduce_all(partials):
    return [lax.psum_scatter(p,AXES,scatter_dimension=0,tiled=True).astype(jnp.float32) for p in partials]

def gather_vectors(vectors,wide):
    rows=jnp.stack([jnp.pad(v,(0,128-v.shape[0])) for v in list(vectors)+[wide]])
    rows=jnp.pad(rows,((0,15-len(vectors)),(0,0)))
    whole=lax.all_gather(rows,AXES).astype(jnp.float32)
    return whole[:,:,:vectors[0].shape[0]].transpose(1,0,2).reshape(16,-1),whole[:,len(vectors),:wide.shape[0]].reshape(1,-1)

def pack_grads(vectors,wide,devices):
    each=1024//devices
    flat=jnp.stack(vectors).reshape(len(vectors),devices,each).transpose(1,0,2).reshape(devices,-1)
    flat=jnp.concatenate([flat,wide.reshape(devices,4*each)],1)
    return jnp.pad(flat,((0,0),(0,1024-flat.shape[1]))).reshape(devices*8,128)

def shards(devices, depth, unit_states, dec_states, enc_states, unit_len, text_len, task_flag, cotangent,
    ln1_gain, ln1_shift, self_wq, self_bq, self_wk, self_wv, self_bv, self_wo, self_bo,
    ln2_gain, ln2_shift, cross_wq, cross_bq, cross_wk, cross_wv, cross_bv, cross_wo, cross_bo,
    ln3_gain, ln3_shift, ffn_w1, ffn_b1, ffn_w2, ffn_b2):
    steps=8
    each=1024//devices
    if depth:
        part=4*each//steps
        ffn_w1=ffn_w1.reshape(each,devices,steps,part).transpose(0,2,1,3).reshape(each,4096)
    w1=lax.all_gather(ffn_w1,AXES,axis=0,tiled=True)
    w2=lax.all_gather(ffn_w2,AXES,axis=0,tiled=True)
    small=[ln1_gain,ln1_shift,self_bq,self_bv,self_bo,ln2_gain,ln2_shift,cross_bq,cross_bv,cross_bo,ln3_gain,ln3_shift,ffn_b2]
    late=[self_wo,cross_wq,cross_wk,cross_wv,cross_wo]
    if depth:
        wq,wk,wv,vectors,b1=gather_first([self_wq,self_wk,self_wv],small,ffn_b1,depth,1)
    else:
        wq,wk,wv,*late=gather_all([self_wq,self_wk,self_wv]+late)
        vectors,b1=gather_vectors(small,ffn_b1)
    g1,s1,bq,bv,bo,g2,s2,cbq,cbv,cbo,g3,s3,b2=[vectors[i] for i in range(13)]
    units=unit_states[0].astype(jnp.float32)
    memory=jnp.where(task_flag[0]==1,dec_states[0],enc_states[0])
    n1=low(layer_norm(units,g1,s1))
    q=low(dot(n1,wq)+bq); k=low(dot(n1,wk)); v=low(dot(n1,wv)+bv)
    if depth: ctx,lse,late=flash_fwd(q,k,v,text_len,True,moves=late,depth=depth,collective_id=2)
    else: ctx,lse,_=flash_fwd(q,k,v,text_len,True)
    wo,cwq,cwk,cwv,cwo=late
    after_self=units+(dot(ctx,wo)+bo)
    n2=low(layer_norm(after_self,g2,s2))
    cq=low(dot(n2,cwq)+cbq); ck=low(dot(memory,cwk)); cv=low(dot(memory,cwv)+cbv)
    cctx,clse,_=flash_fwd(cq,ck,cv,text_len,False)
    after_cross=after_self+(dot(cctx,cwo)+cbo)
    last=jnp.concatenate([vectors[10:13],jnp.zeros((5,1024),jnp.float32)])
    if depth:
        b1=b1.reshape(devices,steps,part).transpose(1,0,2).reshape(1,4096)
        mixed,g_cross,gc,g_cctx,dw1,dw2,db1,dvec=feed_forward(after_cross,cotangent[0],unit_len,w1,w2.reshape(devices,4*each,1024),b1,last,cwo,depth=depth,collective_id=3)
        dw1=dw1.reshape(each,steps,devices,part).transpose(0,2,1,3).reshape(each,4096)
        dw2=dw2.reshape(4*each,1024)
        db1=db1.reshape(steps,devices,part).transpose(1,0,2)
    else:
        mixed,g_cross,gc,g_cctx,dw1,dw2,db1,dvec=feed_forward(after_cross,cotangent[0],unit_len,w1,w2[None],b1,last,cwo)
        dw1,dw2=reduce_all([dw1,dw2[0]])
    gain1,gain2=vectors[0:1],vectors[5:6]
    if depth:
        g_self,gs,g_ctx,g_dec,g_enc,csums,dcwq,dcwk,dcwv,dcwo=sub_layer_back(
            cq,ck,cv,g_cctx,cctx,clse,text_len,task_flag,False,n2,memory,gc,gain2,[cwq,cwk,cwv,wo,after_self,g_cross],depth,4)
        g_units,sums,dwq,dwk,dwv,dwo=sub_layer_back(
            q,k,v,g_ctx,ctx,lse,text_len,task_flag,True,n1,memory,gs,gain1,[wq,wk,wv,unit_states[0],g_self],depth,5)
        small_grads=[sums[3],sums[4],sums[0],sums[1],sums[2],csums[3],csums[4],csums[0],csums[1],csums[2],dvec[0],dvec[1],dvec[2]]
    else:
        gcq,gck,gcv=flash_bwd(cq,ck,cv,g_cctx,cctx,clse,text_len,False)
        dcwq,dcwk,dcwv,dcwo=reduce_all([low(dot(n2,gcq,TN)),low(dot(memory,gck,TN)),low(dot(memory,gcv,TN)),low(dot(cctx,gc,TN))])
        g_memory=dot(gck,cwk,NT)+dot(gcv,cwv,NT)
        pulled,dg2,ds2=layer_norm_back(after_self,g2,dot(gcq,cwq,NT))
        g_self=g_cross+pulled
        gs=low(g_self)
        gq,gk,gv=flash_bwd(q,k,v,low(dot(gs,wo,NT)),ctx,lse,text_len,True)
        dwq,dwk,dwv,dwo=reduce_all([low(dot(n1,gq,TN)),low(dot(n1,gk,TN)),low(dot(n1,gv,TN)),low(dot(ctx,gs,TN))])
        pulled,dg1,ds1=layer_norm_back(units,g1,dot(gq,wq,NT)+dot(gk,wk,NT)+dot(gv,wv,NT))
        g_units=g_self+pulled
        is_dec=(task_flag[0]==1).astype(jnp.float32)
        g_dec,g_enc=g_memory*is_dec,g_memory*(1.0-is_dec)
        small_grads=[dg1,ds1,columns(gq),columns(gv),columns(gs),dg2,ds2,columns(gcq),columns(gcv),columns(gc),dvec[0],dvec[1],dvec[2]]
    grads=pack_grads(small_grads,db1,devices)
    grads,=reduce_rows([grads],depth,6) if depth else reduce_all([grads])
    grads=grads.reshape(1024)
    ng=[grads[i*each:(i+1)*each] for i in range(13)]
    db1=grads[13*each:17*each]
    return (mixed[None],g_units[None],g_dec[None],g_enc[None],
        ng[0],ng[1],dwq,ng[2],dwk,dwv,ng[3],dwo,ng[4],ng[5],ng[6],dcwq,ng[7],dcwk,dcwv,ng[8],dcwo,ng[9],ng[10],ng[11],dw1,db1,dw2,ng[12])

def solution(mesh):
    devices=mesh.shape["dp"]*mesh.shape["fsdp"]
    depth=mesh.shape["fsdp"]//2 if mesh.shape["dp"]==4 and (1024//devices)%16==0 else 0
    cube,flat,row=P(AXES,None,None),P(AXES),P(AXES,None)
    return jax.shard_map(
        functools.partial(shards,devices,depth),
        mesh=mesh,
        in_specs=(cube,)*3+(flat,)*3+(cube,flat,flat,row,flat,row,row,flat,row,flat,flat,flat,row,flat,row,row,flat,row,flat,flat,flat,row,flat,row,flat),
        out_specs=(cube,)*4+(flat,flat,row,flat,row,row,flat,row,flat,flat,flat,row,flat,row,row,flat,row,flat,flat,flat,row,flat,row,flat),
        check_vma=False,
    )
```

```python
import functools

import jax
import jax.numpy as jnp
from jax import lax
from jax.experimental import pallas as pl
from jax.experimental.pallas import tpu as pltpu
from jax.sharding import PartitionSpec as P

MIB=1<<20

NEGATIVE=-1e30
NN=(((1,),(0,)),((),()))
NT=(((1,),(1,)),((),()))
TN=(((0,),(0,)),((),()))
def dot(a,b,dims=NN):
    return lax.dot_general(a,b,dims,preferred_element_type=jnp.float32)

def head_masks(width):
    lane=lax.broadcasted_iota(jnp.int32,(1,128),1)
    return [((lane//width)==h) for h in range(128//width)]

def run_beside(plan,depth):
    begin,ticks,finish=plan
    step=pl.program_id(0); steps=pl.num_programs(0)
    @pl.when(step==0)
    def _():
        greet(depth)
        begin()
    for n in range(7):
        @pl.when(step==n+1)
        def _():
            if n<len(ticks): ticks[n]()
    def after():
        @pl.when(step==steps-1)
        def _():
            for tick in ticks[7:]: tick()
            finish()
    return after

def fwd_kernel(causal, block, width, moved, depth, lim_ref, q_ref, k_ref, v_ref, *refs):
    ctx_ref,lse_ref=refs[moved:moved+2]
    if moved:
        after=run_beside(gather_plan(refs[:moved],refs[moved+2:2*moved+2],refs[2*moved+2:],depth),depth)
    rows=q_ref.shape[0]; keys=k_ref.shape[0]
    masks=head_masks(width)
    k=k_ref[...]
    v=v_ref[...]
    vm=[jnp.where(m,v,jnp.zeros_like(v)) for m in masks]
    for i in range(rows//block):
        kend=(i+1)*block if causal else keys
        q=q_ref[pl.ds(i*block,block),:]*jnp.bfloat16(width**-0.5)
        ctx=None
        for h,m in enumerate(masks):
            s=dot(jnp.where(m,q,jnp.zeros_like(q)),k[:kend],NT)
            if causal:
                tail=s[:,kend-block:]
                r=lax.broadcasted_iota(jnp.int32,tail.shape,0)
                c=lax.broadcasted_iota(jnp.int32,tail.shape,1)
                tail=jnp.where(c<=r,tail,NEGATIVE)
                s=tail if kend==block else jnp.concatenate([s[:,:kend-block],tail],1)
            else:
                c=lax.broadcasted_iota(jnp.int32,s.shape,1)
                s=jnp.where(c<lim_ref[0],s,NEGATIVE)
            top=jnp.max(s,axis=1,keepdims=True)
            p=jnp.exp(s-top)
            total=jnp.sum(p,axis=1,keepdims=True)
            part=dot(p.astype(jnp.bfloat16),vm[h][:kend])*(1.0/total)
            ctx=part if ctx is None else ctx+part
            lse=jnp.broadcast_to(top+jnp.log(total),(block,128))
            lse_ref[0,pl.ds(h,1),pl.ds(i*block,block)]=jnp.transpose(lse)[:1]
        ctx_ref[pl.ds(i*block,block),:]=ctx.astype(jnp.bfloat16)
    if moved: after()

def flash_fwd(q,k,v,limit,causal,block=256,width=64,moves=(),depth=0,collective_id=None):
    rows,d=q.shape; keys=k.shape[0]
    pairs=d//128
    per=128//width
    count=len(moves)
    any_=pl.BlockSpec(memory_space=pl.ANY)
    spec=lambda n: pl.BlockSpec((n,128),lambda i,lim:(0,i))
    outs=pl.pallas_call(
        functools.partial(fwd_kernel,causal,block,width,count,depth),
        grid_spec=pltpu.PrefetchScalarGridSpec(
            num_scalar_prefetch=1, grid=(pairs,),
            in_specs=[spec(rows),spec(keys),spec(keys)]+[any_]*count,
            out_specs=[spec(rows),pl.BlockSpec((1,per,rows),lambda i,lim:(i,0,0))]+[any_]*count,
            scratch_shapes=gather_sems(count,depth) if count else []),
        out_shape=[jax.ShapeDtypeStruct((rows,d),jnp.bfloat16),jax.ShapeDtypeStruct((pairs,per,rows),jnp.float32)]+gather_shapes(moves,depth),
        compiler_params=pltpu.CompilerParams(vmem_limit_bytes=48*MIB,collective_id=collective_id,has_side_effects=count>0),
        cost_estimate=pl.CostEstimate(flops=4*rows*keys*d//(2 if causal else 1),bytes_accessed=4*rows*d*2,transcendentals=rows*keys*16//(2 if causal else 1)),
        name="attend_causal" if causal else "attend_text",
    )(limit,q,k,v,*moves)
    return outs[0],outs[1],gather_result(outs[2:],moves)

def back_of_pair(causal, block, width, lim_ref, q_ref, k_ref, v_ref, g_ref, ctx_ref, lse_ref, dq_ref, dk_acc, dv_acc, middle=None):
    rows=q_ref.shape[0]; keys=k_ref.shape[0]
    masks=head_masks(width)
    scale=jnp.bfloat16(width**-0.5)
    k=k_ref[...]; v=v_ref[...]
    km=[jnp.where(m,k*scale,jnp.zeros_like(k)) for m in masks]
    dk_acc[...]=jnp.zeros_like(dk_acc); dv_acc[...]=jnp.zeros_like(dv_acc)
    for i in range(rows//block):
        kend=(i+1)*block if causal else keys
        sl=pl.ds(i*block,block)
        q=q_ref[sl,:]*scale
        g=g_ref[sl,:]
        prod=g.astype(jnp.float32)*ctx_ref[sl,:].astype(jnp.float32)
        dq=None
        for h,m in enumerate(masks):
            qm=jnp.where(m,q,jnp.zeros_like(q))
            gm=jnp.where(m,g,jnp.zeros_like(g))
            delta=jnp.sum(jnp.where(m,prod,0.0),axis=1,keepdims=True)
            delta=jnp.transpose(jnp.broadcast_to(delta,(block,128)))[:1]
            lse=lse_ref[0,pl.ds(h,1),sl]
            s=dot(k[:kend],qm,NT)
            if causal:
                tail=s[kend-block:]
                r=lax.broadcasted_iota(jnp.int32,tail.shape,0)
                c=lax.broadcasted_iota(jnp.int32,tail.shape,1)
                tail=jnp.where(r<=c,tail,NEGATIVE)
                s=tail if kend==block else jnp.concatenate([s[:kend-block],tail],0)
            else:
                r=lax.broadcasted_iota(jnp.int32,s.shape,0)
                s=jnp.where(r<lim_ref[0],s,NEGATIVE)
            p=jnp.exp(s-lse)
            dp=dot(v[:kend],gm,NT)
            ds=(p*(dp-delta)).astype(jnp.bfloat16)
            dk_acc[:kend,:]+=dot(ds,qm)
            dv_acc[:kend,:]+=dot(p.astype(jnp.bfloat16),gm)
            part=dot(ds,km[h][:kend],TN)
            dq=part if dq is None else dq+part
        dq_ref[sl,:]=dq.astype(jnp.bfloat16)
        if middle and i==rows//block//2: middle()

def bwd_kernel(causal, block, width, lim_ref, *refs):
    dq_ref,dk_ref,dv_ref,dk_acc,dv_acc=refs[6:]
    back_of_pair(causal,block,width,lim_ref,*refs[:6],dq_ref,dk_acc,dv_acc)
    dk_ref[...]=dk_acc[...].astype(jnp.bfloat16)
    dv_ref[...]=dv_acc[...].astype(jnp.bfloat16)

def flash_bwd(q,k,v,g,ctx,lse,limit,causal,block=256,width=64):
    rows,d=q.shape; keys=k.shape[0]
    pairs=d//128; per=128//width
    spec=lambda n: pl.BlockSpec((n,128),lambda i,lim:(0,i))
    return pl.pallas_call(
        functools.partial(bwd_kernel,causal,block,width),
        grid_spec=pltpu.PrefetchScalarGridSpec(
            num_scalar_prefetch=1,grid=(pairs,),
            in_specs=[spec(rows),spec(keys),spec(keys),spec(rows),spec(rows),pl.BlockSpec((1,per,rows),lambda i,lim:(i,0,0))],
            out_specs=[spec(rows),spec(keys),spec(keys)],
            scratch_shapes=[pltpu.VMEM((keys,128),jnp.float32)]*2),
        out_shape=[jax.ShapeDtypeStruct((n,d),jnp.bfloat16) for n in (rows,keys,keys)],
        compiler_params=pltpu.CompilerParams(vmem_limit_bytes=60*MIB),
        name="attend_causal_back" if causal else "attend_text_back",
    )(limit,q,k,v,g,ctx,lse)

def sub_layer_kernel(causal, block, width, pairs, depth, lim_ref, flag_ref, *refs):
    pair_refs=refs[:6]; refs=refs[6:]
    normed_ref,source_ref,whole_ref,out_ref,gain_ref=refs[:5]; refs=refs[5:]
    late_count=5 if causal else 6
    late_in=refs[:late_count]; refs=refs[late_count:]
    carried=4 if causal else 2
    before,starts=refs[:2],refs[2:2+carried]; refs=refs[2+carried:]
    if causal: grad_out,sums_ref=refs[:2]; refs=refs[2:]
    else: grad_out,low_out,ctx_out,dec_ref,enc_ref,sums_ref=refs[:6]; refs=refs[6:]
    results=refs[:4]; refs=refs[4:]
    left=(None,None)
    if not causal: left=refs[:2]; refs=refs[2:]
    ends=refs[:carried]; refs=refs[carried:]
    late=refs[:late_count]; late_sem=refs[late_count]; refs=refs[late_count+1:]
    normed_t,source_t,whole_t,dq_all,dk_all,dv_all,dk_acc,dv_acc,out_part=refs[:9]; refs=refs[9:]
    low_all,ctx_all=(None,None) if causal else refs[:2]
    streams=refs if causal else refs[2:]
    half=STREAM
    earlier=streams[2*half:]; streams=streams[:2*half]
    count=pairs if causal else pairs-CROSS_LATE
    before_late=CROSS_LATE if causal else FFN_LATE
    step=pl.program_id(0)
    rows=pair_refs[0].shape[0]
    def keep_pair(first):
        def store(i,total):
            for n in range(2):
                results[first+n][:,pl.ds(pl.multiple_of(i*128,128),128)]=total[:,n*128:(n+1)*128]
        return store
    tick1,middle1=stream_plan(count,0,keep_pair(0),streams[:half],depth)
    tick2,middle2=stream_plan(count,1,keep_pair(2),streams[half:],depth)
    def store_earlier(w,total):
        if causal:
            at=pairs-before_late+w//2
            for n in range(2): ends[w%2*2+n][:,at*128:(at+1)*128]=total[:,n*128:(n+1)*128]
        elif w%2==0:
            wide=total.shape[1]
            at=ends[0].shape[1]//wide-before_late+w//2
            ends[0][:,at*wide:(at+1)*wide]=total
        else:
            ends[1][ends[1].shape[0]-before_late+w//2]=total
    begin,ticks,finish=(lambda: None),[],(lambda: None)
    if before_late: begin,ticks,finish=reduce_plan([before[w%2].at[w//2] for w in range(2*before_late)],store_earlier,earlier,depth)
    def leave(n):
        m=(pairs-CROSS_LATE+n)%2
        return [pltpu.make_async_copy(streams[half*h].at[m],left[h].at[n],late_sem.at[late_count+2*n+h]) for h in (0,1)]
    def late_copy(n): return pltpu.make_async_copy(late_in[n],late[n],late_sem.at[n])
    @pl.when(step==0)
    def _():
        greet(depth)
        begin()
        for n in range(late_count): late_copy(n).start()
        for a,b in zip(starts,ends): b[...]=a[...]
        normed_t[...]=jnp.transpose(normed_ref[...])
        whole_t[...]=jnp.transpose(whole_ref[...])
        if not causal: source_t[...]=jnp.transpose(source_ref[...])
    tick1(step); tick2(step)
    for n in range(len(ticks)):
        @pl.when(step==n+1)
        def _(): ticks[n]()
    here=pl.ds(pl.multiple_of(step*128,128),128)
    back_of_pair(causal,block,width,lim_ref,*pair_refs,dq_all.at[:,here],dk_acc,dv_acc,lambda: (middle1(step),middle2(step)))
    dq=dq_all[:,here]; dk=dk_acc[...].astype(jnp.bfloat16); dv=dv_acc[...].astype(jnp.bfloat16)
    dk_all[:,here]=dk; dv_all[:,here]=dv
    def add_sum(n,value): sums_ref[n:n+1,here]=jnp.sum(value.astype(jnp.float32),axis=0,keepdims=True)
    add_sum(0,dq); add_sum(1,dv)
    @pl.when(step%2==0)
    def _():
        out_part[...]=dot(whole_t[...],out_ref[...]).astype(jnp.bfloat16)
        add_sum(2,out_ref[:,:128])
        write_made(streams[half],step,128,out_part[:,:128])
    @pl.when(step%2==1)
    def _():
        add_sum(2,out_ref[:,128:])
        write_made(streams[half],step,128,out_part[:,128:])
    if causal:
        write_made(streams[0],step,0,dot(normed_t[...],jnp.concatenate([dq,dk],1)).astype(jnp.bfloat16))
        write_made(streams[half],step,0,dot(normed_t[...],dv).astype(jnp.bfloat16))
    else:
        both=dot(source_t[...],jnp.concatenate([dk,dv],1)).astype(jnp.bfloat16)
        write_made(streams[0],step,0,dot(normed_t[...],dq).astype(jnp.bfloat16))
        write_made(streams[0],step,128,both[:,:128])
        write_made(streams[half],step,0,both[:,128:])
        for n in range(CROSS_LATE):
            @pl.when(step==pairs-CROSS_LATE+n)
            def _():
                for copy in leave(n): copy.start()
    @pl.when(step==pairs-1)
    def _():
        for n in range(late_count): late_copy(n).wait()
        gain=gain_ref[0:1,:]
        sums_ref[3:8,:]=jnp.zeros((5,sums_ref.shape[1]),jnp.float32)
        strip=256
        for r in range(rows//strip):
            tick1(pairs+r); tick2(pairs+r)
            sl=pl.ds(r*strip,strip)
            if causal:
                wq,wk,wv,residual,total=late
                grad=dot(dq_all[sl,:],wq[...],NT)+dot(dk_all[sl,:],wk[...],NT)+dot(dv_all[sl,:],wv[...],NT)
            else:
                wq,wk,wv,wo,residual,total=late
                grad=dot(dq_all[sl,:],wq[...],NT)
            hat,inverse=normal(residual[sl,:].astype(jnp.float32))
            sums_ref[3:4,:]+=jnp.sum(grad*hat,axis=0,keepdims=True)
            sums_ref[4:5,:]+=jnp.sum(grad,axis=0,keepdims=True)
            whole=total[sl,:]+pull_norm(hat,inverse,gain,grad)
            total[sl,:]=whole
            middle1(pairs+r); middle2(pairs+r)
            if not causal:
                low_all[sl,:]=whole.astype(jnp.bfloat16)
                ctx_all[sl,:]=dot(low_all[sl,:],wo[...],NT).astype(jnp.bfloat16)
        copies=[pltpu.make_async_copy(late[-1],grad_out,late_sem.at[0])]
        if not causal:
            copies+=[pltpu.make_async_copy(low_all,low_out,late_sem.at[1]),pltpu.make_async_copy(ctx_all,ctx_out,late_sem.at[2])]
        for copy in copies: copy.start()
        for t in range(pairs+rows//strip,count+LAST_LAG): tick1(t); tick2(t); middle1(t); middle2(t)
        finish()
        if not causal:
            memory_grad=dot(dk_all[...],late[1][...],NT)+dot(dv_all[...],late[2][...],NT)
            flag=jnp.where(flag_ref[0]==1,1.0,0.0)
            dec_ref[...]=memory_grad*flag
            enc_ref[...]=memory_grad*(1.0-flag)
            for n in range(CROSS_LATE): copies+=leave(n)
        for copy in copies: copy.wait()

def sub_layer_back(q,k,v,g,ctx,lse,limit,flag,causal,normed,source,out_grad,gain,late,before,starts,depth,collective_id,block=256,width=64):
    rows,d=q.shape; keys=k.shape[0]
    pairs=d//128; per=128//width
    each=d//(8*depth)
    bf=jnp.bfloat16; f32=jnp.float32
    spec=lambda n: pl.BlockSpec((n,128),lambda i,a,b:(0,i))
    once=lambda shape: pl.BlockSpec(shape,lambda i,a,b:(0,0),pipeline_mode=pl.Buffered(1))
    keep=lambda shape: pl.BlockSpec(shape,lambda i,a,b:(0,0))
    any_=pl.BlockSpec(memory_space=pl.ANY)
    shape=lambda n,t: jax.ShapeDtypeStruct((n,d),t)
    in_specs=[spec(rows),spec(keys),spec(keys),spec(rows),spec(rows),pl.BlockSpec((1,per,rows),lambda i,a,b:(i,0,0))]
    in_specs+=[once((rows,d)),once(source.shape),once((rows,d)),pl.BlockSpec((rows,256),lambda i,a,b:(0,i//2)),once(gain.shape)]+[any_]*(len(late)+2)
    in_specs+=[pl.BlockSpec(a.shape,lambda i,a,b,n=a.ndim:(0,)*n,pipeline_mode=pl.Buffered(1)) for a in starts]
    out_specs=[any_]; out_shape=[shape(rows,f32)]
    scratch=[pltpu.VMEM(a.shape,a.dtype) for a in late]+[DMA((len(late)+2*CROSS_LATE,))]
    scratch+=[pltpu.VMEM((d,rows),bf),pltpu.VMEM((8,128) if causal else (d,keys),bf),pltpu.VMEM((d,rows),bf)]
    scratch+=[pltpu.VMEM((n,d),bf) for n in (rows,keys,keys)]+[pltpu.VMEM((keys,128),f32)]*2+[pltpu.VMEM((d,256),bf)]
    if not causal:
        out_specs+=[any_,any_,keep((keys,d)),keep((keys,d))]
        out_shape+=[shape(rows,bf),shape(rows,bf),shape(keys,f32),shape(keys,f32)]
        scratch+=[pltpu.VMEM((rows,d),bf)]*2
    out_specs+=[keep((8,d))]+[keep((each,d))]*4
    out_shape+=[shape(8,f32)]+[shape(each,f32)]*4
    if not causal:
        out_specs+=[any_]*2
        out_shape+=[jax.ShapeDtypeStruct((max(CROSS_LATE,1),2,2,depth,2,each,256),bf)]*2
    out_specs+=[pl.BlockSpec(a.shape,lambda i,a,b,n=a.ndim:(0,)*n) for a in starts]
    out_shape+=[jax.ShapeDtypeStruct(a.shape,a.dtype) for a in starts]
    scratch+=stream_scratch(each,256,depth)*2
    before_late=CROSS_LATE if causal else FFN_LATE
    if before_late: scratch+=reduce_scratch([before[w%2].shape[5:]+(bf,) for w in range(2*before_late)],depth)
    return pl.pallas_call(
        functools.partial(sub_layer_kernel,causal,block,width,pairs,depth),
        grid_spec=pltpu.PrefetchScalarGridSpec(num_scalar_prefetch=2,grid=(pairs,),in_specs=in_specs,out_specs=out_specs,scratch_shapes=scratch),
        out_shape=out_shape,
        compiler_params=pltpu.CompilerParams(vmem_limit_bytes=62*MIB,collective_id=collective_id,has_side_effects=True),
        cost_estimate=pl.CostEstimate(flops=20*rows*keys*d,bytes_accessed=20*rows*d*2,transcendentals=rows*keys*16),
        name="self_back" if causal else "cross_back",
    )(limit,flag,q,k,v,g,ctx,lse,normed,source,ctx,out_grad,gain,*late,*before,*starts)

MESH=pl.DeviceIdType.MESH
DMA=pltpu.SemaphoreType.DMA

def place():
    dp=lax.axis_index("dp"); fs=lax.axis_index("fsdp")
    return dp,fs,fs//2,fs%2

def turned(index,bit):
    return index+bit-2*bit*((index//bit)%2)

def greet(depth):
    dp,fs,z,c=place()
    partners=[(dp,lax.rem(z+k,depth)*2+c) for k in range(1,depth)]+[(turned(dp,1),fs),(turned(dp,2),fs),(dp,z*2+1-c)]
    barrier=pltpu.get_barrier_semaphore()
    for device in partners:
        pl.semaphore_signal(barrier,inc=1,device_id=device,device_id_type=MESH)
    pl.semaphore_wait(barrier,len(partners))

PIECES=2
AHEAD=2

def gather_sems(count,depth):
    count=PIECES*count
    return [DMA((count,)),DMA((count,depth-1)),DMA((count,depth-1)),DMA((count,3)),DMA((count,3)),DMA((count,4)),DMA((count,4))]

def gather_plan(ins,outs,sems,depth):
    parts=[]
    for a,b in zip(ins,outs):
        wide=a.shape[1]//PIECES
        if wide%128: parts+=[(a,b)]
        else: parts+=[(a.at[:,n*wide:(n+1)*wide],b.at[:,:,:,:,n*wide:(n+1)*wide]) for n in range(PIECES)]
    ins,outs=[p[0] for p in parts],[p[1] for p in parts]
    count=len(ins)
    local,z_send,z_recv,a_send,a_recv,c_send,c_recv=sems
    dp,fs,z,c=place()
    def line(w,k):
        return pltpu.make_async_remote_copy(ins[w],outs[w].at[dp,z,c],z_send.at[w,k-1],z_recv.at[w,k-1],(dp,lax.rem(z+k,depth)*2+c),MESH)
    def across(w,n,src_dp,bit):
        ref=outs[w].at[src_dp,:,c]
        return pltpu.make_async_remote_copy(ref,ref,a_send.at[w,n],a_recv.at[w,n],(turned(dp,bit),fs),MESH)
    def core(w,n,src_dp):
        ref=outs[w].at[src_dp,:,c]
        return pltpu.make_async_remote_copy(ref,ref,c_send.at[w,n],c_recv.at[w,n],(dp,z*2+1-c),MESH)
    def own(w):
        return pltpu.make_async_copy(ins[w],outs[w].at[dp,z,c],local.at[w])
    def bits(w):
        return 1+w%2,2-w%2
    def step0(w):
        f,g=bits(w)
        own(w).wait()
        for k in range(1,depth): line(w,k).wait_recv()
        across(w,0,dp,f).start()
        across(w,1,dp,g).start()
        core(w,0,dp).start()
    def step1(w):
        f,g=bits(w)
        across(w,0,dp,f).wait_recv()
        across(w,2,turned(dp,f),g).start()
        core(w,1,turned(dp,f)).start()
    def step2(w):
        f,g=bits(w)
        across(w,1,dp,g).wait_recv()
        core(w,2,turned(dp,g)).start()
    def step3(w):
        f,g=bits(w)
        across(w,2,turned(dp,f),g).wait_recv()
        core(w,3,turned(turned(dp,f),g)).start()
    def along(t):
        for w in (2*t,2*t+1):
            if w<count:
                own(w).start()
                for k in range(1,depth): line(w,k).start()
    def begin():
        for t in range(AHEAD): along(t)
    def tick(t):
        along(t+AHEAD)
        for n,step in enumerate((step0,step1,step2,step3)):
            for w in (2*(t-n),2*(t-n)+1):
                if 0<=w<count: step(w)
    def finish():
        for w in range(count):
            f,g=bits(w)
            for k in range(1,depth): line(w,k).wait_send()
            across(w,0,dp,f).wait_send(); across(w,1,dp,g).wait_send(); across(w,2,dp,g).wait_send()
            for n in range(4): core(w,n,dp).wait()
    return begin,[functools.partial(tick,t) for t in range((count+1)//2+3)],finish

def reduce_scratch(kinds,depth):
    count=len(kinds)
    vmem=lambda *lead: [pltpu.VMEM(lead+(r,n),d) for r,n,d in kinds]
    return (vmem(2,2,depth)+vmem(2,2,depth)+vmem(2,depth)+vmem(depth)+vmem(depth-1)
      +[DMA((count,)),DMA((count,)),DMA((count,)),DMA((count,2)),DMA((count,2)),DMA((count,depth-1)),DMA((count,depth-1))])

def reduce_plan(ins,store,scratch,depth):
    count=len(ins)
    held,r0,r1,r2,r3=(scratch[n*count:(n+1)*count] for n in range(5))
    local,c_send,c_recv,a_send,a_recv,z_send,z_recv=scratch[5*count:]
    dp,fs,z,c=place()
    hi,lo=dp//2,dp%2
    def own(w):
        return pltpu.make_async_copy(ins[w].at[:,:,:,c],held[w],local.at[w])
    def core(w):
        return pltpu.make_async_remote_copy(ins[w].at[:,:,:,1-c],r0[w],c_send.at[w],c_recv.at[w],(dp,z*2+1-c),MESH)
    def first(w):
        if w%2: return pltpu.make_async_remote_copy(held[w].at[1-hi],r1[w],a_send.at[w,0],a_recv.at[w,0],(turned(dp,2),fs),MESH)
        return pltpu.make_async_remote_copy(held[w].at[:,1-lo],r1[w],a_send.at[w,0],a_recv.at[w,0],(turned(dp,1),fs),MESH)
    def second(w):
        if w%2: return pltpu.make_async_remote_copy(held[w].at[hi,1-lo],r2[w],a_send.at[w,1],a_recv.at[w,1],(turned(dp,1),fs),MESH)
        return pltpu.make_async_remote_copy(held[w].at[1-hi,lo],r2[w],a_send.at[w,1],a_recv.at[w,1],(turned(dp,2),fs),MESH)
    def line(w,k):
        return pltpu.make_async_remote_copy(held[w].at[hi,lo,lax.rem(z+k,depth)],r3[w].at[k-1],z_send.at[w,k-1],z_recv.at[w,k-1],(dp,lax.rem(z+k,depth)*2+c),MESH)
    def step0(w):
        own(w).wait(); core(w).wait_recv()
        for i in range(4): held[w][i//2,i%2]=held[w][i//2,i%2]+r0[w][i//2,i%2]
        first(w).start()
    def step1(w):
        first(w).wait_recv()
        for i in range(2):
            if w%2: held[w][hi,i]=held[w][hi,i]+r1[w][i]
            else: held[w][i,lo]=held[w][i,lo]+r1[w][i]
        second(w).start()
    def step2(w):
        second(w).wait_recv()
        held[w][hi,lo]=held[w][hi,lo]+r2[w][...]
        for k in range(1,depth): line(w,k).start()
    def step3(w):
        total=held[w][hi,lo,z].astype(jnp.float32)
        for k in range(1,depth):
            line(w,k).wait_recv()
            total=total+r3[w][k-1].astype(jnp.float32)
        store(w,total)
    def begin():
        for w in range(count):
            core(w).start(); own(w).start()
    def tick(t):
        for n,step in enumerate((step0,step1,step2,step3)):
            if 0<=t-n<count: step(t-n)
    def finish():
        for w in range(count):
            core(w).wait_send(); first(w).wait_send(); second(w).wait_send()
            for k in range(1,depth): line(w,k).wait_send()
    return begin,[functools.partial(tick,t) for t in range(count+3)],finish

def gather_shapes(shards,depth):
    return [jax.ShapeDtypeStruct((4,depth,2)+s.shape,s.dtype) for s in shards]

def gather_result(outs,shards):
    return [o.reshape((-1,)+s.shape[1:]) for o,s in zip(outs,shards)]

def reduce_parts(partials,depth):
    return [p.reshape((2,2,depth,2,p.shape[0]//(8*depth),p.shape[1])) for p in partials]

def shuffle(read,write,outer,inner,part):
    each=128//part
    for t in range(outer*inner//each):
        whole=None
        for u in range(each):
            b,a=divmod(t*each+u,outer)
            tile,at=divmod(a*inner+b,each)
            piece=read(tile)
            if u!=at: piece=pltpu.roll(piece,(u-at)*part%128,1)
            lane=lax.broadcasted_iota(jnp.int32,piece.shape,1)
            whole=piece if whole is None else jnp.where(lane>=u*part,piece,whole)
        write(t,whole)

def first_kernel(count,lines,depth,blocks,*refs):
    ins,vectors,wide=refs[:count],refs[count:count+lines],refs[count+lines]
    refs=refs[count+lines+1:]
    outs,table,long=refs[:count],refs[count],refs[count+1]
    packed,every=refs[count+2:count+4]
    part=128//blocks
    each=vectors[0].shape[1]
    greet(depth)
    packed[...]=jnp.zeros_like(packed)
    for n in range(lines): packed[n:n+1,:each]=vectors[n][...].astype(jnp.float32)
    packed[lines:lines+1,:]=wide[...].astype(jnp.float32)
    begin,ticks,finish=gather_plan([packed]+list(ins),[every]+list(outs),refs[count+4:],depth)
    begin()
    for tick in ticks: tick()
    finish()
    lane=lax.broadcasted_iota(jnp.int32,(16,128),1)
    group=128//each
    def device(n): return every[n//(2*depth),(n//2)%depth,n%2]
    for m in range(8*depth//group):
        tile=device(m*group)
        for r in range(1,group):
            tile=jnp.where(lane>=r*each,pltpu.roll(device(m*group+r),r*each,1),tile)
        table[:,m*128:(m+1)*128]=tile
    def write_long(t,value): long[:,t*128:(t+1)*128]=value
    shuffle(lambda n: device(n)[lines:lines+1],write_long,8*depth,blocks,part)

def gather_first(shards,vectors,wide,blocks,depth,collective_id):
    count=len(shards); lines=len(vectors)
    any_=pl.BlockSpec(memory_space=pl.ANY); vm=pl.BlockSpec(memory_space=pltpu.VMEM)
    total=vectors[0].shape[0]*8*depth
    outs=pl.pallas_call(
        functools.partial(first_kernel,count,lines,depth,blocks),
        in_specs=[any_]*count+[vm]*(lines+1),
        out_specs=[any_]*count+[vm]*2,
        out_shape=gather_shapes(shards,depth)+[jax.ShapeDtypeStruct((16,total),jnp.float32),jax.ShapeDtypeStruct((1,128*8*depth),jnp.float32)],
        scratch_shapes=[pltpu.VMEM((16,128),jnp.float32),pltpu.VMEM((4,depth,2,16,128),jnp.float32)]+gather_sems(count+1,depth),
        compiler_params=pltpu.CompilerParams(collective_id=collective_id,has_side_effects=True),
        name="gather_first",
    )(*shards,*[v[None] for v in vectors],wide[None])
    return gather_result(outs[:count],shards)+list(outs[count:])

def last_kernel(count,depth,*refs):
    ins,outs,scratch=refs[:count],refs[count:2*count],refs[2*count:]
    greet(depth)
    def store(w,total): outs[w][...]=total
    begin,ticks,finish=reduce_plan(ins,store,scratch,depth)
    begin()
    for tick in ticks: tick()
    finish()

def reduce_rows(partials,depth,collective_id):
    count=len(partials)
    parts=reduce_parts(partials,depth)
    kinds=[p.shape[4:]+(p.dtype,) for p in parts]
    return pl.pallas_call(
        functools.partial(last_kernel,count,depth),
        in_specs=[pl.BlockSpec(memory_space=pl.ANY)]*count,
        out_specs=[pl.BlockSpec(memory_space=pltpu.VMEM)]*count,
        out_shape=[jax.ShapeDtypeStruct(k[:2],jnp.float32) for k in kinds],
        scratch_shapes=reduce_scratch(kinds,depth),
        compiler_params=pltpu.CompilerParams(collective_id=collective_id,has_side_effects=True,vmem_limit_bytes=60*MIB),
        name="reduce_rows",
    )(*parts)

SLOTS=4
STREAM=14
LAST_LAG=5

def stream_scratch(rows,cols,depth):
    vmem=lambda *lead: pltpu.VMEM(lead+(rows,cols),jnp.bfloat16)
    return [vmem(2,2,2,depth,2),vmem(SLOTS,2,2,depth),vmem(SLOTS,2,2,depth),vmem(SLOTS,2,depth),vmem(SLOTS,2,depth),vmem(SLOTS,depth),vmem(SLOTS,depth),vmem(SLOTS,depth-1),
      DMA((SLOTS,)),DMA((SLOTS,)),DMA((SLOTS,2)),DMA((SLOTS,2)),DMA((SLOTS,depth-1)),DMA((SLOTS,depth-1))]

def stream_plan(count,odd,store,scratch,depth):
    made,r0,sum0,r1,sum1,r2,sum2,r3,c_send,c_recv,a_send,a_recv,z_send,z_recv=scratch
    dp,fs,z,c=place()
    hi,lo=dp//2,dp%2
    here,there=(hi,1-hi) if odd else (lo,1-lo)
    here2,there2=(lo,1-lo) if odd else (hi,1-hi)
    def slot(i): return lax.rem(i,SLOTS)
    def core(i):
        s=slot(i)
        return pltpu.make_async_remote_copy(made.at[lax.rem(i,2),:,:,:,1-c],r0.at[s],c_send.at[s],c_recv.at[s],(dp,z*2+1-c),MESH)
    def first(i):
        s=slot(i)
        src=sum0.at[s,there] if odd else sum0.at[s,:,there]
        return pltpu.make_async_remote_copy(src,r1.at[s],a_send.at[s,0],a_recv.at[s,0],(turned(dp,2 if odd else 1),fs),MESH)
    def second(i):
        s=slot(i)
        return pltpu.make_async_remote_copy(sum1.at[s,there2],r2.at[s],a_send.at[s,1],a_recv.at[s,1],(turned(dp,1 if odd else 2),fs),MESH)
    def line(i,k):
        s=slot(i)
        return pltpu.make_async_remote_copy(sum2.at[s,lax.rem(z+k,depth)],r3.at[s,k-1],z_send.at[s,k-1],z_recv.at[s,k-1],(dp,lax.rem(z+k,depth)*2+c),MESH)
    def step0(i):
        s=slot(i); m=lax.rem(i,2)
        core(i).wait()
        for a in range(4):
            sum0[s,a//2,a%2]=made[m,a//2,a%2,:,c]+r0[s,a//2,a%2]
        first(i).start()
    def step1(i):
        s=slot(i)
        first(i).wait()
        for a in range(2):
            sum1[s,a]=(sum0[s,here,a] if odd else sum0[s,a,here])+r1[s,a]
        second(i).start()
    def step2(i):
        s=slot(i)
        second(i).wait()
        sum2[s]=sum1[s,here2]+r2[s]
        for k in range(1,depth): line(i,k).start()
    def step3(i):
        s=slot(i)
        total=sum2[s,z].astype(jnp.float32)
        for k in range(1,depth):
            line(i,k).wait()
            total=total+r3[s,k-1].astype(jnp.float32)
        store(i,total)
    def run(j,stages):
        for lag,step in stages:
            if isinstance(j,int):
                if 0<=j-lag<count: step(jnp.int32(j-lag))
            else:
                @pl.when((j>=lag)&(j<lag+count))
                def _(): step(j-lag)
    def tick(j):
        run(j,((5,step3),(4,step2),(3,step1),(1,lambda i: core(i).start())))
    def middle(j):
        run(j,((1,step0),))
    return tick,middle

def write_made(made,i,col,value):
    shape=made.shape[1:6]+value.shape[1:]
    made[lax.rem(i,2),:,:,:,:,:,col:col+value.shape[1]]=value.reshape(shape)


def deliver_kernel(count,devices,blocks,*refs):
    ins,outs,held,(here,there)=refs[:count],refs[count:2*count],refs[2*count:3*count-1],refs[3*count-1:]
    come=[pltpu.make_async_copy(ins[n],held[n-1],here.at[n]) for n in range(1,count)]
    go=[pltpu.make_async_copy(held[n-1],outs[n],there.at[n]) for n in range(1,count)]
    for copy in come: copy.start()
    def read(t): return ins[0][:,t*128:(t+1)*128]
    def write(t,value): outs[0][:,t*128:(t+1)*128]=value
    shuffle(read,write,blocks,devices,128//blocks)
    for a,b in zip(come,go):
        a.wait()
        b.start()
    for copy in go: copy.wait()

def deliver(arrays,devices,blocks):
    count=len(arrays)
    any_=pl.BlockSpec(memory_space=pl.ANY); vm=pl.BlockSpec(memory_space=pltpu.VMEM)
    return pl.pallas_call(
        functools.partial(deliver_kernel,count,devices,blocks),
        in_specs=[vm]+[any_]*(count-1),
        out_specs=[vm]+[any_]*(count-1),
        out_shape=[jax.ShapeDtypeStruct(a.shape,a.dtype) for a in arrays],
        scratch_shapes=[pltpu.VMEM(a.shape,a.dtype) for a in arrays[1:]]+[DMA((count,)),DMA((count,))],
        compiler_params=pltpu.CompilerParams(vmem_limit_bytes=62*MIB),
        name="deliver",
    )(*arrays)

def order_kernel(blocks,outer,shard,out):
    def read(t): return shard[:,t*128:(t+1)*128].astype(jnp.float32)
    def write(t,value): out[:,t*128:(t+1)*128]=value.astype(jnp.bfloat16)
    shuffle(read,write,outer,blocks,128//blocks)

def order_columns(shard,outer,blocks):
    return pl.pallas_call(
        functools.partial(order_kernel,blocks,outer),
        out_shape=jax.ShapeDtypeStruct(shard.shape,shard.dtype),
        name="order_columns",
    )(shard)

EPSILON=1e-05
def normal(tensor):
    centre=tensor-jnp.mean(tensor,axis=-1,keepdims=True)
    spread=jnp.mean(centre*centre,axis=-1,keepdims=True)
    inverse=lax.rsqrt(spread+EPSILON)
    return centre*inverse,inverse

def pull_norm(hat,inverse,gain,grad):
    scaled=grad*gain
    return inverse*(scaled-jnp.mean(scaled,axis=-1,keepdims=True)-hat*jnp.mean(scaled*hat,axis=-1,keepdims=True))

FFN_LATE=0
CROSS_LATE=0

def ffn_kernel(strip, steps, depth, length_ref, after_ref, cot_ref, w1_ref, w2_ref, b1_ref, vec_ref, wo_ref,
               mixed_ref, grad_ref, low_ref, ctx_ref, dw1_ref, dw2_ref, db1_ref, dvec_ref, late1_ref, late2_ref, n3, n3t, gf, branch, gn, wo, sem, *refs):
    j=pl.program_id(0)
    rows,d=after_ref.shape
    gain,shift,b2=vec_ref[0:1,:],vec_ref[1:2,:],vec_ref[2:3,:]
    def live(r):
        return (r*strip+lax.broadcasted_iota(jnp.int32,(strip,1),0)<length_ref[0]).astype(jnp.float32)
    if depth:
        half=len(refs)//2
        wide=w1_ref.shape[1]
        def store1(i,total): dw1_ref[:,pl.ds(pl.multiple_of(i*wide,128),wide)]=total
        def store2(i,total): dw2_ref[i]=total
        tick1,middle1=stream_plan(steps-FFN_LATE,0,store1,refs[:half],depth)
        tick2,middle2=stream_plan(steps-FFN_LATE,1,store2,refs[half:],depth)
        def leave(n):
            m=(steps-FFN_LATE+n)%2
            return [pltpu.make_async_copy(refs[0].at[m],late1_ref.at[n],sem.at[4+2*n]),pltpu.make_async_copy(refs[half].at[m],late2_ref.at[n],sem.at[5+2*n])]
    @pl.when(j==0)
    def _():
        if depth: greet(depth)
        pltpu.make_async_copy(wo_ref,wo,sem.at[2]).start()
        def one(r,total):
            sl=pl.ds(r*strip,strip)
            hat,_=normal(after_ref[sl,:])
            n3[sl,:]=(hat*gain+shift).astype(jnp.bfloat16)
            top=(cot_ref[sl,:].astype(jnp.float32)*live(r)).astype(jnp.bfloat16)
            gf[sl,:]=top
            return total+jnp.sum(top.astype(jnp.float32),axis=0,keepdims=True)
        dvec_ref[...]=jnp.zeros_like(dvec_ref)
        dvec_ref[2:3,:]=lax.fori_loop(0,rows//strip,one,jnp.zeros((1,d),jnp.float32))
        n3t[...]=jnp.transpose(n3[...])
        branch[...]=jnp.zeros_like(branch); gn[...]=jnp.zeros_like(gn)
    if depth:
        tick1(j); tick2(j)
    w1=w1_ref[...]; w2=w2_ref[...].reshape(w1.shape[1],d)
    pre=dot(n3[...],w1)+b1_ref[...]
    back=dot(gf[...],w2,NT).astype(jnp.bfloat16).astype(jnp.float32)
    if depth:
        middle1(j); middle2(j)
    root=0.7978845608028654
    square=pre*pre
    t=jnp.tanh(root*pre*(1.0+0.044715*square))
    half_t=0.5*(1.0+t)
    hidden=(pre*half_t).astype(jnp.bfloat16)
    slope=half_t+0.5*pre*(1.0-t*t)*(root*(1.0+3*0.044715*square))
    g_pre=(back*slope).astype(jnp.bfloat16)
    db1_ref[...]=jnp.sum(g_pre.astype(jnp.float32),axis=0,keepdims=True)
    branch[...]+=dot(hidden,w2)
    dw2=dot(hidden,gf[...],TN).astype(jnp.bfloat16)
    dw1=dot(n3t[...],g_pre).astype(jnp.bfloat16)
    if depth:
        write_made(refs[0],j,0,dw1)
        write_made(refs[half],j,0,dw2)
        for n in range(FFN_LATE):
            @pl.when(j==steps-FFN_LATE+n)
            def _():
                for copy in leave(n): copy.start()
    else:
        dw1_ref[...]=dw1
        dw2_ref[...]=dw2.reshape(dw2_ref.shape)
    gn[...]+=dot(g_pre,w1,NT)
    @pl.when(j==steps-1)
    def _():
        def one(r):
            sl=pl.ds(r*strip,strip)
            valid=live(r)
            after=after_ref[sl,:]
            n3[sl,:]=((after+(branch[sl,:]+b2))*valid).astype(jnp.bfloat16)
            hat,inverse=normal(after)
            grad=gn[sl,:]
            dvec_ref[0:1,:]+=jnp.sum(grad*hat,axis=0,keepdims=True)
            dvec_ref[1:2,:]+=jnp.sum(grad,axis=0,keepdims=True)
            grad=cot_ref[sl,:].astype(jnp.float32)*valid+pull_norm(hat,inverse,gain,grad)
            gn[sl,:]=grad
            gf[sl,:]=grad.astype(jnp.bfloat16)
            n3t[sl,:]=dot(gf[sl,:],wo[...],NT).astype(jnp.bfloat16)
        pltpu.make_async_copy(wo_ref,wo,sem.at[2]).wait()
        for r in range(rows//strip):
            if depth and r%2==0:
                tick1(steps+r//2); tick2(steps+r//2)
            one(r)
            if depth and r%2==0:
                middle1(steps+r//2); middle2(steps+r//2)
        copies=[pltpu.make_async_copy(a,b,sem.at[n]) for n,(a,b) in enumerate(((n3,mixed_ref),(gn,grad_ref),(gf,low_ref),(n3t,ctx_ref)))]
        for copy in copies: copy.start()
        if depth:
            for t in range(steps+rows//strip//2,steps-FFN_LATE+LAST_LAG):
                tick1(t); tick2(t); middle1(t); middle2(t)
            for n in range(FFN_LATE): copies+=leave(n)
        for copy in copies: copy.wait()

def feed_forward(after,cot,length,w1,w2,b1,vec,wo,block=512,strip=128,depth=0,collective_id=None):
    rows,d=after.shape; ff=w1.shape[1]
    steps=ff//block
    once=lambda shape: pl.BlockSpec(shape,lambda j,n:(0,0),pipeline_mode=pl.Buffered(1))
    keep=lambda shape: pl.BlockSpec(shape,lambda j,n:(0,)*len(shape))
    any_=pl.BlockSpec(memory_space=pl.ANY)
    wide=pl.BlockSpec((d,block),lambda j,n:(0,j)); line=pl.BlockSpec((1,block),lambda j,n:(0,j))
    tall=pl.BlockSpec((w2.shape[0],block//w2.shape[0],d),lambda j,n:(0,j,0))
    bf=jnp.bfloat16; f32=jnp.float32
    scratch=[pltpu.VMEM((rows,d),bf),pltpu.VMEM((d,rows),bf),pltpu.VMEM((rows,d),bf),pltpu.VMEM((rows,d),f32),pltpu.VMEM((rows,d),f32),pltpu.VMEM((d,d),bf),DMA((4+2*FFN_LATE,))]
    if depth:
        each=d//(8*depth); part=block//(8*depth)
        grad_specs=[keep((each,ff)),keep((steps,part,d))]
        grad_shapes=[jax.ShapeDtypeStruct((each,ff),f32),jax.ShapeDtypeStruct((steps,part,d),f32)]
        late_shapes=[jax.ShapeDtypeStruct((max(FFN_LATE,1),2,2,depth,2,each,block),bf),jax.ShapeDtypeStruct((max(FFN_LATE,1),2,2,depth,2,part,d),bf)]
        scratch+=stream_scratch(each,block,depth)+stream_scratch(part,d,depth)
    else:
        grad_specs=[wide,tall]
        grad_shapes=[jax.ShapeDtypeStruct(w1.shape,bf),jax.ShapeDtypeStruct(w2.shape,bf)]
        late_shapes=[jax.ShapeDtypeStruct((8,128),bf)]*2
    return pl.pallas_call(
        functools.partial(ffn_kernel,strip,steps,depth),
        grid_spec=pltpu.PrefetchScalarGridSpec(
            num_scalar_prefetch=1,grid=(steps,),
            in_specs=[once((rows,d)),once((rows,d)),wide,tall,line,once(vec.shape),any_],
            out_specs=[any_]*4+grad_specs+[line,keep((8,d)),any_,any_],
            scratch_shapes=scratch),
        out_shape=[jax.ShapeDtypeStruct((rows,d),bf),jax.ShapeDtypeStruct((rows,d),f32)]+[jax.ShapeDtypeStruct((rows,d),bf)]*2+grad_shapes+[jax.ShapeDtypeStruct((1,ff),f32),jax.ShapeDtypeStruct((8,d),f32)]+late_shapes,
        compiler_params=pltpu.CompilerParams(vmem_limit_bytes=62*MIB,collective_id=collective_id,has_side_effects=depth>0),
        cost_estimate=pl.CostEstimate(flops=12*rows*d*ff,bytes_accessed=4*d*ff*2+rows*d*12,transcendentals=rows*ff),
        name="feed_forward",
    )(length,after,cot,w1,w2,b1,vec,wo)

AXES=("dp","fsdp")

def layer_norm(tensor, gain, shift):
    return normal(tensor)[0]*gain+shift

def layer_norm_back(tensor, gain, grad):
    hat,inverse=normal(tensor)
    return pull_norm(hat,inverse,gain,grad),jnp.sum(grad*hat,axis=0),jnp.sum(grad,axis=0)

def low(tensor):
    return tensor.astype(jnp.bfloat16)

def columns(tensor):
    return jnp.sum(tensor.astype(jnp.float32),axis=0)

def gather_all(shards):
    return [lax.all_gather(s,AXES,axis=0,tiled=True) for s in shards]

def reduce_all(partials):
    return [lax.psum_scatter(p,AXES,scatter_dimension=0,tiled=True).astype(jnp.float32) for p in partials]

def gather_vectors(vectors,wide):
    rows=jnp.stack([jnp.pad(v,(0,128-v.shape[0])) for v in list(vectors)+[wide]])
    rows=jnp.pad(rows,((0,15-len(vectors)),(0,0)))
    whole=lax.all_gather(rows,AXES).astype(jnp.float32)
    return whole[:,:,:vectors[0].shape[0]].transpose(1,0,2).reshape(16,-1),whole[:,len(vectors),:wide.shape[0]].reshape(1,-1)

def pack_grads(vectors,wide,devices):
    each=1024//devices
    flat=jnp.stack(vectors).reshape(len(vectors),devices,each).transpose(1,0,2).reshape(devices,-1)
    flat=jnp.concatenate([flat,wide.reshape(devices,4*each)],1)
    return jnp.pad(flat,((0,0),(0,1024-flat.shape[1]))).reshape(devices*8,128)

def shards(devices, depth, unit_states, dec_states, enc_states, unit_len, text_len, task_flag, cotangent,
    ln1_gain, ln1_shift, self_wq, self_bq, self_wk, self_wv, self_bv, self_wo, self_bo,
    ln2_gain, ln2_shift, cross_wq, cross_bq, cross_wk, cross_wv, cross_bv, cross_wo, cross_bo,
    ln3_gain, ln3_shift, ffn_w1, ffn_b1, ffn_w2, ffn_b2):
    steps=8
    each=1024//devices
    if depth: ffn_w1=order_columns(ffn_w1,devices,steps)
    w1=lax.all_gather(ffn_w1,AXES,axis=0,tiled=True)
    w2=lax.all_gather(ffn_w2,AXES,axis=0,tiled=True)
    small=[ln1_gain,ln1_shift,self_bq,self_bv,self_bo,ln2_gain,ln2_shift,cross_bq,cross_bv,cross_bo,ln3_gain,ln3_shift,ffn_b2]
    late=[self_wo,cross_wq,cross_wk,cross_wv,cross_wo]
    if depth:
        part=4*each//steps
        wq,wk,wv,vectors,b1=gather_first([self_wq,self_wk,self_wv],small,ffn_b1,steps,depth,1)
    else:
        wq,wk,wv,*late=gather_all([self_wq,self_wk,self_wv]+late)
        vectors,b1=gather_vectors(small,ffn_b1)
    g1,s1,bq,bv,bo,g2,s2,cbq,cbv,cbo,g3,s3,b2=[vectors[i] for i in range(13)]
    units=unit_states[0].astype(jnp.float32)
    memory=jnp.where(task_flag[0]==1,dec_states[0],enc_states[0])
    n1=low(layer_norm(units,g1,s1))
    q=low(dot(n1,wq)+bq); k=low(dot(n1,wk)); v=low(dot(n1,wv)+bv)
    if depth: ctx,lse,late=flash_fwd(q,k,v,text_len,True,moves=late,depth=depth,collective_id=2)
    else: ctx,lse,_=flash_fwd(q,k,v,text_len,True)
    wo,cwq,cwk,cwv,cwo=late
    after_self=units+(dot(ctx,wo)+bo)
    n2=low(layer_norm(after_self,g2,s2))
    cq=low(dot(n2,cwq)+cbq); ck=low(dot(memory,cwk)); cv=low(dot(memory,cwv)+cbv)
    cctx,clse,_=flash_fwd(cq,ck,cv,text_len,False)
    after_cross=after_self+(dot(cctx,cwo)+cbo)
    last=jnp.concatenate([vectors[10:13],jnp.zeros((5,1024),jnp.float32)])
    if depth:
        mixed,g_cross,gc,g_cctx,dw1,dw2,db1,dvec,*before=feed_forward(after_cross,cotangent[0],unit_len,w1,w2.reshape(devices,4*each,1024),b1,last,cwo,depth=depth,collective_id=3)
        db1=db1.reshape(steps,devices,part).transpose(1,0,2)
    else:
        mixed,g_cross,gc,g_cctx,dw1,dw2,db1,dvec,*_=feed_forward(after_cross,cotangent[0],unit_len,w1,w2[None],b1,last,cwo)
        dw1,dw2=reduce_all([dw1,dw2[0]])
    gain1,gain2=vectors[0:1],vectors[5:6]
    if depth:
        g_self,gs,g_ctx,g_dec,g_enc,csums,*starts,left1,left2,dw1,dw2=sub_layer_back(
            cq,ck,cv,g_cctx,cctx,clse,text_len,task_flag,False,n2,memory,gc,gain2,[cwq,cwk,cwv,wo,after_self,g_cross],before,[dw1,dw2],depth,4)
        dw2=dw2.reshape(4*each,1024)
        g_units,sums,dwq,dwk,dwv,dwo,dcwq,dcwk,dcwv,dcwo=sub_layer_back(
            q,k,v,g_ctx,ctx,lse,text_len,task_flag,True,n1,memory,gs,gain1,[wq,wk,wv,unit_states[0],g_self],[left1,left2],starts,depth,5)
        small_grads=[sums[3],sums[4],sums[0],sums[1],sums[2],csums[3],csums[4],csums[0],csums[1],csums[2],dvec[0],dvec[1],dvec[2]]
    else:
        gcq,gck,gcv=flash_bwd(cq,ck,cv,g_cctx,cctx,clse,text_len,False)
        dcwq,dcwk,dcwv,dcwo=reduce_all([low(dot(n2,gcq,TN)),low(dot(memory,gck,TN)),low(dot(memory,gcv,TN)),low(dot(cctx,gc,TN))])
        g_memory=dot(gck,cwk,NT)+dot(gcv,cwv,NT)
        pulled,dg2,ds2=layer_norm_back(after_self,g2,dot(gcq,cwq,NT))
        g_self=g_cross+pulled
        gs=low(g_self)
        gq,gk,gv=flash_bwd(q,k,v,low(dot(gs,wo,NT)),ctx,lse,text_len,True)
        dwq,dwk,dwv,dwo=reduce_all([low(dot(n1,gq,TN)),low(dot(n1,gk,TN)),low(dot(n1,gv,TN)),low(dot(ctx,gs,TN))])
        pulled,dg1,ds1=layer_norm_back(units,g1,dot(gq,wq,NT)+dot(gk,wk,NT)+dot(gv,wv,NT))
        g_units=g_self+pulled
        is_dec=(task_flag[0]==1).astype(jnp.float32)
        g_dec,g_enc=g_memory*is_dec,g_memory*(1.0-is_dec)
        small_grads=[dg1,ds1,columns(gq),columns(gv),columns(gs),dg2,ds2,columns(gcq),columns(gcv),columns(gc),dvec[0],dvec[1],dvec[2]]
    grads=pack_grads(small_grads,db1,devices)
    grads,=reduce_rows([grads],depth,6) if depth else reduce_all([grads])
    grads=grads.reshape(1024)
    ng=[grads[i*each:(i+1)*each] for i in range(13)]
    db1=grads[13*each:17*each]
    if depth:
        dw1,mixed,g_units,g_dec,g_enc,dwq,dwk,dwv,dwo,dcwq,dcwk,dcwv,dcwo,dw2=deliver(
            [dw1,mixed,g_units,g_dec,g_enc,dwq,dwk,dwv,dwo,dcwq,dcwk,dcwv,dcwo,dw2],devices,steps)
    return (mixed[None],g_units[None],g_dec[None],g_enc[None],
        ng[0],ng[1],dwq,ng[2],dwk,dwv,ng[3],dwo,ng[4],ng[5],ng[6],dcwq,ng[7],dcwk,dcwv,ng[8],dcwo,ng[9],ng[10],ng[11],dw1,db1,dw2,ng[12])

def solution(mesh):
    devices=mesh.shape["dp"]*mesh.shape["fsdp"]
    depth=mesh.shape["fsdp"]//2 if mesh.shape["dp"]==4 and (1024//devices)%16==0 else 0
    cube,flat,row=P(AXES,None,None),P(AXES),P(AXES,None)
    return jax.shard_map(
        functools.partial(shards,devices,depth),
        mesh=mesh,
        in_specs=(cube,)*3+(flat,)*3+(cube,flat,flat,row,flat,row,row,flat,row,flat,flat,flat,row,flat,row,row,flat,row,flat,flat,flat,row,flat,row,flat),
        out_specs=(cube,)*4+(flat,flat,row,flat,row,row,flat,row,flat,flat,flat,row,flat,row,row,flat,row,flat,flat,flat,row,flat,row,flat),
        check_vma=False,
    )
```

```python
import functools

import jax
import jax.numpy as jnp
from jax import lax
from jax.experimental import pallas as pl
from jax.experimental.pallas import tpu as pltpu
from jax.sharding import PartitionSpec as P

MIB=1<<20

NEGATIVE=-1e30
NN=(((1,),(0,)),((),()))
NT=(((1,),(1,)),((),()))
TN=(((0,),(0,)),((),()))
def dot(a,b,dims=NN):
    return lax.dot_general(a,b,dims,preferred_element_type=jnp.float32)

def head_masks(width):
    lane=lax.broadcasted_iota(jnp.int32,(1,128),1)
    return [((lane//width)==h) for h in range(128//width)]

def run_beside(plan,depth):
    begin,ticks,finish=plan
    step=pl.program_id(0); steps=pl.num_programs(0)
    @pl.when(step==0)
    def _():
        greet(depth)
        begin()
    for n in range(7):
        @pl.when(step==n+1)
        def _():
            if n<len(ticks): ticks[n]()
    def after():
        @pl.when(step==steps-1)
        def _():
            for tick in ticks[7:]: tick()
            finish()
    return after

def fwd_kernel(causal, block, width, moved, depth, lim_ref, q_ref, k_ref, v_ref, *refs):
    ctx_ref,lse_ref=refs[moved:moved+2]
    if moved:
        after=run_beside(gather_plan(refs[:moved],refs[moved+2:2*moved+2],refs[2*moved+2:],depth),depth)
    rows=q_ref.shape[0]; keys=k_ref.shape[0]
    masks=head_masks(width)
    k=k_ref[...]
    v=v_ref[...]
    vm=[jnp.where(m,v,jnp.zeros_like(v)) for m in masks]
    for i in range(rows//block):
        kend=(i+1)*block if causal else keys
        q=q_ref[pl.ds(i*block,block),:]*jnp.bfloat16(width**-0.5)
        ctx=None
        for h,m in enumerate(masks):
            s=dot(jnp.where(m,q,jnp.zeros_like(q)),k[:kend],NT)
            if causal:
                tail=s[:,kend-block:]
                r=lax.broadcasted_iota(jnp.int32,tail.shape,0)
                c=lax.broadcasted_iota(jnp.int32,tail.shape,1)
                tail=jnp.where(c<=r,tail,NEGATIVE)
                s=tail if kend==block else jnp.concatenate([s[:,:kend-block],tail],1)
            else:
                c=lax.broadcasted_iota(jnp.int32,s.shape,1)
                s=jnp.where(c<lim_ref[0],s,NEGATIVE)
            top=jnp.max(s,axis=1,keepdims=True)
            p=jnp.exp(s-top)
            total=jnp.sum(p,axis=1,keepdims=True)
            part=dot(p.astype(jnp.bfloat16),vm[h][:kend])*(1.0/total)
            ctx=part if ctx is None else ctx+part
            lse=jnp.broadcast_to(top+jnp.log(total),(block,128))
            lse_ref[0,pl.ds(h,1),pl.ds(i*block,block)]=jnp.transpose(lse)[:1]
        ctx_ref[pl.ds(i*block,block),:]=ctx.astype(jnp.bfloat16)
    if moved: after()

def flash_fwd(q,k,v,limit,causal,block=256,width=64,moves=(),depth=0,collective_id=None):
    rows,d=q.shape; keys=k.shape[0]
    pairs=d//128
    per=128//width
    count=len(moves)
    any_=pl.BlockSpec(memory_space=pl.ANY)
    spec=lambda n: pl.BlockSpec((n,128),lambda i,lim:(0,i))
    outs=pl.pallas_call(
        functools.partial(fwd_kernel,causal,block,width,count,depth),
        grid_spec=pltpu.PrefetchScalarGridSpec(
            num_scalar_prefetch=1, grid=(pairs,),
            in_specs=[spec(rows),spec(keys),spec(keys)]+[any_]*count,
            out_specs=[spec(rows),pl.BlockSpec((1,per,rows),lambda i,lim:(i,0,0))]+[any_]*count,
            scratch_shapes=gather_sems(count,depth) if count else []),
        out_shape=[jax.ShapeDtypeStruct((rows,d),jnp.bfloat16),jax.ShapeDtypeStruct((pairs,per,rows),jnp.float32)]+gather_shapes(moves,depth),
        compiler_params=pltpu.CompilerParams(vmem_limit_bytes=48*MIB,collective_id=collective_id,has_side_effects=count>0),
        cost_estimate=pl.CostEstimate(flops=4*rows*keys*d//(2 if causal else 1),bytes_accessed=4*rows*d*2,transcendentals=rows*keys*16//(2 if causal else 1)),
        name="attend_causal" if causal else "attend_text",
    )(limit,q,k,v,*moves)
    return outs[0],outs[1],gather_result(outs[2:],moves)

def back_of_pair(causal, block, width, lim_ref, q_ref, k_ref, v_ref, g_ref, ctx_ref, lse_ref, dq_ref, dk_acc, dv_acc, middle=None):
    rows=q_ref.shape[0]; keys=k_ref.shape[0]
    masks=head_masks(width)
    scale=jnp.bfloat16(width**-0.5)
    k=k_ref[...]; v=v_ref[...]
    km=[jnp.where(m,k*scale,jnp.zeros_like(k)) for m in masks]
    dk_acc[...]=jnp.zeros_like(dk_acc); dv_acc[...]=jnp.zeros_like(dv_acc)
    for i in range(rows//block):
        kend=(i+1)*block if causal else keys
        sl=pl.ds(i*block,block)
        q=q_ref[sl,:]*scale
        g=g_ref[sl,:]
        prod=g.astype(jnp.float32)*ctx_ref[sl,:].astype(jnp.float32)
        dq=None
        for h,m in enumerate(masks):
            qm=jnp.where(m,q,jnp.zeros_like(q))
            gm=jnp.where(m,g,jnp.zeros_like(g))
            delta=jnp.sum(jnp.where(m,prod,0.0),axis=1,keepdims=True)
            delta=jnp.transpose(jnp.broadcast_to(delta,(block,128)))[:1]
            lse=lse_ref[0,pl.ds(h,1),sl]
            s=dot(k[:kend],qm,NT)
            if causal:
                tail=s[kend-block:]
                r=lax.broadcasted_iota(jnp.int32,tail.shape,0)
                c=lax.broadcasted_iota(jnp.int32,tail.shape,1)
                tail=jnp.where(r<=c,tail,NEGATIVE)
                s=tail if kend==block else jnp.concatenate([s[:kend-block],tail],0)
            else:
                r=lax.broadcasted_iota(jnp.int32,s.shape,0)
                s=jnp.where(r<lim_ref[0],s,NEGATIVE)
            p=jnp.exp(s-lse)
            dp=dot(v[:kend],gm,NT)
            ds=(p*(dp-delta)).astype(jnp.bfloat16)
            dk_acc[:kend,:]+=dot(ds,qm)
            dv_acc[:kend,:]+=dot(p.astype(jnp.bfloat16),gm)
            part=dot(ds,km[h][:kend],TN)
            dq=part if dq is None else dq+part
        dq_ref[sl,:]=dq.astype(jnp.bfloat16)
        if middle and i==rows//block//2: middle()

def bwd_kernel(causal, block, width, lim_ref, *refs):
    dq_ref,dk_ref,dv_ref,dk_acc,dv_acc=refs[6:]
    back_of_pair(causal,block,width,lim_ref,*refs[:6],dq_ref,dk_acc,dv_acc)
    dk_ref[...]=dk_acc[...].astype(jnp.bfloat16)
    dv_ref[...]=dv_acc[...].astype(jnp.bfloat16)

def flash_bwd(q,k,v,g,ctx,lse,limit,causal,block=256,width=64):
    rows,d=q.shape; keys=k.shape[0]
    pairs=d//128; per=128//width
    spec=lambda n: pl.BlockSpec((n,128),lambda i,lim:(0,i))
    return pl.pallas_call(
        functools.partial(bwd_kernel,causal,block,width),
        grid_spec=pltpu.PrefetchScalarGridSpec(
            num_scalar_prefetch=1,grid=(pairs,),
            in_specs=[spec(rows),spec(keys),spec(keys),spec(rows),spec(rows),pl.BlockSpec((1,per,rows),lambda i,lim:(i,0,0))],
            out_specs=[spec(rows),spec(keys),spec(keys)],
            scratch_shapes=[pltpu.VMEM((keys,128),jnp.float32)]*2),
        out_shape=[jax.ShapeDtypeStruct((n,d),jnp.bfloat16) for n in (rows,keys,keys)],
        compiler_params=pltpu.CompilerParams(vmem_limit_bytes=60*MIB),
        name="attend_causal_back" if causal else "attend_text_back",
    )(limit,q,k,v,g,ctx,lse)

def sub_layer_kernel(causal, block, width, pairs, depth, lim_ref, flag_ref, *refs):
    pair_refs=refs[:6]; refs=refs[6:]
    normed_ref,source_ref,whole_ref,out_ref,gain_ref=refs[:5]; refs=refs[5:]
    late_count=5 if causal else 6
    late_in=refs[:late_count]; refs=refs[late_count:]
    carried=4 if causal else 2
    before,starts=refs[:2],refs[2:2+carried]; refs=refs[2+carried:]
    if causal: cross_sums,last_sums,wide=refs[:3]; refs=refs[3:]
    if causal: grad_out,sums_ref=refs[:2]; refs=refs[2:]
    else: grad_out,low_out,ctx_out,dec_ref,enc_ref,sums_ref=refs[:6]; refs=refs[6:]
    results=refs[:4]; refs=refs[4:]
    left=(None,None)
    if not causal: left=refs[:2]; refs=refs[2:]
    ends=refs[:carried]; refs=refs[carried:]
    if causal: small_out=refs[0]; refs=refs[1:]
    late=refs[:late_count]; late_sem=refs[late_count]; refs=refs[late_count+1:]
    normed_t,source_t,whole_t,dq_all,dk_all,dv_all,dk_acc,dv_acc,out_part=refs[:9]; refs=refs[9:]
    low_all,ctx_all=(None,None) if causal else refs[:2]
    streams=refs if causal else refs[2:]
    half=STREAM
    earlier=streams[2*half:]; streams=streams[:2*half]
    if causal: table,packed=earlier[-14:-12]; vector_scratch=earlier[-12:]; earlier=earlier[:-14]
    count=pairs if causal else pairs-CROSS_LATE
    before_late=CROSS_LATE if causal else FFN_LATE
    step=pl.program_id(0)
    rows=pair_refs[0].shape[0]
    def keep_pair(first):
        def store(i,total):
            for n in range(2):
                results[first+n][:,pl.ds(pl.multiple_of(i*128,128),128)]=total[:,n*128:(n+1)*128]
        return store
    tick1,middle1=stream_plan(count,0,keep_pair(0),streams[:half],depth)
    tick2,middle2=stream_plan(count,1,keep_pair(2),streams[half:],depth)
    def store_earlier(w,total):
        if causal:
            at=pairs-before_late+w//2
            for n in range(2): ends[w%2*2+n][:,at*128:(at+1)*128]=total[:,n*128:(n+1)*128]
        elif w%2==0:
            wide=total.shape[1]
            at=ends[0].shape[1]//wide-before_late+w//2
            ends[0][:,at*wide:(at+1)*wide]=total
        else:
            ends[1][ends[1].shape[0]-before_late+w//2]=total
    begin,ticks,finish=(lambda: None),[],(lambda: None)
    if before_late: begin,ticks,finish=reduce_plan([before[w%2].at[w//2] for w in range(2*before_late)],store_earlier,earlier,depth)
    def leave(n):
        m=(pairs-CROSS_LATE+n)%2
        return [pltpu.make_async_copy(streams[half*h].at[m],left[h].at[n],late_sem.at[late_count+2*n+h]) for h in (0,1)]
    def late_copy(n): return pltpu.make_async_copy(late_in[n],late[n],late_sem.at[n])
    @pl.when(step==0)
    def _():
        greet(depth)
        begin()
        for n in range(late_count): late_copy(n).start()
        for a,b in zip(starts,ends): b[...]=a[...]
        normed_t[...]=jnp.transpose(normed_ref[...])
        whole_t[...]=jnp.transpose(whole_ref[...])
        if not causal: source_t[...]=jnp.transpose(source_ref[...])
    tick1(step); tick2(step)
    for n in range(len(ticks)):
        @pl.when(step==n+1)
        def _(): ticks[n]()
    here=pl.ds(pl.multiple_of(step*128,128),128)
    back_of_pair(causal,block,width,lim_ref,*pair_refs,dq_all.at[:,here],dk_acc,dv_acc,lambda: (middle1(step),middle2(step)))
    dq=dq_all[:,here]; dk=dk_acc[...].astype(jnp.bfloat16); dv=dv_acc[...].astype(jnp.bfloat16)
    dk_all[:,here]=dk; dv_all[:,here]=dv
    def add_sum(n,value): sums_ref[n:n+1,here]=jnp.sum(value.astype(jnp.float32),axis=0,keepdims=True)
    add_sum(0,dq); add_sum(1,dv)
    @pl.when(step%2==0)
    def _():
        out_part[...]=dot(whole_t[...],out_ref[...]).astype(jnp.bfloat16)
        add_sum(2,out_ref[:,:128])
        write_made(streams[half],step,128,out_part[:,:128])
    @pl.when(step%2==1)
    def _():
        add_sum(2,out_ref[:,128:])
        write_made(streams[half],step,128,out_part[:,128:])
    if causal:
        write_made(streams[0],step,0,dot(normed_t[...],jnp.concatenate([dq,dk],1)).astype(jnp.bfloat16))
        write_made(streams[half],step,0,dot(normed_t[...],dv).astype(jnp.bfloat16))
    else:
        both=dot(source_t[...],jnp.concatenate([dk,dv],1)).astype(jnp.bfloat16)
        write_made(streams[0],step,0,dot(normed_t[...],dq).astype(jnp.bfloat16))
        write_made(streams[0],step,128,both[:,:128])
        write_made(streams[half],step,0,both[:,128:])
        for n in range(CROSS_LATE):
            @pl.when(step==pairs-CROSS_LATE+n)
            def _():
                for copy in leave(n): copy.start()
    @pl.when(step==pairs-1)
    def _():
        for n in range(late_count): late_copy(n).wait()
        gain=gain_ref[0:1,:]
        sums_ref[3:8,:]=jnp.zeros((5,sums_ref.shape[1]),jnp.float32)
        strip=256
        for r in range(rows//strip):
            tick1(pairs+r); tick2(pairs+r)
            sl=pl.ds(r*strip,strip)
            if causal:
                wq,wk,wv,residual,total=late
                grad=dot(dq_all[sl,:],wq[...],NT)+dot(dk_all[sl,:],wk[...],NT)+dot(dv_all[sl,:],wv[...],NT)
            else:
                wq,wk,wv,wo,residual,total=late
                grad=dot(dq_all[sl,:],wq[...],NT)
            hat,inverse=normal(residual[sl,:].astype(jnp.float32))
            sums_ref[3:4,:]+=jnp.sum(grad*hat,axis=0,keepdims=True)
            sums_ref[4:5,:]+=jnp.sum(grad,axis=0,keepdims=True)
            whole=total[sl,:]+pull_norm(hat,inverse,gain,grad)
            total[sl,:]=whole
            middle1(pairs+r); middle2(pairs+r)
            if not causal:
                low_all[sl,:]=whole.astype(jnp.bfloat16)
                ctx_all[sl,:]=dot(low_all[sl,:],wo[...],NT).astype(jnp.bfloat16)
        copies=[pltpu.make_async_copy(late[-1],grad_out,late_sem.at[0])]
        if not causal:
            copies+=[pltpu.make_async_copy(low_all,low_out,late_sem.at[1]),pltpu.make_async_copy(ctx_all,ctx_out,late_sem.at[2])]
        for copy in copies: copy.start()
        if causal:
            for n,(ref,row) in enumerate([(sums_ref,r) for r in (3,4,0,1,2)]+[(cross_sums,r) for r in (3,4,0,1,2)]+[(last_sums,r) for r in (0,1,2)]):
                table[n:n+1,:]=ref[row:row+1,:]
            table[13:,:]=jnp.zeros((3,table.shape[1]),jnp.float32)
            each=results[0].shape[0]
            for n in range(8*depth):
                at=n*each//128*128
                turn=-n*each%128
                tile=table[:,at:at+128]
                dest=packed.at[n//(4*depth),n//(2*depth)%2,n//2%depth,n%2]
                dest[...]=pltpu.roll(tile,turn,1) if turn else tile
            def write_wide(n,value): packed.at[n//(4*depth),n//(2*depth)%2,n//2%depth,n%2][13:14,:]=value
            shuffle(lambda t: wide[:,t*128:(t+1)*128],write_wide,pairs,8*depth,128//pairs)
            def store_small(w,total): small_out[...]=total
            small_begin,small_ticks,small_finish=reduce_plan([packed],store_small,vector_scratch,depth)
            small_begin()
        for t in range(pairs+rows//strip,count+LAST_LAG): tick1(t); tick2(t); middle1(t); middle2(t)
        finish()
        if causal:
            for small_tick in small_ticks: small_tick()
            small_finish()
        if not causal:
            memory_grad=dot(dk_all[...],late[1][...],NT)+dot(dv_all[...],late[2][...],NT)
            flag=jnp.where(flag_ref[0]==1,1.0,0.0)
            dec_ref[...]=memory_grad*flag
            enc_ref[...]=memory_grad*(1.0-flag)
            for n in range(CROSS_LATE): copies+=leave(n)
        for copy in copies: copy.wait()

def sub_layer_back(q,k,v,g,ctx,lse,limit,flag,causal,normed,source,out_grad,gain,late,before,starts,small,depth,collective_id,block=256,width=64):
    rows,d=q.shape; keys=k.shape[0]
    pairs=d//128; per=128//width
    each=d//(8*depth)
    bf=jnp.bfloat16; f32=jnp.float32
    spec=lambda n: pl.BlockSpec((n,128),lambda i,a,b:(0,i))
    once=lambda shape: pl.BlockSpec(shape,lambda i,a,b:(0,0),pipeline_mode=pl.Buffered(1))
    keep=lambda shape: pl.BlockSpec(shape,lambda i,a,b:(0,0))
    any_=pl.BlockSpec(memory_space=pl.ANY)
    shape=lambda n,t: jax.ShapeDtypeStruct((n,d),t)
    in_specs=[spec(rows),spec(keys),spec(keys),spec(rows),spec(rows),pl.BlockSpec((1,per,rows),lambda i,a,b:(i,0,0))]
    in_specs+=[once((rows,d)),once(source.shape),once((rows,d)),pl.BlockSpec((rows,256),lambda i,a,b:(0,i//2)),once(gain.shape)]+[any_]*(len(late)+2)
    in_specs+=[pl.BlockSpec(a.shape,lambda i,a,b,n=a.ndim:(0,)*n,pipeline_mode=pl.Buffered(1)) for a in starts]
    in_specs+=[once(a.shape) for a in small]
    out_specs=[any_]; out_shape=[shape(rows,f32)]
    scratch=[pltpu.VMEM(a.shape,a.dtype) for a in late]+[DMA((len(late)+2*CROSS_LATE,))]
    scratch+=[pltpu.VMEM((d,rows),bf),pltpu.VMEM((8,128) if causal else (d,keys),bf),pltpu.VMEM((d,rows),bf)]
    scratch+=[pltpu.VMEM((n,d),bf) for n in (rows,keys,keys)]+[pltpu.VMEM((keys,128),f32)]*2+[pltpu.VMEM((d,256),bf)]
    if not causal:
        out_specs+=[any_,any_,keep((keys,d)),keep((keys,d))]
        out_shape+=[shape(rows,bf),shape(rows,bf),shape(keys,f32),shape(keys,f32)]
        scratch+=[pltpu.VMEM((rows,d),bf)]*2
    out_specs+=[keep((8,d))]+[keep((each,d))]*4
    out_shape+=[shape(8,f32)]+[shape(each,f32)]*4
    if not causal:
        out_specs+=[any_]*2
        out_shape+=[jax.ShapeDtypeStruct((max(CROSS_LATE,1),2,2,depth,2,each,256),bf)]*2
    out_specs+=[pl.BlockSpec(a.shape,lambda i,a,b,n=a.ndim:(0,)*n) for a in starts]
    out_shape+=[jax.ShapeDtypeStruct(a.shape,a.dtype) for a in starts]
    if causal:
        out_specs+=[keep((16,128))]
        out_shape+=[jax.ShapeDtypeStruct((16,128),f32)]
    scratch+=stream_scratch(each,256,depth)*2
    before_late=CROSS_LATE if causal else FFN_LATE
    if before_late: scratch+=reduce_scratch([before[w%2].shape[5:]+(bf,) for w in range(2*before_late)],depth)
    if causal: scratch+=[pltpu.VMEM((16,d),f32),pltpu.VMEM((2,2,depth,2,16,128),f32)]+reduce_scratch([(16,128,f32)],depth)
    return pl.pallas_call(
        functools.partial(sub_layer_kernel,causal,block,width,pairs,depth),
        grid_spec=pltpu.PrefetchScalarGridSpec(num_scalar_prefetch=2,grid=(pairs,),in_specs=in_specs,out_specs=out_specs,scratch_shapes=scratch),
        out_shape=out_shape,
        compiler_params=pltpu.CompilerParams(vmem_limit_bytes=62*MIB,collective_id=collective_id,has_side_effects=True),
        cost_estimate=pl.CostEstimate(flops=20*rows*keys*d,bytes_accessed=20*rows*d*2,transcendentals=rows*keys*16),
        name="self_back" if causal else "cross_back",
    )(limit,flag,q,k,v,g,ctx,lse,normed,source,ctx,out_grad,gain,*late,*before,*starts,*small)

MESH=pl.DeviceIdType.MESH
DMA=pltpu.SemaphoreType.DMA

def place():
    dp=lax.axis_index("dp"); fs=lax.axis_index("fsdp")
    return dp,fs,fs//2,fs%2

def turned(index,bit):
    return index+bit-2*bit*((index//bit)%2)

def greet(depth):
    dp,fs,z,c=place()
    partners=[(dp,lax.rem(z+k,depth)*2+c) for k in range(1,depth)]+[(turned(dp,1),fs),(turned(dp,2),fs),(dp,z*2+1-c)]
    barrier=pltpu.get_barrier_semaphore()
    for device in partners:
        pl.semaphore_signal(barrier,inc=1,device_id=device,device_id_type=MESH)
    pl.semaphore_wait(barrier,len(partners))

PIECES=2
AHEAD=2

def gather_sems(count,depth):
    count=PIECES*count
    return [DMA((count,)),DMA((count,depth-1)),DMA((count,depth-1)),DMA((count,3)),DMA((count,3)),DMA((count,4)),DMA((count,4))]

def gather_plan(ins,outs,sems,depth):
    parts=[]
    for a,b in zip(ins,outs):
        wide=a.shape[1]//PIECES
        if wide%128: parts+=[(a,b)]
        else: parts+=[(a.at[:,n*wide:(n+1)*wide],b.at[:,:,:,:,n*wide:(n+1)*wide]) for n in range(PIECES)]
    ins,outs=[p[0] for p in parts],[p[1] for p in parts]
    count=len(ins)
    local,z_send,z_recv,a_send,a_recv,c_send,c_recv=sems
    dp,fs,z,c=place()
    def line(w,k):
        return pltpu.make_async_remote_copy(ins[w],outs[w].at[dp,z,c],z_send.at[w,k-1],z_recv.at[w,k-1],(dp,lax.rem(z+k,depth)*2+c),MESH)
    def across(w,n,src_dp,bit):
        ref=outs[w].at[src_dp,:,c]
        return pltpu.make_async_remote_copy(ref,ref,a_send.at[w,n],a_recv.at[w,n],(turned(dp,bit),fs),MESH)
    def core(w,n,src_dp):
        ref=outs[w].at[src_dp,:,c]
        return pltpu.make_async_remote_copy(ref,ref,c_send.at[w,n],c_recv.at[w,n],(dp,z*2+1-c),MESH)
    def own(w):
        return pltpu.make_async_copy(ins[w],outs[w].at[dp,z,c],local.at[w])
    def bits(w):
        return 1+w%2,2-w%2
    def step0(w):
        f,g=bits(w)
        own(w).wait()
        for k in range(1,depth): line(w,k).wait_recv()
        across(w,0,dp,f).start()
        across(w,1,dp,g).start()
        core(w,0,dp).start()
    def step1(w):
        f,g=bits(w)
        across(w,0,dp,f).wait_recv()
        across(w,2,turned(dp,f),g).start()
        core(w,1,turned(dp,f)).start()
    def step2(w):
        f,g=bits(w)
        across(w,1,dp,g).wait_recv()
        core(w,2,turned(dp,g)).start()
    def step3(w):
        f,g=bits(w)
        across(w,2,turned(dp,f),g).wait_recv()
        core(w,3,turned(turned(dp,f),g)).start()
    def along(t):
        for w in (2*t,2*t+1):
            if w<count:
                own(w).start()
                for k in range(1,depth): line(w,k).start()
    def begin():
        for t in range(AHEAD): along(t)
    def tick(t):
        along(t+AHEAD)
        for n,step in enumerate((step0,step1,step2,step3)):
            for w in (2*(t-n),2*(t-n)+1):
                if 0<=w<count: step(w)
    def finish():
        for w in range(count):
            f,g=bits(w)
            for k in range(1,depth): line(w,k).wait_send()
            across(w,0,dp,f).wait_send(); across(w,1,dp,g).wait_send(); across(w,2,dp,g).wait_send()
            for n in range(4): core(w,n,dp).wait()
    return begin,[functools.partial(tick,t) for t in range((count+1)//2+3)],finish

def reduce_scratch(kinds,depth):
    count=len(kinds)
    vmem=lambda *lead: [pltpu.VMEM(lead+(r,n),d) for r,n,d in kinds]
    return (vmem(2,2,depth)+vmem(2,2,depth)+vmem(2,depth)+vmem(depth)+vmem(depth-1)
      +[DMA((count,)),DMA((count,)),DMA((count,)),DMA((count,2)),DMA((count,2)),DMA((count,depth-1)),DMA((count,depth-1))])

def reduce_plan(ins,store,scratch,depth):
    count=len(ins)
    held,r0,r1,r2,r3=(scratch[n*count:(n+1)*count] for n in range(5))
    local,c_send,c_recv,a_send,a_recv,z_send,z_recv=scratch[5*count:]
    dp,fs,z,c=place()
    hi,lo=dp//2,dp%2
    def own(w):
        return pltpu.make_async_copy(ins[w].at[:,:,:,c],held[w],local.at[w])
    def core(w):
        return pltpu.make_async_remote_copy(ins[w].at[:,:,:,1-c],r0[w],c_send.at[w],c_recv.at[w],(dp,z*2+1-c),MESH)
    def first(w):
        if w%2: return pltpu.make_async_remote_copy(held[w].at[1-hi],r1[w],a_send.at[w,0],a_recv.at[w,0],(turned(dp,2),fs),MESH)
        return pltpu.make_async_remote_copy(held[w].at[:,1-lo],r1[w],a_send.at[w,0],a_recv.at[w,0],(turned(dp,1),fs),MESH)
    def second(w):
        if w%2: return pltpu.make_async_remote_copy(held[w].at[hi,1-lo],r2[w],a_send.at[w,1],a_recv.at[w,1],(turned(dp,1),fs),MESH)
        return pltpu.make_async_remote_copy(held[w].at[1-hi,lo],r2[w],a_send.at[w,1],a_recv.at[w,1],(turned(dp,2),fs),MESH)
    def line(w,k):
        return pltpu.make_async_remote_copy(held[w].at[hi,lo,lax.rem(z+k,depth)],r3[w].at[k-1],z_send.at[w,k-1],z_recv.at[w,k-1],(dp,lax.rem(z+k,depth)*2+c),MESH)
    def step0(w):
        own(w).wait(); core(w).wait_recv()
        for i in range(4): held[w][i//2,i%2]=held[w][i//2,i%2]+r0[w][i//2,i%2]
        first(w).start()
    def step1(w):
        first(w).wait_recv()
        for i in range(2):
            if w%2: held[w][hi,i]=held[w][hi,i]+r1[w][i]
            else: held[w][i,lo]=held[w][i,lo]+r1[w][i]
        second(w).start()
    def step2(w):
        second(w).wait_recv()
        held[w][hi,lo]=held[w][hi,lo]+r2[w][...]
        for k in range(1,depth): line(w,k).start()
    def step3(w):
        total=held[w][hi,lo,z].astype(jnp.float32)
        for k in range(1,depth):
            line(w,k).wait_recv()
            total=total+r3[w][k-1].astype(jnp.float32)
        store(w,total)
    def begin():
        for w in range(count):
            core(w).start(); own(w).start()
    def tick(t):
        for n,step in enumerate((step0,step1,step2,step3)):
            if 0<=t-n<count: step(t-n)
    def finish():
        for w in range(count):
            core(w).wait_send(); first(w).wait_send(); second(w).wait_send()
            for k in range(1,depth): line(w,k).wait_send()
    return begin,[functools.partial(tick,t) for t in range(count+3)],finish

def gather_shapes(shards,depth):
    return [jax.ShapeDtypeStruct((4,depth,2)+s.shape,s.dtype) for s in shards]

def gather_result(outs,shards):
    return [o.reshape((-1,)+s.shape[1:]) for o,s in zip(outs,shards)]

def reduce_parts(partials,depth):
    return [p.reshape((2,2,depth,2,p.shape[0]//(8*depth),p.shape[1])) for p in partials]

def shuffle(read,write,outer,inner,part):
    each=128//part
    for t in range(outer*inner//each):
        whole=None
        for u in range(each):
            b,a=divmod(t*each+u,outer)
            tile,at=divmod(a*inner+b,each)
            piece=read(tile)
            if u!=at: piece=pltpu.roll(piece,(u-at)*part%128,1)
            lane=lax.broadcasted_iota(jnp.int32,piece.shape,1)
            whole=piece if whole is None else jnp.where(lane>=u*part,piece,whole)
        write(t,whole)

def first_kernel(count,lines,depth,blocks,*refs):
    ins,vectors,wide=refs[:count],refs[count:count+lines],refs[count+lines]
    refs=refs[count+lines+1:]
    outs,table,long=refs[:count],refs[count],refs[count+1]
    packed,every=refs[count+2:count+4]
    part=128//blocks
    each=vectors[0].shape[1]
    greet(depth)
    packed[...]=jnp.zeros_like(packed)
    for n in range(lines): packed[n:n+1,:each]=vectors[n][...].astype(jnp.float32)
    packed[lines:lines+1,:]=wide[...].astype(jnp.float32)
    begin,ticks,finish=gather_plan([packed]+list(ins),[every]+list(outs),refs[count+4:],depth)
    begin()
    for tick in ticks: tick()
    finish()
    lane=lax.broadcasted_iota(jnp.int32,(16,128),1)
    group=128//each
    def device(n): return every[n//(2*depth),(n//2)%depth,n%2]
    for m in range(8*depth//group):
        tile=device(m*group)
        for r in range(1,group):
            tile=jnp.where(lane>=r*each,pltpu.roll(device(m*group+r),r*each,1),tile)
        table[:,m*128:(m+1)*128]=tile
    def write_long(t,value): long[:,t*128:(t+1)*128]=value
    shuffle(lambda n: device(n)[lines:lines+1],write_long,8*depth,blocks,part)

def gather_first(shards,vectors,wide,blocks,depth,collective_id):
    count=len(shards); lines=len(vectors)
    any_=pl.BlockSpec(memory_space=pl.ANY); vm=pl.BlockSpec(memory_space=pltpu.VMEM)
    total=vectors[0].shape[0]*8*depth
    outs=pl.pallas_call(
        functools.partial(first_kernel,count,lines,depth,blocks),
        in_specs=[any_]*count+[vm]*(lines+1),
        out_specs=[any_]*count+[vm]*2,
        out_shape=gather_shapes(shards,depth)+[jax.ShapeDtypeStruct((16,total),jnp.float32),jax.ShapeDtypeStruct((1,128*8*depth),jnp.float32)],
        scratch_shapes=[pltpu.VMEM((16,128),jnp.float32),pltpu.VMEM((4,depth,2,16,128),jnp.float32)]+gather_sems(count+1,depth),
        compiler_params=pltpu.CompilerParams(collective_id=collective_id,has_side_effects=True),
        name="gather_first",
    )(*shards,*[v[None] for v in vectors],wide[None])
    return gather_result(outs[:count],shards)+list(outs[count:])

def last_kernel(count,depth,*refs):
    ins,outs,scratch=refs[:count],refs[count:2*count],refs[2*count:]
    greet(depth)
    def store(w,total): outs[w][...]=total
    begin,ticks,finish=reduce_plan(ins,store,scratch,depth)
    begin()
    for tick in ticks: tick()
    finish()

def reduce_rows(partials,depth,collective_id):
    count=len(partials)
    parts=reduce_parts(partials,depth)
    kinds=[p.shape[4:]+(p.dtype,) for p in parts]
    return pl.pallas_call(
        functools.partial(last_kernel,count,depth),
        in_specs=[pl.BlockSpec(memory_space=pl.ANY)]*count,
        out_specs=[pl.BlockSpec(memory_space=pltpu.VMEM)]*count,
        out_shape=[jax.ShapeDtypeStruct(k[:2],jnp.float32) for k in kinds],
        scratch_shapes=reduce_scratch(kinds,depth),
        compiler_params=pltpu.CompilerParams(collective_id=collective_id,has_side_effects=True,vmem_limit_bytes=60*MIB),
        name="reduce_rows",
    )(*parts)

SLOTS=4
STREAM=14
LAST_LAG=5

def stream_scratch(rows,cols,depth):
    vmem=lambda *lead: pltpu.VMEM(lead+(rows,cols),jnp.bfloat16)
    return [vmem(2,2,2,depth,2),vmem(2,2,2,depth),vmem(2,2,2,depth),vmem(SLOTS,2,depth),vmem(SLOTS,2,depth),vmem(SLOTS,depth),vmem(SLOTS,depth),vmem(SLOTS,depth-1),
      DMA((SLOTS,)),DMA((SLOTS,)),DMA((SLOTS,2)),DMA((SLOTS,2)),DMA((SLOTS,depth-1)),DMA((SLOTS,depth-1))]

def stream_plan(count,odd,store,scratch,depth):
    made,r0,sum0,r1,sum1,r2,sum2,r3,c_send,c_recv,a_send,a_recv,z_send,z_recv=scratch
    dp,fs,z,c=place()
    hi,lo=dp//2,dp%2
    here,there=(hi,1-hi) if odd else (lo,1-lo)
    here2,there2=(lo,1-lo) if odd else (hi,1-hi)
    def slot(i): return lax.rem(i,SLOTS)
    def core(i):
        s=slot(i)
        return pltpu.make_async_remote_copy(made.at[lax.rem(i,2),:,:,:,1-c],r0.at[lax.rem(i,2)],c_send.at[s],c_recv.at[s],(dp,z*2+1-c),MESH)
    def first(i):
        s=slot(i)
        m=lax.rem(i,2)
        src=sum0.at[m,there] if odd else sum0.at[m,:,there]
        return pltpu.make_async_remote_copy(src,r1.at[s],a_send.at[s,0],a_recv.at[s,0],(turned(dp,2 if odd else 1),fs),MESH)
    def second(i):
        s=slot(i)
        return pltpu.make_async_remote_copy(sum1.at[s,there2],r2.at[s],a_send.at[s,1],a_recv.at[s,1],(turned(dp,1 if odd else 2),fs),MESH)
    def line(i,k):
        s=slot(i)
        return pltpu.make_async_remote_copy(sum2.at[s,lax.rem(z+k,depth)],r3.at[s,k-1],z_send.at[s,k-1],z_recv.at[s,k-1],(dp,lax.rem(z+k,depth)*2+c),MESH)
    def step0(i):
        m=lax.rem(i,2)
        core(i).wait()
        for a in range(4):
            sum0[m,a//2,a%2]=made[m,a//2,a%2,:,c]+r0[m,a//2,a%2]
        first(i).start()
    def step1(i):
        s=slot(i); m=lax.rem(i,2)
        first(i).wait()
        for a in range(2):
            sum1[s,a]=(sum0[m,here,a] if odd else sum0[m,a,here])+r1[s,a]
        second(i).start()
    def step2(i):
        s=slot(i)
        second(i).wait()
        sum2[s]=sum1[s,here2]+r2[s]
        for k in range(1,depth): line(i,k).start()
    def step3(i):
        s=slot(i)
        total=sum2[s,z].astype(jnp.float32)
        for k in range(1,depth):
            line(i,k).wait()
            total=total+r3[s,k-1].astype(jnp.float32)
        store(i,total)
    def run(j,stages):
        for lag,step in stages:
            if isinstance(j,int):
                if 0<=j-lag<count: step(jnp.int32(j-lag))
            else:
                @pl.when((j>=lag)&(j<lag+count))
                def _(): step(j-lag)
    def tick(j):
        run(j,((5,step3),(4,step2),(3,step1),(1,lambda i: core(i).start())))
    def middle(j):
        run(j,((1,step0),))
    return tick,middle

def write_made(made,i,col,value):
    shape=made.shape[1:6]+value.shape[1:]
    made[lax.rem(i,2),:,:,:,:,:,col:col+value.shape[1]]=value.reshape(shape)


def deliver_kernel(count,devices,blocks,*refs):
    ins,outs,held,(here,there)=refs[:count],refs[count:2*count],refs[2*count:3*count-1],refs[3*count-1:]
    come=[pltpu.make_async_copy(ins[n],held[n-1],here.at[n]) for n in range(1,count)]
    go=[pltpu.make_async_copy(held[n-1],outs[n],there.at[n]) for n in range(1,count)]
    for copy in come: copy.start()
    def read(t): return ins[0][:,t*128:(t+1)*128]
    def write(t,value): outs[0][:,t*128:(t+1)*128]=value
    shuffle(read,write,blocks,devices,128//blocks)
    for a,b in zip(come,go):
        a.wait()
        b.start()
    for copy in go: copy.wait()

def deliver(arrays,devices,blocks):
    count=len(arrays)
    any_=pl.BlockSpec(memory_space=pl.ANY); vm=pl.BlockSpec(memory_space=pltpu.VMEM)
    return pl.pallas_call(
        functools.partial(deliver_kernel,count,devices,blocks),
        in_specs=[vm]+[any_]*(count-1),
        out_specs=[vm]+[any_]*(count-1),
        out_shape=[jax.ShapeDtypeStruct(a.shape,a.dtype) for a in arrays],
        scratch_shapes=[pltpu.VMEM(a.shape,a.dtype) for a in arrays[1:]]+[DMA((count,)),DMA((count,))],
        compiler_params=pltpu.CompilerParams(vmem_limit_bytes=62*MIB),
        name="deliver",
    )(*arrays)

def order_kernel(blocks,outer,shard,out):
    def read(t): return shard[:,t*128:(t+1)*128].astype(jnp.float32)
    def write(t,value): out[:,t*128:(t+1)*128]=value.astype(jnp.bfloat16)
    shuffle(read,write,outer,blocks,128//blocks)

def order_columns(shard,outer,blocks):
    return pl.pallas_call(
        functools.partial(order_kernel,blocks,outer),
        out_shape=jax.ShapeDtypeStruct(shard.shape,shard.dtype),
        name="order_columns",
    )(shard)

EPSILON=1e-05
def normal(tensor):
    centre=tensor-jnp.mean(tensor,axis=-1,keepdims=True)
    spread=jnp.mean(centre*centre,axis=-1,keepdims=True)
    inverse=lax.rsqrt(spread+EPSILON)
    return centre*inverse,inverse

def pull_norm(hat,inverse,gain,grad):
    scaled=grad*gain
    return inverse*(scaled-jnp.mean(scaled,axis=-1,keepdims=True)-hat*jnp.mean(scaled*hat,axis=-1,keepdims=True))

FFN_LATE=0
CROSS_LATE=0

def ffn_kernel(strip, steps, depth, length_ref, n3, n3t, gf, after_in, cot_in, w1_ref, w2_ref, b1_ref, vec_ref, wo_ref,
               mixed_ref, grad_ref, low_ref, ctx_ref, dw1_ref, dw2_ref, db1_ref, dvec_ref, late1_ref, late2_ref, mixed, ctx, after_ref, cot_ref, branch, gn, wo, sem, *refs):
    j=pl.program_id(0)
    rows,d=after_ref.shape
    gain,b2=vec_ref[0:1,:],vec_ref[2:3,:]
    def live(r):
        return (r*strip+lax.broadcasted_iota(jnp.int32,(strip,1),0)<length_ref[0]).astype(jnp.float32)
    if depth:
        half=len(refs)//2
        wide=w1_ref.shape[1]
        def store1(i,total): dw1_ref[:,pl.ds(pl.multiple_of(i*wide,128),wide)]=total
        def store2(i,total): dw2_ref[i]=total
        tick1,middle1=stream_plan(steps-FFN_LATE,0,store1,refs[:half],depth)
        tick2,middle2=stream_plan(steps-FFN_LATE,1,store2,refs[half:],depth)
        def leave(n):
            m=(steps-FFN_LATE+n)%2
            return [pltpu.make_async_copy(refs[0].at[m],late1_ref.at[n],sem.at[4+2*n]),pltpu.make_async_copy(refs[half].at[m],late2_ref.at[n],sem.at[5+2*n])]
    @pl.when(j==0)
    def _():
        if depth: greet(depth)
        pltpu.make_async_copy(wo_ref,wo,sem.at[2]).start()
        pltpu.make_async_copy(after_in,after_ref,sem.at[0]).start()
        pltpu.make_async_copy(cot_in,cot_ref,sem.at[1]).start()
        dvec_ref[...]=jnp.zeros_like(dvec_ref)
        dvec_ref[2:3,:]=jnp.sum(gf[...].astype(jnp.float32),axis=0,keepdims=True)
        branch[...]=jnp.zeros_like(branch); gn[...]=jnp.zeros_like(gn)
    if depth:
        tick1(j); tick2(j)
    w1=w1_ref[...]; w2=w2_ref[...].reshape(w1.shape[1],d)
    pre=dot(n3[...],w1)+b1_ref[...]
    back=dot(gf[...],w2,NT).astype(jnp.bfloat16).astype(jnp.float32)
    if depth:
        middle1(j); middle2(j)
    root=0.7978845608028654
    square=pre*pre
    t=jnp.tanh(root*pre*(1.0+0.044715*square))
    half_t=0.5*(1.0+t)
    hidden=(pre*half_t).astype(jnp.bfloat16)
    slope=half_t+0.5*pre*(1.0-t*t)*(root*(1.0+3*0.044715*square))
    g_pre=(back*slope).astype(jnp.bfloat16)
    db1_ref[...]=jnp.sum(g_pre.astype(jnp.float32),axis=0,keepdims=True)
    branch[...]+=dot(hidden,w2)
    dw2=dot(hidden,gf[...],TN).astype(jnp.bfloat16)
    dw1=dot(n3t[...],g_pre).astype(jnp.bfloat16)
    if depth:
        write_made(refs[0],j,0,dw1)
        write_made(refs[half],j,0,dw2)
        for n in range(FFN_LATE):
            @pl.when(j==steps-FFN_LATE+n)
            def _():
                for copy in leave(n): copy.start()
    else:
        dw1_ref[...]=dw1
        dw2_ref[...]=dw2.reshape(dw2_ref.shape)
    gn[...]+=dot(g_pre,w1,NT)
    @pl.when(j==steps-1)
    def _():
        def one(r):
            sl=pl.ds(r*strip,strip)
            valid=live(r)
            after=after_ref[sl,:]
            mixed[sl,:]=((after+(branch[sl,:]+b2))*valid).astype(jnp.bfloat16)
            hat,inverse=normal(after)
            grad=gn[sl,:]
            dvec_ref[0:1,:]+=jnp.sum(grad*hat,axis=0,keepdims=True)
            dvec_ref[1:2,:]+=jnp.sum(grad,axis=0,keepdims=True)
            grad=cot_ref[sl,:].astype(jnp.float32)*valid+pull_norm(hat,inverse,gain,grad)
            gn[sl,:]=grad
            cot_ref[sl,:]=grad.astype(jnp.bfloat16)
            ctx[sl,:]=dot(cot_ref[sl,:],wo[...],NT).astype(jnp.bfloat16)
        pltpu.make_async_copy(wo_ref,wo,sem.at[2]).wait()
        pltpu.make_async_copy(after_in,after_ref,sem.at[0]).wait()
        pltpu.make_async_copy(cot_in,cot_ref,sem.at[1]).wait()
        for r in range(rows//strip):
            if depth and r%2==0:
                tick1(steps+r//2); tick2(steps+r//2)
            one(r)
            if depth and r%2==0:
                middle1(steps+r//2); middle2(steps+r//2)
        copies=[pltpu.make_async_copy(a,b,sem.at[n]) for n,(a,b) in enumerate(((mixed,mixed_ref),(gn,grad_ref),(cot_ref,low_ref),(ctx,ctx_ref)))]
        for copy in copies: copy.start()
        if depth:
            for t in range(steps+rows//strip//2,steps-FFN_LATE+LAST_LAG):
                tick1(t); tick2(t); middle1(t); middle2(t)
            for n in range(FFN_LATE): copies+=leave(n)
        for copy in copies: copy.wait()

def feed_forward(ready,after,cot,length,w1,w2,b1,vec,wo,block=512,strip=128,depth=0,collective_id=None):
    rows,d=after.shape; ff=w1.shape[1]
    steps=ff//block
    once=lambda shape: pl.BlockSpec(shape,lambda j,n:(0,0),pipeline_mode=pl.Buffered(1))
    keep=lambda shape: pl.BlockSpec(shape,lambda j,n:(0,)*len(shape))
    any_=pl.BlockSpec(memory_space=pl.ANY)
    wide=pl.BlockSpec((d,block),lambda j,n:(0,j)); line=pl.BlockSpec((1,block),lambda j,n:(0,j))
    tall=pl.BlockSpec((w2.shape[0],block//w2.shape[0],d),lambda j,n:(0,j,0))
    bf=jnp.bfloat16; f32=jnp.float32
    scratch=[pltpu.VMEM((rows,d),bf),pltpu.VMEM((rows,d),bf),pltpu.VMEM((rows,d),f32),pltpu.VMEM((rows,d),bf),pltpu.VMEM((rows,d),f32),pltpu.VMEM((rows,d),f32),pltpu.VMEM((d,d),bf),DMA((4+2*FFN_LATE,))]
    if depth:
        each=d//(8*depth); part=block//(8*depth)
        grad_specs=[keep((each,ff)),keep((steps,part,d))]
        grad_shapes=[jax.ShapeDtypeStruct((each,ff),f32),jax.ShapeDtypeStruct((steps,part,d),f32)]
        late_shapes=[jax.ShapeDtypeStruct((max(FFN_LATE,1),2,2,depth,2,each,block),bf),jax.ShapeDtypeStruct((max(FFN_LATE,1),2,2,depth,2,part,d),bf)]
        scratch+=stream_scratch(each,block,depth)+stream_scratch(part,d,depth)
    else:
        grad_specs=[wide,tall]
        grad_shapes=[jax.ShapeDtypeStruct(w1.shape,bf),jax.ShapeDtypeStruct(w2.shape,bf)]
        late_shapes=[jax.ShapeDtypeStruct((8,128),bf)]*2
    return pl.pallas_call(
        functools.partial(ffn_kernel,strip,steps,depth),
        grid_spec=pltpu.PrefetchScalarGridSpec(
            num_scalar_prefetch=1,grid=(steps,),
            in_specs=[once((rows,d)),once((d,rows)),once((rows,d)),any_,any_,wide,tall,line,once(vec.shape),any_],
            out_specs=[any_]*4+grad_specs+[line,keep((8,d)),any_,any_],
            scratch_shapes=scratch),
        out_shape=[jax.ShapeDtypeStruct((rows,d),bf),jax.ShapeDtypeStruct((rows,d),f32)]+[jax.ShapeDtypeStruct((rows,d),bf)]*2+grad_shapes+[jax.ShapeDtypeStruct((1,ff),f32),jax.ShapeDtypeStruct((8,d),f32)]+late_shapes,
        compiler_params=pltpu.CompilerParams(vmem_limit_bytes=62*MIB,collective_id=collective_id,has_side_effects=depth>0),
        cost_estimate=pl.CostEstimate(flops=12*rows*d*ff,bytes_accessed=4*d*ff*2+rows*d*12,transcendentals=rows*ff),
        name="feed_forward",
    )(length,*ready,after,cot,w1,w2,b1,vec,wo)

AXES=("dp","fsdp")

def layer_norm(tensor, gain, shift):
    return normal(tensor)[0]*gain+shift

def layer_norm_back(tensor, gain, grad):
    hat,inverse=normal(tensor)
    return pull_norm(hat,inverse,gain,grad),jnp.sum(grad*hat,axis=0),jnp.sum(grad,axis=0)

def low(tensor):
    return tensor.astype(jnp.bfloat16)

def columns(tensor):
    return jnp.sum(tensor.astype(jnp.float32),axis=0)

def gather_all(shards):
    return [lax.all_gather(s,AXES,axis=0,tiled=True) for s in shards]

def reduce_all(partials):
    return [lax.psum_scatter(p,AXES,scatter_dimension=0,tiled=True).astype(jnp.float32) for p in partials]

def gather_vectors(vectors,wide):
    rows=jnp.stack([jnp.pad(v,(0,128-v.shape[0])) for v in list(vectors)+[wide]])
    rows=jnp.pad(rows,((0,15-len(vectors)),(0,0)))
    whole=lax.all_gather(rows,AXES).astype(jnp.float32)
    return whole[:,:,:vectors[0].shape[0]].transpose(1,0,2).reshape(16,-1),whole[:,len(vectors),:wide.shape[0]].reshape(1,-1)

def pack_grads(vectors,wide,devices):
    each=1024//devices
    flat=jnp.stack(vectors).reshape(len(vectors),devices,each).transpose(1,0,2).reshape(devices,-1)
    flat=jnp.concatenate([flat,wide.reshape(devices,4*each)],1)
    return jnp.pad(flat,((0,0),(0,1024-flat.shape[1]))).reshape(devices*8,128)

def shards(devices, depth, unit_states, dec_states, enc_states, unit_len, text_len, task_flag, cotangent,
    ln1_gain, ln1_shift, self_wq, self_bq, self_wk, self_wv, self_bv, self_wo, self_bo,
    ln2_gain, ln2_shift, cross_wq, cross_bq, cross_wk, cross_wv, cross_bv, cross_wo, cross_bo,
    ln3_gain, ln3_shift, ffn_w1, ffn_b1, ffn_w2, ffn_b2):
    steps=8
    each=1024//devices
    if depth: ffn_w1=order_columns(ffn_w1,devices,steps)
    w1=lax.all_gather(ffn_w1,AXES,axis=0,tiled=True)
    w2=lax.all_gather(ffn_w2,AXES,axis=0,tiled=True)
    small=[ln1_gain,ln1_shift,self_bq,self_bv,self_bo,ln2_gain,ln2_shift,cross_bq,cross_bv,cross_bo,ln3_gain,ln3_shift,ffn_b2]
    late=[self_wo,cross_wq,cross_wk,cross_wv,cross_wo]
    if depth:
        part=4*each//steps
        wq,wk,wv,vectors,b1=gather_first([self_wq,self_wk,self_wv],small,ffn_b1,steps,depth,1)
    else:
        wq,wk,wv,*late=gather_all([self_wq,self_wk,self_wv]+late)
        vectors,b1=gather_vectors(small,ffn_b1)
    g1,s1,bq,bv,bo,g2,s2,cbq,cbv,cbo,g3,s3,b2=[vectors[i] for i in range(13)]
    units=unit_states[0].astype(jnp.float32)
    memory=jnp.where(task_flag[0]==1,dec_states[0],enc_states[0])
    n1=low(layer_norm(units,g1,s1))
    q=low(dot(n1,wq)+bq); k=low(dot(n1,wk)); v=low(dot(n1,wv)+bv)
    if depth: ctx,lse,late=flash_fwd(q,k,v,text_len,True,moves=late,depth=depth,collective_id=2)
    else: ctx,lse,_=flash_fwd(q,k,v,text_len,True)
    wo,cwq,cwk,cwv,cwo=late
    after_self=units+(dot(ctx,wo)+bo)
    n2=low(layer_norm(after_self,g2,s2))
    cq=low(dot(n2,cwq)+cbq); ck=low(dot(memory,cwk)); cv=low(dot(memory,cwv)+cbv)
    cctx,clse,_=flash_fwd(cq,ck,cv,text_len,False)
    after_cross=after_self+(dot(cctx,cwo)+cbo)
    n3=low(layer_norm(after_cross,g3,s3))
    valid=(jnp.arange(units.shape[0],dtype=jnp.int32)<unit_len[0]).astype(jnp.float32)[:,None]
    gf=low(cotangent[0].astype(jnp.float32)*valid)
    ready=(n3,n3.T,gf)
    last=jnp.concatenate([vectors[10:13],jnp.zeros((5,1024),jnp.float32)])
    if depth:
        mixed,g_cross,gc,g_cctx,dw1,dw2,db1,dvec,*before=feed_forward(ready,after_cross,cotangent[0],unit_len,w1,w2.reshape(devices,4*each,1024),b1,last,cwo,depth=depth,collective_id=3)
    else:
        mixed,g_cross,gc,g_cctx,dw1,dw2,db1,dvec,*_=feed_forward(ready,after_cross,cotangent[0],unit_len,w1,w2[None],b1,last,cwo)
        dw1,dw2=reduce_all([dw1,dw2[0]])
    gain1,gain2=vectors[0:1],vectors[5:6]
    if depth:
        g_self,gs,g_ctx,g_dec,g_enc,csums,*starts,left1,left2,dw1,dw2=sub_layer_back(
            cq,ck,cv,g_cctx,cctx,clse,text_len,task_flag,False,n2,memory,gc,gain2,[cwq,cwk,cwv,wo,after_self,g_cross],before,[dw1,dw2],[],depth,4)
        dw2=dw2.reshape(4*each,1024)
        g_units,sums,dwq,dwk,dwv,dwo,dcwq,dcwk,dcwv,dcwo,grads=sub_layer_back(
            q,k,v,g_ctx,ctx,lse,text_len,task_flag,True,n1,memory,gs,gain1,[wq,wk,wv,unit_states[0],g_self],[left1,left2],starts,[csums,dvec,db1],depth,5)
        ng=[grads[i,:each] for i in range(13)]
        db1=grads[13]
    else:
        gcq,gck,gcv=flash_bwd(cq,ck,cv,g_cctx,cctx,clse,text_len,False)
        dcwq,dcwk,dcwv,dcwo=reduce_all([low(dot(n2,gcq,TN)),low(dot(memory,gck,TN)),low(dot(memory,gcv,TN)),low(dot(cctx,gc,TN))])
        g_memory=dot(gck,cwk,NT)+dot(gcv,cwv,NT)
        pulled,dg2,ds2=layer_norm_back(after_self,g2,dot(gcq,cwq,NT))
        g_self=g_cross+pulled
        gs=low(g_self)
        gq,gk,gv=flash_bwd(q,k,v,low(dot(gs,wo,NT)),ctx,lse,text_len,True)
        dwq,dwk,dwv,dwo=reduce_all([low(dot(n1,gq,TN)),low(dot(n1,gk,TN)),low(dot(n1,gv,TN)),low(dot(ctx,gs,TN))])
        pulled,dg1,ds1=layer_norm_back(units,g1,dot(gq,wq,NT)+dot(gk,wk,NT)+dot(gv,wv,NT))
        g_units=g_self+pulled
        is_dec=(task_flag[0]==1).astype(jnp.float32)
        g_dec,g_enc=g_memory*is_dec,g_memory*(1.0-is_dec)
        small_grads=[dg1,ds1,columns(gq),columns(gv),columns(gs),dg2,ds2,columns(gcq),columns(gcv),columns(gc),dvec[0],dvec[1],dvec[2]]
        grads,=reduce_all([pack_grads(small_grads,db1,devices)])
        grads=grads.reshape(1024)
        ng=[grads[i*each:(i+1)*each] for i in range(13)]
        db1=grads[13*each:17*each]
    if depth:
        dw1,mixed,g_units,g_dec,g_enc,dwq,dwk,dwv,dwo,dcwq,dcwk,dcwv,dcwo,dw2=deliver(
            [dw1,mixed,g_units,g_dec,g_enc,dwq,dwk,dwv,dwo,dcwq,dcwk,dcwv,dcwo,dw2],devices,steps)
    return (mixed[None],g_units[None],g_dec[None],g_enc[None],
        ng[0],ng[1],dwq,ng[2],dwk,dwv,ng[3],dwo,ng[4],ng[5],ng[6],dcwq,ng[7],dcwk,dcwv,ng[8],dcwo,ng[9],ng[10],ng[11],dw1,db1,dw2,ng[12])

def solution(mesh):
    devices=mesh.shape["dp"]*mesh.shape["fsdp"]
    depth=mesh.shape["fsdp"]//2 if mesh.shape["dp"]==4 and (1024//devices)%16==0 else 0
    cube,flat,row=P(AXES,None,None),P(AXES),P(AXES,None)
    return jax.shard_map(
        functools.partial(shards,devices,depth),
        mesh=mesh,
        in_specs=(cube,)*3+(flat,)*3+(cube,flat,flat,row,flat,row,row,flat,row,flat,flat,flat,row,flat,row,row,flat,row,flat,flat,flat,row,flat,row,flat),
        out_specs=(cube,)*4+(flat,flat,row,flat,row,row,flat,row,flat,flat,flat,row,flat,row,row,flat,row,flat,flat,flat,row,flat,row,flat),
        check_vma=False,
    )
```

```python
import functools

import jax
import jax.numpy as jnp
from jax import lax
from jax.experimental import pallas as pl
from jax.experimental.pallas import tpu as pltpu
from jax.sharding import PartitionSpec as P

MIB=1<<20

NEGATIVE=-1e30
NN=(((1,),(0,)),((),()))
NT=(((1,),(1,)),((),()))
TN=(((0,),(0,)),((),()))
def dot(a,b,dims=NN):
    return lax.dot_general(a,b,dims,preferred_element_type=jnp.float32)

def head_masks(width):
    lane=lax.broadcasted_iota(jnp.int32,(1,128),1)
    return [((lane//width)==h) for h in range(128//width)]

def run_beside(plan,depth):
    begin,ticks,finish=plan
    step=pl.program_id(0); steps=pl.num_programs(0)
    @pl.when(step==0)
    def _():
        greet(depth)
        begin()
    for n in range(7):
        @pl.when(step==n+1)
        def _():
            if n<len(ticks): ticks[n]()
    def after():
        @pl.when(step==steps-1)
        def _():
            for tick in ticks[7:]: tick()
            finish()
    return after

def fwd_kernel(causal, block, width, moved, depth, lim_ref, q_ref, k_ref, v_ref, *refs):
    ctx_ref,lse_ref=refs[moved:moved+2]
    if moved:
        after=run_beside(gather_plan(refs[:moved],refs[moved+2:2*moved+2],refs[2*moved+2:],depth),depth)
    rows=q_ref.shape[0]; keys=k_ref.shape[0]
    masks=head_masks(width)
    k=k_ref[...]
    v=v_ref[...]
    vm=[jnp.where(m,v,jnp.zeros_like(v)) for m in masks]
    for i in range(rows//block):
        kend=(i+1)*block if causal else keys
        q=q_ref[pl.ds(i*block,block),:]*jnp.bfloat16(width**-0.5)
        ctx=None
        for h,m in enumerate(masks):
            s=dot(jnp.where(m,q,jnp.zeros_like(q)),k[:kend],NT)
            if causal:
                tail=s[:,kend-block:]
                r=lax.broadcasted_iota(jnp.int32,tail.shape,0)
                c=lax.broadcasted_iota(jnp.int32,tail.shape,1)
                tail=jnp.where(c<=r,tail,NEGATIVE)
                s=tail if kend==block else jnp.concatenate([s[:,:kend-block],tail],1)
            else:
                c=lax.broadcasted_iota(jnp.int32,s.shape,1)
                s=jnp.where(c<lim_ref[0],s,NEGATIVE)
            top=jnp.max(s,axis=1,keepdims=True)
            p=jnp.exp(s-top)
            total=jnp.sum(p,axis=1,keepdims=True)
            part=dot(p.astype(jnp.bfloat16),vm[h][:kend])*(1.0/total)
            ctx=part if ctx is None else ctx+part
            lse=jnp.broadcast_to(top+jnp.log(total),(block,128))
            lse_ref[0,pl.ds(h,1),pl.ds(i*block,block)]=jnp.transpose(lse)[:1]
        ctx_ref[pl.ds(i*block,block),:]=ctx.astype(jnp.bfloat16)
    if moved: after()

def flash_fwd(q,k,v,limit,causal,block=256,width=64,moves=(),depth=0,collective_id=None):
    rows,d=q.shape; keys=k.shape[0]
    pairs=d//128
    per=128//width
    count=len(moves)
    any_=pl.BlockSpec(memory_space=pl.ANY)
    spec=lambda n: pl.BlockSpec((n,128),lambda i,lim:(0,i))
    outs=pl.pallas_call(
        functools.partial(fwd_kernel,causal,block,width,count,depth),
        grid_spec=pltpu.PrefetchScalarGridSpec(
            num_scalar_prefetch=1, grid=(pairs,),
            in_specs=[spec(rows),spec(keys),spec(keys)]+[any_]*count,
            out_specs=[spec(rows),pl.BlockSpec((1,per,rows),lambda i,lim:(i,0,0))]+[any_]*count,
            scratch_shapes=gather_sems(count,depth) if count else []),
        out_shape=[jax.ShapeDtypeStruct((rows,d),jnp.bfloat16),jax.ShapeDtypeStruct((pairs,per,rows),jnp.float32)]+gather_shapes(moves,depth),
        compiler_params=pltpu.CompilerParams(vmem_limit_bytes=48*MIB,collective_id=collective_id,has_side_effects=count>0),
        cost_estimate=pl.CostEstimate(flops=4*rows*keys*d//(2 if causal else 1),bytes_accessed=4*rows*d*2,transcendentals=rows*keys*16//(2 if causal else 1)),
        name="attend_causal" if causal else "attend_text",
    )(limit,q,k,v,*moves)
    return outs[0],outs[1],gather_result(outs[2:],moves)

def back_of_pair(causal, block, width, lim_ref, q_ref, k_ref, v_ref, g_ref, ctx_ref, lse_ref, dq_ref, dk_acc, dv_acc, middle=None):
    rows=q_ref.shape[0]; keys=k_ref.shape[0]
    masks=head_masks(width)
    scale=jnp.bfloat16(width**-0.5)
    k=k_ref[...]; v=v_ref[...]
    km=[jnp.where(m,k*scale,jnp.zeros_like(k)) for m in masks]
    dk_acc[...]=jnp.zeros_like(dk_acc); dv_acc[...]=jnp.zeros_like(dv_acc)
    for i in range(rows//block):
        kend=(i+1)*block if causal else keys
        sl=pl.ds(i*block,block)
        q=q_ref[sl,:]*scale
        g=g_ref[sl,:]
        prod=g.astype(jnp.float32)*ctx_ref[sl,:].astype(jnp.float32)
        dq=None
        for h,m in enumerate(masks):
            qm=jnp.where(m,q,jnp.zeros_like(q))
            gm=jnp.where(m,g,jnp.zeros_like(g))
            delta=jnp.sum(jnp.where(m,prod,0.0),axis=1,keepdims=True)
            delta=jnp.transpose(jnp.broadcast_to(delta,(block,128)))[:1]
            lse=lse_ref[0,pl.ds(h,1),sl]
            s=dot(k[:kend],qm,NT)
            if causal:
                tail=s[kend-block:]
                r=lax.broadcasted_iota(jnp.int32,tail.shape,0)
                c=lax.broadcasted_iota(jnp.int32,tail.shape,1)
                tail=jnp.where(r<=c,tail,NEGATIVE)
                s=tail if kend==block else jnp.concatenate([s[:kend-block],tail],0)
            else:
                r=lax.broadcasted_iota(jnp.int32,s.shape,0)
                s=jnp.where(r<lim_ref[0],s,NEGATIVE)
            p=jnp.exp(s-lse)
            dp=dot(v[:kend],gm,NT)
            ds=(p*(dp-delta)).astype(jnp.bfloat16)
            dk_acc[:kend,:]+=dot(ds,qm)
            dv_acc[:kend,:]+=dot(p.astype(jnp.bfloat16),gm)
            part=dot(ds,km[h][:kend],TN)
            dq=part if dq is None else dq+part
        dq_ref[sl,:]=dq.astype(jnp.bfloat16)
        if middle and i==rows//block//2: middle()

def bwd_kernel(causal, block, width, lim_ref, *refs):
    dq_ref,dk_ref,dv_ref,dk_acc,dv_acc=refs[6:]
    back_of_pair(causal,block,width,lim_ref,*refs[:6],dq_ref,dk_acc,dv_acc)
    dk_ref[...]=dk_acc[...].astype(jnp.bfloat16)
    dv_ref[...]=dv_acc[...].astype(jnp.bfloat16)

def flash_bwd(q,k,v,g,ctx,lse,limit,causal,block=256,width=64):
    rows,d=q.shape; keys=k.shape[0]
    pairs=d//128; per=128//width
    spec=lambda n: pl.BlockSpec((n,128),lambda i,lim:(0,i))
    return pl.pallas_call(
        functools.partial(bwd_kernel,causal,block,width),
        grid_spec=pltpu.PrefetchScalarGridSpec(
            num_scalar_prefetch=1,grid=(pairs,),
            in_specs=[spec(rows),spec(keys),spec(keys),spec(rows),spec(rows),pl.BlockSpec((1,per,rows),lambda i,lim:(i,0,0))],
            out_specs=[spec(rows),spec(keys),spec(keys)],
            scratch_shapes=[pltpu.VMEM((keys,128),jnp.float32)]*2),
        out_shape=[jax.ShapeDtypeStruct((n,d),jnp.bfloat16) for n in (rows,keys,keys)],
        compiler_params=pltpu.CompilerParams(vmem_limit_bytes=60*MIB),
        name="attend_causal_back" if causal else "attend_text_back",
    )(limit,q,k,v,g,ctx,lse)

def sub_layer_kernel(causal, block, width, pairs, depth, lim_ref, flag_ref, *refs):
    pair_refs=refs[:6]; refs=refs[6:]
    normed_ref,source_ref,whole_ref,out_ref,gain_ref=refs[:5]; refs=refs[5:]
    late_count=5 if causal else 6
    late_in=refs[:late_count]; refs=refs[late_count:]
    carried=4 if causal else 2
    before,starts=refs[:2],refs[2:2+carried]; refs=refs[2+carried:]
    if causal: cross_sums,last_sums,wide=refs[:3]; refs=refs[3:]
    if causal: grad_out,sums_ref=refs[:2]; refs=refs[2:]
    else: grad_out,low_out,ctx_out,dec_ref,enc_ref,sums_ref=refs[:6]; refs=refs[6:]
    results=refs[:4]; refs=refs[4:]
    left=(None,None)
    if not causal: left=refs[:2]; refs=refs[2:]
    ends=refs[:carried]; refs=refs[carried:]
    if causal: small_out=refs[0]; refs=refs[1:]
    late=refs[:late_count]; late_sem=refs[late_count]; refs=refs[late_count+1:]
    normed_t,source_t,whole_t,dq_all,dk_all,dv_all,dk_acc,dv_acc,out_part=refs[:9]; refs=refs[9:]
    low_all,ctx_all=(None,None) if causal else refs[:2]
    streams=refs if causal else refs[2:]
    half=STREAM
    earlier=streams[2*half:]; streams=streams[:2*half]
    if causal: table,packed=earlier[-14:-12]; vector_scratch=earlier[-12:]; earlier=earlier[:-14]
    count=pairs if causal else pairs-CROSS_LATE
    before_late=CROSS_LATE if causal else FFN_LATE
    step=pl.program_id(0)
    rows=pair_refs[0].shape[0]
    def keep_pair(first):
        def store(i,total):
            for n in range(2):
                results[first+n][:,pl.ds(pl.multiple_of(i*128,128),128)]=total[:,n*128:(n+1)*128]
        return store
    tick1,middle1=stream_plan(count,0,keep_pair(0),streams[:half],depth)
    tick2,middle2=stream_plan(count,1,keep_pair(2),streams[half:],depth)
    def store_earlier(w,total):
        if causal:
            at=pairs-before_late+w//2
            for n in range(2): ends[w%2*2+n][:,at*128:(at+1)*128]=total[:,n*128:(n+1)*128]
        elif w%2==0:
            wide=total.shape[1]
            at=ends[0].shape[1]//wide-before_late+w//2
            ends[0][:,at*wide:(at+1)*wide]=total
        else:
            ends[1][ends[1].shape[0]-before_late+w//2]=total
    begin,ticks,finish=(lambda: None),[],(lambda: None)
    if before_late: begin,ticks,finish=reduce_plan([before[w%2].at[w//2] for w in range(2*before_late)],store_earlier,earlier,depth)
    def leave(n):
        m=(pairs-CROSS_LATE+n)%2
        return [pltpu.make_async_copy(streams[half*h].at[m],left[h].at[n],late_sem.at[late_count+2*n+h]) for h in (0,1)]
    def late_copy(n): return pltpu.make_async_copy(late_in[n],late[n],late_sem.at[n])
    @pl.when(step==0)
    def _():
        greet(depth)
        begin()
        for n in range(late_count): late_copy(n).start()
        for a,b in zip(starts,ends): b[...]=a[...]
        normed_t[...]=jnp.transpose(normed_ref[...])
        whole_t[...]=jnp.transpose(whole_ref[...])
        if not causal: source_t[...]=jnp.transpose(source_ref[...])
    tick1(step); tick2(step)
    for n in range(len(ticks)):
        @pl.when(step==n+1)
        def _(): ticks[n]()
    here=pl.ds(pl.multiple_of(step*128,128),128)
    back_of_pair(causal,block,width,lim_ref,*pair_refs,dq_all.at[:,here],dk_acc,dv_acc,lambda: (middle1(step),middle2(step)))
    dq=dq_all[:,here]; dk=dk_acc[...].astype(jnp.bfloat16); dv=dv_acc[...].astype(jnp.bfloat16)
    dk_all[:,here]=dk; dv_all[:,here]=dv
    def add_sum(n,value): sums_ref[n:n+1,here]=jnp.sum(value.astype(jnp.float32),axis=0,keepdims=True)
    add_sum(0,dq); add_sum(1,dv)
    @pl.when(step%2==0)
    def _():
        out_part[...]=dot(whole_t[...],out_ref[...]).astype(jnp.bfloat16)
        add_sum(2,out_ref[:,:128])
        write_made(streams[half],step,128,out_part[:,:128])
    @pl.when(step%2==1)
    def _():
        add_sum(2,out_ref[:,128:])
        write_made(streams[half],step,128,out_part[:,128:])
    if causal:
        write_made(streams[0],step,0,dot(normed_t[...],jnp.concatenate([dq,dk],1)).astype(jnp.bfloat16))
        write_made(streams[half],step,0,dot(normed_t[...],dv).astype(jnp.bfloat16))
    else:
        both=dot(source_t[...],jnp.concatenate([dk,dv],1)).astype(jnp.bfloat16)
        write_made(streams[0],step,0,dot(normed_t[...],dq).astype(jnp.bfloat16))
        write_made(streams[0],step,128,both[:,:128])
        write_made(streams[half],step,0,both[:,128:])
        for n in range(CROSS_LATE):
            @pl.when(step==pairs-CROSS_LATE+n)
            def _():
                for copy in leave(n): copy.start()
    @pl.when(step==pairs-1)
    def _():
        for n in range(late_count): late_copy(n).wait()
        gain=gain_ref[0:1,:]
        sums_ref[3:8,:]=jnp.zeros((5,sums_ref.shape[1]),jnp.float32)
        strip=256
        for r in range(rows//strip):
            tick1(pairs+r); tick2(pairs+r)
            sl=pl.ds(r*strip,strip)
            if causal:
                wq,wk,wv,residual,total=late
                grad=dot(dq_all[sl,:],wq[...],NT)+dot(dk_all[sl,:],wk[...],NT)+dot(dv_all[sl,:],wv[...],NT)
            else:
                wq,wk,wv,wo,residual,total=late
                grad=dot(dq_all[sl,:],wq[...],NT)
            hat,inverse=normal(residual[sl,:].astype(jnp.float32))
            sums_ref[3:4,:]+=jnp.sum(grad*hat,axis=0,keepdims=True)
            sums_ref[4:5,:]+=jnp.sum(grad,axis=0,keepdims=True)
            whole=total[sl,:]+pull_norm(hat,inverse,gain,grad)
            total[sl,:]=whole
            middle1(pairs+r); middle2(pairs+r)
            if not causal:
                low_all[sl,:]=whole.astype(jnp.bfloat16)
                ctx_all[sl,:]=dot(low_all[sl,:],wo[...],NT).astype(jnp.bfloat16)
        copies=[pltpu.make_async_copy(late[-1],grad_out,late_sem.at[0])]
        if not causal:
            copies+=[pltpu.make_async_copy(low_all,low_out,late_sem.at[1]),pltpu.make_async_copy(ctx_all,ctx_out,late_sem.at[2])]
        for copy in copies: copy.start()
        if causal:
            for n,(ref,row) in enumerate([(sums_ref,r) for r in (3,4,0,1,2)]+[(cross_sums,r) for r in (3,4,0,1,2)]+[(last_sums,r) for r in (0,1,2)]):
                table[n:n+1,:]=ref[row:row+1,:]
            table[13:,:]=jnp.zeros((3,table.shape[1]),jnp.float32)
            each=results[0].shape[0]
            for n in range(8*depth):
                at=n*each//128*128
                turn=-n*each%128
                tile=table[:,at:at+128]
                dest=packed.at[n//(4*depth),n//(2*depth)%2,n//2%depth,n%2]
                dest[...]=pltpu.roll(tile,turn,1) if turn else tile
            def write_wide(n,value): packed.at[n//(4*depth),n//(2*depth)%2,n//2%depth,n%2][13:14,:]=value
            shuffle(lambda t: wide[:,t*128:(t+1)*128],write_wide,pairs,8*depth,128//pairs)
            def store_small(w,total): small_out[...]=total
            small_begin,small_ticks,small_finish=reduce_plan([packed],store_small,vector_scratch,depth)
            small_begin()
        for t in range(pairs+rows//strip,count+LAST_LAG): tick1(t); tick2(t); middle1(t); middle2(t)
        finish()
        if causal:
            for small_tick in small_ticks: small_tick()
            small_finish()
        if not causal:
            memory_grad=dot(dk_all[...],late[1][...],NT)+dot(dv_all[...],late[2][...],NT)
            flag=jnp.where(flag_ref[0]==1,1.0,0.0)
            dec_ref[...]=memory_grad*flag
            enc_ref[...]=memory_grad*(1.0-flag)
            for n in range(CROSS_LATE): copies+=leave(n)
        for copy in copies: copy.wait()

def sub_layer_back(q,k,v,g,ctx,lse,limit,flag,causal,normed,source,out_grad,gain,late,before,starts,small,depth,collective_id,block=256,width=64):
    rows,d=q.shape; keys=k.shape[0]
    pairs=d//128; per=128//width
    each=d//(8*depth)
    bf=jnp.bfloat16; f32=jnp.float32
    spec=lambda n: pl.BlockSpec((n,128),lambda i,a,b:(0,i))
    once=lambda shape: pl.BlockSpec(shape,lambda i,a,b:(0,0),pipeline_mode=pl.Buffered(1))
    keep=lambda shape: pl.BlockSpec(shape,lambda i,a,b:(0,0))
    any_=pl.BlockSpec(memory_space=pl.ANY)
    shape=lambda n,t: jax.ShapeDtypeStruct((n,d),t)
    in_specs=[spec(rows),spec(keys),spec(keys),spec(rows),spec(rows),pl.BlockSpec((1,per,rows),lambda i,a,b:(i,0,0))]
    in_specs+=[once((rows,d)),once(source.shape),once((rows,d)),pl.BlockSpec((rows,256),lambda i,a,b:(0,i//2)),once(gain.shape)]+[any_]*(len(late)+2)
    in_specs+=[pl.BlockSpec(a.shape,lambda i,a,b,n=a.ndim:(0,)*n,pipeline_mode=pl.Buffered(1)) for a in starts]
    in_specs+=[once(a.shape) for a in small]
    out_specs=[any_]; out_shape=[shape(rows,f32)]
    scratch=[pltpu.VMEM(a.shape,a.dtype) for a in late]+[DMA((len(late)+2*CROSS_LATE,))]
    scratch+=[pltpu.VMEM((d,rows),bf),pltpu.VMEM((8,128) if causal else (d,keys),bf),pltpu.VMEM((d,rows),bf)]
    scratch+=[pltpu.VMEM((n,d),bf) for n in (rows,keys,keys)]+[pltpu.VMEM((keys,128),f32)]*2+[pltpu.VMEM((d,256),bf)]
    if not causal:
        out_specs+=[any_,any_,keep((keys,d)),keep((keys,d))]
        out_shape+=[shape(rows,bf),shape(rows,bf),shape(keys,f32),shape(keys,f32)]
        scratch+=[pltpu.VMEM((rows,d),bf)]*2
    out_specs+=[keep((8,d))]+[keep((each,d))]*4
    out_shape+=[shape(8,f32)]+[shape(each,f32)]*4
    if not causal:
        out_specs+=[any_]*2
        out_shape+=[jax.ShapeDtypeStruct((max(CROSS_LATE,1),2,2,depth,2,each,256),bf)]*2
    out_specs+=[pl.BlockSpec(a.shape,lambda i,a,b,n=a.ndim:(0,)*n) for a in starts]
    out_shape+=[jax.ShapeDtypeStruct(a.shape,a.dtype) for a in starts]
    if causal:
        out_specs+=[keep((16,128))]
        out_shape+=[jax.ShapeDtypeStruct((16,128),f32)]
    scratch+=stream_scratch(each,256,depth)*2
    before_late=CROSS_LATE if causal else FFN_LATE
    if before_late: scratch+=reduce_scratch([before[w%2].shape[5:]+(bf,) for w in range(2*before_late)],depth)
    if causal: scratch+=[pltpu.VMEM((16,d),f32),pltpu.VMEM((2,2,depth,2,16,128),f32)]+reduce_scratch([(16,128,f32)],depth)
    return pl.pallas_call(
        functools.partial(sub_layer_kernel,causal,block,width,pairs,depth),
        grid_spec=pltpu.PrefetchScalarGridSpec(num_scalar_prefetch=2,grid=(pairs,),in_specs=in_specs,out_specs=out_specs,scratch_shapes=scratch),
        out_shape=out_shape,
        compiler_params=pltpu.CompilerParams(vmem_limit_bytes=62*MIB,collective_id=collective_id,has_side_effects=True),
        cost_estimate=pl.CostEstimate(flops=20*rows*keys*d,bytes_accessed=20*rows*d*2,transcendentals=rows*keys*16),
        name="self_back" if causal else "cross_back",
    )(limit,flag,q,k,v,g,ctx,lse,normed,source,ctx,out_grad,gain,*late,*before,*starts,*small)

MESH=pl.DeviceIdType.MESH
DMA=pltpu.SemaphoreType.DMA

def place():
    dp=lax.axis_index("dp"); fs=lax.axis_index("fsdp")
    return dp,fs,fs//2,fs%2

def turned(index,bit):
    return index+bit-2*bit*((index//bit)%2)

def greet(depth):
    dp,fs,z,c=place()
    partners=[(dp,lax.rem(z+k,depth)*2+c) for k in range(1,depth)]+[(turned(dp,1),fs),(turned(dp,2),fs),(dp,z*2+1-c)]
    barrier=pltpu.get_barrier_semaphore()
    for device in partners:
        pl.semaphore_signal(barrier,inc=1,device_id=device,device_id_type=MESH)
    pl.semaphore_wait(barrier,len(partners))

PIECES=4
AHEAD=1

def gather_sems(count,depth):
    count=PIECES*count
    return [DMA((count,)),DMA((count,depth-1)),DMA((count,depth-1)),DMA((count,3)),DMA((count,3)),DMA((count,4)),DMA((count,4))]

def gather_plan(ins,outs,sems,depth):
    parts=[]
    for a,b in zip(ins,outs):
        wide=a.shape[1]//PIECES
        if wide%128: parts+=[(a,b)]
        else: parts+=[(a.at[:,n*wide:(n+1)*wide],b.at[:,:,:,:,n*wide:(n+1)*wide]) for n in range(PIECES)]
    ins,outs=[p[0] for p in parts],[p[1] for p in parts]
    count=len(ins)
    local,z_send,z_recv,a_send,a_recv,c_send,c_recv=sems
    dp,fs,z,c=place()
    def line(w,k):
        return pltpu.make_async_remote_copy(ins[w],outs[w].at[dp,z,c],z_send.at[w,k-1],z_recv.at[w,k-1],(dp,lax.rem(z+k,depth)*2+c),MESH)
    def across(w,n,src_dp,bit):
        ref=outs[w].at[src_dp,:,c]
        return pltpu.make_async_remote_copy(ref,ref,a_send.at[w,n],a_recv.at[w,n],(turned(dp,bit),fs),MESH)
    def core(w,n,src_dp):
        ref=outs[w].at[src_dp,:,c]
        return pltpu.make_async_remote_copy(ref,ref,c_send.at[w,n],c_recv.at[w,n],(dp,z*2+1-c),MESH)
    def own(w):
        return pltpu.make_async_copy(ins[w],outs[w].at[dp,z,c],local.at[w])
    def bits(w):
        return 1+w%2,2-w%2
    def step0(w):
        f,g=bits(w)
        own(w).wait()
        for k in range(1,depth): line(w,k).wait_recv()
        across(w,0,dp,f).start()
        across(w,1,dp,g).start()
        core(w,0,dp).start()
    def step1(w):
        f,g=bits(w)
        across(w,0,dp,f).wait_recv()
        across(w,2,turned(dp,f),g).start()
        core(w,1,turned(dp,f)).start()
    def step2(w):
        f,g=bits(w)
        across(w,1,dp,g).wait_recv()
        core(w,2,turned(dp,g)).start()
    def step3(w):
        f,g=bits(w)
        across(w,2,turned(dp,f),g).wait_recv()
        core(w,3,turned(turned(dp,f),g)).start()
    def along(t):
        for w in (2*t,2*t+1):
            if w<count:
                own(w).start()
                for k in range(1,depth): line(w,k).start()
    def begin():
        for t in range(AHEAD): along(t)
    def tick(t):
        along(t+AHEAD)
        for n,step in enumerate((step0,step1,step2,step3)):
            for w in (2*(t-n),2*(t-n)+1):
                if 0<=w<count: step(w)
    def finish():
        for w in range(count):
            f,g=bits(w)
            for k in range(1,depth): line(w,k).wait_send()
            across(w,0,dp,f).wait_send(); across(w,1,dp,g).wait_send(); across(w,2,dp,g).wait_send()
            for n in range(4): core(w,n,dp).wait()
    return begin,[functools.partial(tick,t) for t in range((count+1)//2+3)],finish

def reduce_scratch(kinds,depth):
    count=len(kinds)
    vmem=lambda *lead: [pltpu.VMEM(lead+(r,n),d) for r,n,d in kinds]
    return (vmem(2,2,depth)+vmem(2,2,depth)+vmem(2,depth)+vmem(depth)+vmem(depth-1)
      +[DMA((count,)),DMA((count,)),DMA((count,)),DMA((count,2)),DMA((count,2)),DMA((count,depth-1)),DMA((count,depth-1))])

def reduce_plan(ins,store,scratch,depth):
    count=len(ins)
    held,r0,r1,r2,r3=(scratch[n*count:(n+1)*count] for n in range(5))
    local,c_send,c_recv,a_send,a_recv,z_send,z_recv=scratch[5*count:]
    dp,fs,z,c=place()
    hi,lo=dp//2,dp%2
    def own(w):
        return pltpu.make_async_copy(ins[w].at[:,:,:,c],held[w],local.at[w])
    def core(w):
        return pltpu.make_async_remote_copy(ins[w].at[:,:,:,1-c],r0[w],c_send.at[w],c_recv.at[w],(dp,z*2+1-c),MESH)
    def first(w):
        if w%2: return pltpu.make_async_remote_copy(held[w].at[1-hi],r1[w],a_send.at[w,0],a_recv.at[w,0],(turned(dp,2),fs),MESH)
        return pltpu.make_async_remote_copy(held[w].at[:,1-lo],r1[w],a_send.at[w,0],a_recv.at[w,0],(turned(dp,1),fs),MESH)
    def second(w):
        if w%2: return pltpu.make_async_remote_copy(held[w].at[hi,1-lo],r2[w],a_send.at[w,1],a_recv.at[w,1],(turned(dp,1),fs),MESH)
        return pltpu.make_async_remote_copy(held[w].at[1-hi,lo],r2[w],a_send.at[w,1],a_recv.at[w,1],(turned(dp,2),fs),MESH)
    def line(w,k):
        return pltpu.make_async_remote_copy(held[w].at[hi,lo,lax.rem(z+k,depth)],r3[w].at[k-1],z_send.at[w,k-1],z_recv.at[w,k-1],(dp,lax.rem(z+k,depth)*2+c),MESH)
    def step0(w):
        own(w).wait(); core(w).wait_recv()
        for i in range(4): held[w][i//2,i%2]=held[w][i//2,i%2]+r0[w][i//2,i%2]
        first(w).start()
    def step1(w):
        first(w).wait_recv()
        for i in range(2):
            if w%2: held[w][hi,i]=held[w][hi,i]+r1[w][i]
            else: held[w][i,lo]=held[w][i,lo]+r1[w][i]
        second(w).start()
    def step2(w):
        second(w).wait_recv()
        held[w][hi,lo]=held[w][hi,lo]+r2[w][...]
        for k in range(1,depth): line(w,k).start()
    def step3(w):
        total=held[w][hi,lo,z].astype(jnp.float32)
        for k in range(1,depth):
            line(w,k).wait_recv()
            total=total+r3[w][k-1].astype(jnp.float32)
        store(w,total)
    def begin():
        for w in range(count):
            core(w).start(); own(w).start()
    def tick(t):
        for n,step in enumerate((step0,step1,step2,step3)):
            if 0<=t-n<count: step(t-n)
    def finish():
        for w in range(count):
            core(w).wait_send(); first(w).wait_send(); second(w).wait_send()
            for k in range(1,depth): line(w,k).wait_send()
    return begin,[functools.partial(tick,t) for t in range(count+3)],finish

def gather_shapes(shards,depth):
    return [jax.ShapeDtypeStruct((4,depth,2)+s.shape,s.dtype) for s in shards]

def gather_result(outs,shards):
    return [o.reshape((-1,)+s.shape[1:]) for o,s in zip(outs,shards)]

def reduce_parts(partials,depth):
    return [p.reshape((2,2,depth,2,p.shape[0]//(8*depth),p.shape[1])) for p in partials]

def shuffle(read,write,outer,inner,part):
    each=128//part
    for t in range(outer*inner//each):
        whole=None
        for u in range(each):
            b,a=divmod(t*each+u,outer)
            tile,at=divmod(a*inner+b,each)
            piece=read(tile)
            if u!=at: piece=pltpu.roll(piece,(u-at)*part%128,1)
            lane=lax.broadcasted_iota(jnp.int32,piece.shape,1)
            whole=piece if whole is None else jnp.where(lane>=u*part,piece,whole)
        write(t,whole)

def first_kernel(count,lines,depth,blocks,*refs):
    ins,vectors,wide=refs[:count],refs[count:count+lines],refs[count+lines]
    refs=refs[count+lines+1:]
    outs,table,long=refs[:count],refs[count],refs[count+1]
    packed,every=refs[count+2:count+4]
    part=128//blocks
    each=vectors[0].shape[1]
    greet(depth)
    packed[...]=jnp.zeros_like(packed)
    for n in range(lines): packed[n:n+1,:each]=vectors[n][...].astype(jnp.float32)
    packed[lines:lines+1,:]=wide[...].astype(jnp.float32)
    begin,ticks,finish=gather_plan([packed]+list(ins),[every]+list(outs),refs[count+4:],depth)
    begin()
    for tick in ticks: tick()
    finish()
    lane=lax.broadcasted_iota(jnp.int32,(16,128),1)
    group=128//each
    def device(n): return every[n//(2*depth),(n//2)%depth,n%2]
    for m in range(8*depth//group):
        tile=device(m*group)
        for r in range(1,group):
            tile=jnp.where(lane>=r*each,pltpu.roll(device(m*group+r),r*each,1),tile)
        table[:,m*128:(m+1)*128]=tile
    def write_long(t,value): long[:,t*128:(t+1)*128]=value
    shuffle(lambda n: device(n)[lines:lines+1],write_long,8*depth,blocks,part)

def gather_first(shards,vectors,wide,blocks,depth,collective_id):
    count=len(shards); lines=len(vectors)
    any_=pl.BlockSpec(memory_space=pl.ANY); vm=pl.BlockSpec(memory_space=pltpu.VMEM)
    total=vectors[0].shape[0]*8*depth
    outs=pl.pallas_call(
        functools.partial(first_kernel,count,lines,depth,blocks),
        in_specs=[any_]*count+[vm]*(lines+1),
        out_specs=[any_]*count+[vm]*2,
        out_shape=gather_shapes(shards,depth)+[jax.ShapeDtypeStruct((16,total),jnp.float32),jax.ShapeDtypeStruct((1,128*8*depth),jnp.float32)],
        scratch_shapes=[pltpu.VMEM((16,128),jnp.float32),pltpu.VMEM((4,depth,2,16,128),jnp.float32)]+gather_sems(count+1,depth),
        compiler_params=pltpu.CompilerParams(collective_id=collective_id,has_side_effects=True),
        name="gather_first",
    )(*shards,*[v[None] for v in vectors],wide[None])
    return gather_result(outs[:count],shards)+list(outs[count:])

def last_kernel(count,depth,*refs):
    ins,outs,scratch=refs[:count],refs[count:2*count],refs[2*count:]
    greet(depth)
    def store(w,total): outs[w][...]=total
    begin,ticks,finish=reduce_plan(ins,store,scratch,depth)
    begin()
    for tick in ticks: tick()
    finish()

def reduce_rows(partials,depth,collective_id):
    count=len(partials)
    parts=reduce_parts(partials,depth)
    kinds=[p.shape[4:]+(p.dtype,) for p in parts]
    return pl.pallas_call(
        functools.partial(last_kernel,count,depth),
        in_specs=[pl.BlockSpec(memory_space=pl.ANY)]*count,
        out_specs=[pl.BlockSpec(memory_space=pltpu.VMEM)]*count,
        out_shape=[jax.ShapeDtypeStruct(k[:2],jnp.float32) for k in kinds],
        scratch_shapes=reduce_scratch(kinds,depth),
        compiler_params=pltpu.CompilerParams(collective_id=collective_id,has_side_effects=True,vmem_limit_bytes=60*MIB),
        name="reduce_rows",
    )(*parts)

SLOTS=4
STREAM=14
LAST_LAG=5

def stream_scratch(rows,cols,depth):
    vmem=lambda *lead: pltpu.VMEM(lead+(rows,cols),jnp.bfloat16)
    return [vmem(2,2,2,depth,2),vmem(2,2,2,depth),vmem(2,2,2,depth),vmem(SLOTS,2,depth),vmem(SLOTS,2,depth),vmem(SLOTS,depth),vmem(SLOTS,depth),vmem(SLOTS,depth-1),
      DMA((SLOTS,)),DMA((SLOTS,)),DMA((SLOTS,2)),DMA((SLOTS,2)),DMA((SLOTS,depth-1)),DMA((SLOTS,depth-1))]

def stream_plan(count,odd,store,scratch,depth):
    made,r0,sum0,r1,sum1,r2,sum2,r3,c_send,c_recv,a_send,a_recv,z_send,z_recv=scratch
    dp,fs,z,c=place()
    hi,lo=dp//2,dp%2
    here,there=(hi,1-hi) if odd else (lo,1-lo)
    here2,there2=(lo,1-lo) if odd else (hi,1-hi)
    def slot(i): return lax.rem(i,SLOTS)
    def core(i):
        s=slot(i)
        return pltpu.make_async_remote_copy(made.at[lax.rem(i,2),:,:,:,1-c],r0.at[lax.rem(i,2)],c_send.at[s],c_recv.at[s],(dp,z*2+1-c),MESH)
    def first(i):
        s=slot(i)
        m=lax.rem(i,2)
        src=sum0.at[m,there] if odd else sum0.at[m,:,there]
        return pltpu.make_async_remote_copy(src,r1.at[s],a_send.at[s,0],a_recv.at[s,0],(turned(dp,2 if odd else 1),fs),MESH)
    def second(i):
        s=slot(i)
        return pltpu.make_async_remote_copy(sum1.at[s,there2],r2.at[s],a_send.at[s,1],a_recv.at[s,1],(turned(dp,1 if odd else 2),fs),MESH)
    def line(i,k):
        s=slot(i)
        return pltpu.make_async_remote_copy(sum2.at[s,lax.rem(z+k,depth)],r3.at[s,k-1],z_send.at[s,k-1],z_recv.at[s,k-1],(dp,lax.rem(z+k,depth)*2+c),MESH)
    def step0(i):
        m=lax.rem(i,2)
        core(i).wait()
        for a in range(4):
            sum0[m,a//2,a%2]=made[m,a//2,a%2,:,c]+r0[m,a//2,a%2]
        first(i).start()
    def step1(i):
        s=slot(i); m=lax.rem(i,2)
        first(i).wait()
        for a in range(2):
            sum1[s,a]=(sum0[m,here,a] if odd else sum0[m,a,here])+r1[s,a]
        second(i).start()
    def step2(i):
        s=slot(i)
        second(i).wait()
        sum2[s]=sum1[s,here2]+r2[s]
        for k in range(1,depth): line(i,k).start()
    def step3(i):
        s=slot(i)
        total=sum2[s,z].astype(jnp.float32)
        for k in range(1,depth):
            line(i,k).wait()
            total=total+r3[s,k-1].astype(jnp.float32)
        store(i,total)
    def run(j,stages):
        for lag,step in stages:
            if isinstance(j,int):
                if 0<=j-lag<count: step(jnp.int32(j-lag))
            else:
                @pl.when((j>=lag)&(j<lag+count))
                def _(): step(j-lag)
    def tick(j):
        run(j,((5,step3),(4,step2),(3,step1),(1,lambda i: core(i).start())))
    def middle(j):
        run(j,((1,step0),))
    return tick,middle

def write_made(made,i,col,value):
    shape=made.shape[1:6]+value.shape[1:]
    made[lax.rem(i,2),:,:,:,:,:,col:col+value.shape[1]]=value.reshape(shape)


def deliver_kernel(count,devices,blocks,*refs):
    ins,outs,held,(here,there)=refs[:count],refs[count:2*count],refs[2*count:3*count-1],refs[3*count-1:]
    come=[pltpu.make_async_copy(ins[n],held[n-1],here.at[n]) for n in range(1,count)]
    go=[pltpu.make_async_copy(held[n-1],outs[n],there.at[n]) for n in range(1,count)]
    for copy in come: copy.start()
    def read(t): return ins[0][:,t*128:(t+1)*128]
    def write(t,value): outs[0][:,t*128:(t+1)*128]=value
    shuffle(read,write,blocks,devices,128//blocks)
    for a,b in zip(come,go):
        a.wait()
        b.start()
    for copy in go: copy.wait()

def deliver(arrays,devices,blocks):
    count=len(arrays)
    any_=pl.BlockSpec(memory_space=pl.ANY); vm=pl.BlockSpec(memory_space=pltpu.VMEM)
    return pl.pallas_call(
        functools.partial(deliver_kernel,count,devices,blocks),
        in_specs=[vm]+[any_]*(count-1),
        out_specs=[vm]+[any_]*(count-1),
        out_shape=[jax.ShapeDtypeStruct(a.shape,a.dtype) for a in arrays],
        scratch_shapes=[pltpu.VMEM(a.shape,a.dtype) for a in arrays[1:]]+[DMA((count,)),DMA((count,))],
        compiler_params=pltpu.CompilerParams(vmem_limit_bytes=62*MIB),
        name="deliver",
    )(*arrays)

def order_kernel(blocks,outer,shard,out):
    def read(t): return shard[:,t*128:(t+1)*128].astype(jnp.float32)
    def write(t,value): out[:,t*128:(t+1)*128]=value.astype(jnp.bfloat16)
    shuffle(read,write,outer,blocks,128//blocks)

def order_columns(shard,outer,blocks):
    return pl.pallas_call(
        functools.partial(order_kernel,blocks,outer),
        out_shape=jax.ShapeDtypeStruct(shard.shape,shard.dtype),
        name="order_columns",
    )(shard)

EPSILON=1e-05
def normal(tensor):
    centre=tensor-jnp.mean(tensor,axis=-1,keepdims=True)
    spread=jnp.mean(centre*centre,axis=-1,keepdims=True)
    inverse=lax.rsqrt(spread+EPSILON)
    return centre*inverse,inverse

def pull_norm(hat,inverse,gain,grad):
    scaled=grad*gain
    return inverse*(scaled-jnp.mean(scaled,axis=-1,keepdims=True)-hat*jnp.mean(scaled*hat,axis=-1,keepdims=True))

FFN_LATE=0
CROSS_LATE=0

def ffn_kernel(strip, steps, depth, length_ref, n3, n3t, gf, after_in, cot_in, w1_ref, w2_ref, b1_ref, vec_ref, wo_ref,
               mixed_ref, grad_ref, low_ref, ctx_ref, dw1_ref, dw2_ref, db1_ref, dvec_ref, late1_ref, late2_ref, mixed, ctx, after_ref, cot_ref, branch, gn, wo, sem, *refs):
    j=pl.program_id(0)
    rows,d=after_ref.shape
    gain,b2=vec_ref[0:1,:],vec_ref[2:3,:]
    def live(r):
        return (r*strip+lax.broadcasted_iota(jnp.int32,(strip,1),0)<length_ref[0]).astype(jnp.float32)
    if depth:
        half=len(refs)//2
        wide=w1_ref.shape[1]
        def store1(i,total): dw1_ref[:,pl.ds(pl.multiple_of(i*wide,128),wide)]=total
        def store2(i,total): dw2_ref[i]=total
        tick1,middle1=stream_plan(steps-FFN_LATE,0,store1,refs[:half],depth)
        tick2,middle2=stream_plan(steps-FFN_LATE,1,store2,refs[half:],depth)
        def leave(n):
            m=(steps-FFN_LATE+n)%2
            return [pltpu.make_async_copy(refs[0].at[m],late1_ref.at[n],sem.at[4+2*n]),pltpu.make_async_copy(refs[half].at[m],late2_ref.at[n],sem.at[5+2*n])]
    @pl.when(j==0)
    def _():
        if depth: greet(depth)
        pltpu.make_async_copy(wo_ref,wo,sem.at[2]).start()
        pltpu.make_async_copy(after_in,after_ref,sem.at[0]).start()
        pltpu.make_async_copy(cot_in,cot_ref,sem.at[1]).start()
        dvec_ref[...]=jnp.zeros_like(dvec_ref)
        dvec_ref[2:3,:]=jnp.sum(gf[...].astype(jnp.float32),axis=0,keepdims=True)
        branch[...]=jnp.zeros_like(branch); gn[...]=jnp.zeros_like(gn)
    if depth:
        tick1(j); tick2(j)
    w1=w1_ref[...]; w2=w2_ref[...].reshape(w1.shape[1],d)
    pre=dot(n3[...],w1)+b1_ref[...]
    back=dot(gf[...],w2,NT).astype(jnp.bfloat16).astype(jnp.float32)
    if depth:
        middle1(j); middle2(j)
    root=0.7978845608028654
    square=pre*pre
    t=jnp.tanh(root*pre*(1.0+0.044715*square))
    half_t=0.5*(1.0+t)
    hidden=(pre*half_t).astype(jnp.bfloat16)
    slope=half_t+0.5*pre*(1.0-t*t)*(root*(1.0+3*0.044715*square))
    g_pre=(back*slope).astype(jnp.bfloat16)
    db1_ref[...]=jnp.sum(g_pre.astype(jnp.float32),axis=0,keepdims=True)
    branch[...]+=dot(hidden,w2)
    dw2=dot(hidden,gf[...],TN).astype(jnp.bfloat16)
    dw1=dot(n3t[...],g_pre).astype(jnp.bfloat16)
    if depth:
        write_made(refs[0],j,0,dw1)
        write_made(refs[half],j,0,dw2)
        for n in range(FFN_LATE):
            @pl.when(j==steps-FFN_LATE+n)
            def _():
                for copy in leave(n): copy.start()
    else:
        dw1_ref[...]=dw1
        dw2_ref[...]=dw2.reshape(dw2_ref.shape)
    gn[...]+=dot(g_pre,w1,NT)
    @pl.when(j==steps-1)
    def _():
        def one(r):
            sl=pl.ds(r*strip,strip)
            valid=live(r)
            after=after_ref[sl,:]
            mixed[sl,:]=((after+(branch[sl,:]+b2))*valid).astype(jnp.bfloat16)
            hat,inverse=normal(after)
            grad=gn[sl,:]
            dvec_ref[0:1,:]+=jnp.sum(grad*hat,axis=0,keepdims=True)
            dvec_ref[1:2,:]+=jnp.sum(grad,axis=0,keepdims=True)
            grad=cot_ref[sl,:].astype(jnp.float32)*valid+pull_norm(hat,inverse,gain,grad)
            gn[sl,:]=grad
            cot_ref[sl,:]=grad.astype(jnp.bfloat16)
            ctx[sl,:]=dot(cot_ref[sl,:],wo[...],NT).astype(jnp.bfloat16)
        pltpu.make_async_copy(wo_ref,wo,sem.at[2]).wait()
        pltpu.make_async_copy(after_in,after_ref,sem.at[0]).wait()
        pltpu.make_async_copy(cot_in,cot_ref,sem.at[1]).wait()
        for r in range(rows//strip):
            if depth and r%2==0:
                tick1(steps+r//2); tick2(steps+r//2)
            one(r)
            if depth and r%2==0:
                middle1(steps+r//2); middle2(steps+r//2)
        copies=[pltpu.make_async_copy(a,b,sem.at[n]) for n,(a,b) in enumerate(((mixed,mixed_ref),(gn,grad_ref),(cot_ref,low_ref),(ctx,ctx_ref)))]
        for copy in copies: copy.start()
        if depth:
            for t in range(steps+rows//strip//2,steps-FFN_LATE+LAST_LAG):
                tick1(t); tick2(t); middle1(t); middle2(t)
            for n in range(FFN_LATE): copies+=leave(n)
        for copy in copies: copy.wait()

def feed_forward(ready,after,cot,length,w1,w2,b1,vec,wo,block=512,strip=128,depth=0,collective_id=None):
    rows,d=after.shape; ff=w1.shape[1]
    steps=ff//block
    once=lambda shape: pl.BlockSpec(shape,lambda j,n:(0,0),pipeline_mode=pl.Buffered(1))
    keep=lambda shape: pl.BlockSpec(shape,lambda j,n:(0,)*len(shape))
    any_=pl.BlockSpec(memory_space=pl.ANY)
    wide=pl.BlockSpec((d,block),lambda j,n:(0,j)); line=pl.BlockSpec((1,block),lambda j,n:(0,j))
    tall=pl.BlockSpec((w2.shape[0],block//w2.shape[0],d),lambda j,n:(0,j,0))
    bf=jnp.bfloat16; f32=jnp.float32
    scratch=[pltpu.VMEM((rows,d),bf),pltpu.VMEM((rows,d),bf),pltpu.VMEM((rows,d),f32),pltpu.VMEM((rows,d),bf),pltpu.VMEM((rows,d),f32),pltpu.VMEM((rows,d),f32),pltpu.VMEM((d,d),bf),DMA((4+2*FFN_LATE,))]
    if depth:
        each=d//(8*depth); part=block//(8*depth)
        grad_specs=[keep((each,ff)),keep((steps,part,d))]
        grad_shapes=[jax.ShapeDtypeStruct((each,ff),f32),jax.ShapeDtypeStruct((steps,part,d),f32)]
        late_shapes=[jax.ShapeDtypeStruct((max(FFN_LATE,1),2,2,depth,2,each,block),bf),jax.ShapeDtypeStruct((max(FFN_LATE,1),2,2,depth,2,part,d),bf)]
        scratch+=stream_scratch(each,block,depth)+stream_scratch(part,d,depth)
    else:
        grad_specs=[wide,tall]
        grad_shapes=[jax.ShapeDtypeStruct(w1.shape,bf),jax.ShapeDtypeStruct(w2.shape,bf)]
        late_shapes=[jax.ShapeDtypeStruct((8,128),bf)]*2
    return pl.pallas_call(
        functools.partial(ffn_kernel,strip,steps,depth),
        grid_spec=pltpu.PrefetchScalarGridSpec(
            num_scalar_prefetch=1,grid=(steps,),
            in_specs=[once((rows,d)),once((d,rows)),once((rows,d)),any_,any_,wide,tall,line,once(vec.shape),any_],
            out_specs=[any_]*4+grad_specs+[line,keep((8,d)),any_,any_],
            scratch_shapes=scratch),
        out_shape=[jax.ShapeDtypeStruct((rows,d),bf),jax.ShapeDtypeStruct((rows,d),f32)]+[jax.ShapeDtypeStruct((rows,d),bf)]*2+grad_shapes+[jax.ShapeDtypeStruct((1,ff),f32),jax.ShapeDtypeStruct((8,d),f32)]+late_shapes,
        compiler_params=pltpu.CompilerParams(vmem_limit_bytes=62*MIB,collective_id=collective_id,has_side_effects=depth>0),
        cost_estimate=pl.CostEstimate(flops=12*rows*d*ff,bytes_accessed=4*d*ff*2+rows*d*12,transcendentals=rows*ff),
        name="feed_forward",
    )(length,*ready,after,cot,w1,w2,b1,vec,wo)

AXES=("dp","fsdp")

def layer_norm(tensor, gain, shift):
    return normal(tensor)[0]*gain+shift

def layer_norm_back(tensor, gain, grad):
    hat,inverse=normal(tensor)
    return pull_norm(hat,inverse,gain,grad),jnp.sum(grad*hat,axis=0),jnp.sum(grad,axis=0)

def low(tensor):
    return tensor.astype(jnp.bfloat16)

def columns(tensor):
    return jnp.sum(tensor.astype(jnp.float32),axis=0)

def gather_all(shards):
    return [lax.all_gather(s,AXES,axis=0,tiled=True) for s in shards]

def reduce_all(partials):
    return [lax.psum_scatter(p,AXES,scatter_dimension=0,tiled=True).astype(jnp.float32) for p in partials]

def gather_vectors(vectors,wide):
    rows=jnp.stack([jnp.pad(v,(0,128-v.shape[0])) for v in list(vectors)+[wide]])
    rows=jnp.pad(rows,((0,15-len(vectors)),(0,0)))
    whole=lax.all_gather(rows,AXES).astype(jnp.float32)
    return whole[:,:,:vectors[0].shape[0]].transpose(1,0,2).reshape(16,-1),whole[:,len(vectors),:wide.shape[0]].reshape(1,-1)

def pack_grads(vectors,wide,devices):
    each=1024//devices
    flat=jnp.stack(vectors).reshape(len(vectors),devices,each).transpose(1,0,2).reshape(devices,-1)
    flat=jnp.concatenate([flat,wide.reshape(devices,4*each)],1)
    return jnp.pad(flat,((0,0),(0,1024-flat.shape[1]))).reshape(devices*8,128)

def shards(devices, depth, unit_states, dec_states, enc_states, unit_len, text_len, task_flag, cotangent,
    ln1_gain, ln1_shift, self_wq, self_bq, self_wk, self_wv, self_bv, self_wo, self_bo,
    ln2_gain, ln2_shift, cross_wq, cross_bq, cross_wk, cross_wv, cross_bv, cross_wo, cross_bo,
    ln3_gain, ln3_shift, ffn_w1, ffn_b1, ffn_w2, ffn_b2):
    steps=8
    each=1024//devices
    if depth: ffn_w1=order_columns(ffn_w1,devices,steps)
    w1=lax.all_gather(ffn_w1,AXES,axis=0,tiled=True)
    w2=lax.all_gather(ffn_w2,AXES,axis=0,tiled=True)
    small=[ln1_gain,ln1_shift,self_bq,self_bv,self_bo,ln2_gain,ln2_shift,cross_bq,cross_bv,cross_bo,ln3_gain,ln3_shift,ffn_b2]
    late=[self_wo,cross_wq,cross_wk,cross_wv,cross_wo]
    if depth:
        part=4*each//steps
        wq,wk,wv,vectors,b1=gather_first([self_wq,self_wk,self_wv],small,ffn_b1,steps,depth,1)
    else:
        wq,wk,wv,*late=gather_all([self_wq,self_wk,self_wv]+late)
        vectors,b1=gather_vectors(small,ffn_b1)
    g1,s1,bq,bv,bo,g2,s2,cbq,cbv,cbo,g3,s3,b2=[vectors[i] for i in range(13)]
    units=unit_states[0].astype(jnp.float32)
    memory=jnp.where(task_flag[0]==1,dec_states[0],enc_states[0])
    n1=low(layer_norm(units,g1,s1))
    q=low(dot(n1,wq)+bq); k=low(dot(n1,wk)); v=low(dot(n1,wv)+bv)
    if depth: ctx,lse,late=flash_fwd(q,k,v,text_len,True,moves=late,depth=depth,collective_id=2)
    else: ctx,lse,_=flash_fwd(q,k,v,text_len,True)
    wo,cwq,cwk,cwv,cwo=late
    after_self=units+(dot(ctx,wo)+bo)
    n2=low(layer_norm(after_self,g2,s2))
    cq=low(dot(n2,cwq)+cbq); ck=low(dot(memory,cwk)); cv=low(dot(memory,cwv)+cbv)
    cctx,clse,_=flash_fwd(cq,ck,cv,text_len,False)
    after_cross=after_self+(dot(cctx,cwo)+cbo)
    n3=low(layer_norm(after_cross,g3,s3))
    valid=(jnp.arange(units.shape[0],dtype=jnp.int32)<unit_len[0]).astype(jnp.float32)[:,None]
    gf=low(cotangent[0].astype(jnp.float32)*valid)
    ready=(n3,n3.T,gf)
    last=jnp.concatenate([vectors[10:13],jnp.zeros((5,1024),jnp.float32)])
    if depth:
        mixed,g_cross,gc,g_cctx,dw1,dw2,db1,dvec,*before=feed_forward(ready,after_cross,cotangent[0],unit_len,w1,w2.reshape(devices,4*each,1024),b1,last,cwo,depth=depth,collective_id=3)
    else:
        mixed,g_cross,gc,g_cctx,dw1,dw2,db1,dvec,*_=feed_forward(ready,after_cross,cotangent[0],unit_len,w1,w2[None],b1,last,cwo)
        dw1,dw2=reduce_all([dw1,dw2[0]])
    gain1,gain2=vectors[0:1],vectors[5:6]
    if depth:
        g_self,gs,g_ctx,g_dec,g_enc,csums,*starts,left1,left2,dw1,dw2=sub_layer_back(
            cq,ck,cv,g_cctx,cctx,clse,text_len,task_flag,False,n2,memory,gc,gain2,[cwq,cwk,cwv,wo,after_self,g_cross],before,[dw1,dw2],[],depth,4)
        dw2=dw2.reshape(4*each,1024)
        g_units,sums,dwq,dwk,dwv,dwo,dcwq,dcwk,dcwv,dcwo,grads=sub_layer_back(
            q,k,v,g_ctx,ctx,lse,text_len,task_flag,True,n1,memory,gs,gain1,[wq,wk,wv,unit_states[0],g_self],[left1,left2],starts,[csums,dvec,db1],depth,5)
        ng=[grads[i,:each] for i in range(13)]
        db1=grads[13]
    else:
        gcq,gck,gcv=flash_bwd(cq,ck,cv,g_cctx,cctx,clse,text_len,False)
        dcwq,dcwk,dcwv,dcwo=reduce_all([low(dot(n2,gcq,TN)),low(dot(memory,gck,TN)),low(dot(memory,gcv,TN)),low(dot(cctx,gc,TN))])
        g_memory=dot(gck,cwk,NT)+dot(gcv,cwv,NT)
        pulled,dg2,ds2=layer_norm_back(after_self,g2,dot(gcq,cwq,NT))
        g_self=g_cross+pulled
        gs=low(g_self)
        gq,gk,gv=flash_bwd(q,k,v,low(dot(gs,wo,NT)),ctx,lse,text_len,True)
        dwq,dwk,dwv,dwo=reduce_all([low(dot(n1,gq,TN)),low(dot(n1,gk,TN)),low(dot(n1,gv,TN)),low(dot(ctx,gs,TN))])
        pulled,dg1,ds1=layer_norm_back(units,g1,dot(gq,wq,NT)+dot(gk,wk,NT)+dot(gv,wv,NT))
        g_units=g_self+pulled
        is_dec=(task_flag[0]==1).astype(jnp.float32)
        g_dec,g_enc=g_memory*is_dec,g_memory*(1.0-is_dec)
        small_grads=[dg1,ds1,columns(gq),columns(gv),columns(gs),dg2,ds2,columns(gcq),columns(gcv),columns(gc),dvec[0],dvec[1],dvec[2]]
        grads,=reduce_all([pack_grads(small_grads,db1,devices)])
        grads=grads.reshape(1024)
        ng=[grads[i*each:(i+1)*each] for i in range(13)]
        db1=grads[13*each:17*each]
    if depth:
        dw1,mixed,g_units,g_dec,g_enc,dwq,dwk,dwv,dwo,dcwq,dcwk,dcwv,dcwo,dw2=deliver(
            [dw1,mixed,g_units,g_dec,g_enc,dwq,dwk,dwv,dwo,dcwq,dcwk,dcwv,dcwo,dw2],devices,steps)
    return (mixed[None],g_units[None],g_dec[None],g_enc[None],
        ng[0],ng[1],dwq,ng[2],dwk,dwv,ng[3],dwo,ng[4],ng[5],ng[6],dcwq,ng[7],dcwk,dcwv,ng[8],dcwo,ng[9],ng[10],ng[11],dw1,db1,dw2,ng[12])

def solution(mesh):
    devices=mesh.shape["dp"]*mesh.shape["fsdp"]
    depth=mesh.shape["fsdp"]//2 if mesh.shape["dp"]==4 and (1024//devices)%16==0 else 0
    cube,flat,row=P(AXES,None,None),P(AXES),P(AXES,None)
    return jax.shard_map(
        functools.partial(shards,devices,depth),
        mesh=mesh,
        in_specs=(cube,)*3+(flat,)*3+(cube,flat,flat,row,flat,row,row,flat,row,flat,flat,flat,row,flat,row,row,flat,row,flat,flat,flat,row,flat,row,flat),
        out_specs=(cube,)*4+(flat,flat,row,flat,row,row,flat,row,flat,flat,flat,row,flat,row,row,flat,row,flat,flat,flat,row,flat,row,flat),
        check_vma=False,
    )
```
